32 devices in a mesh: dp: 8 (over z, x), mp: 4 (over y, core).
Axes of the slice: x: 2, y: 2, z: 4, core: 2. Of those that a mesh axis runs over, the one named last changes fastest.
Arguments:
- tokens: bfloat16 [16384, 1024], P(('dp', 'mp')), may hold values from -6 to 6
- condition: bfloat16 [64, 768], P(('dp', 'mp')), may hold values from -6 to 6
- buckets: int32 [64], P(('dp', 'mp')), may hold values from 0 to 15
- heads_weight: bfloat16 [1024, 3, 1024], P(None, None, 'mp'), may hold values from -0.1875 to 0.1875
- merge_weight: bfloat16 [1024, 1024], P('mp'), may hold values from -1.5 to 1.5
- expand_weight: bfloat16 [1024, 2, 3072], P(None, None, 'mp'), may hold values from -0.1875 to 0.1875
- reduce_weight: bfloat16 [3072, 1024], P('mp'), may hold values from -0.109375 to 0.109375
- adapt_first: bfloat16 [768, 1024], replicated, may hold values from -0.109375 to 0.109375
- adapt_second: bfloat16 [768, 1024], replicated, may hold values from -0.109375 to 0.109375
- cosine_scale: float32 [16], P('mp'), may hold values from 8 to 24
- cotangent: bfloat16 [16384, 1024], P(('dp', 'mp')), may hold values from -6 to 6
Outputs:
- layer_out: float32 [16384, 1024], P(('dp', 'mp'))
- tokens_grad: float32 [16384, 1024], P(('dp', 'mp'))
- condition_grad: float32 [64, 768], P(('dp', 'mp'))
- heads_grad: float32 [1024, 3, 1024], P(None, None, 'mp')
- merge_grad: float32 [1024, 1024], P('mp')
- expand_grad: float32 [1024, 2, 3072], P(None, None, 'mp')
- reduce_grad: float32 [3072, 1024], P('mp')
- first_grad: float32 [768, 1024], replicated
- second_grad: float32 [768, 1024], replicated
- cosine_grad: float32 [16], P('mp')
The draws below stay inside these ranges and needn't reach their ends.
Inputs may be any that keep to these rules, and one draw needn't show every extreme that they name: `buckets`: each image's bucket indexes the table of 256-slot grids in the reference program.
All inputs are finite; a program needn't handle non-finite values.
Results may differ from the reference program's by a relative error of at most 0.025.
Values may be sent and summed in bfloat16 or wider, within the bound.
No kernel may reach another device: no remote copies, remote signals or barrier semaphores. Data moves between devices by JAX's collectives and lax.ppermute only.
A program may use at most 192 MiB of HBM per device.

```python
import math
import jax
import jax.numpy as jnp
import numpy as np
from jax import lax

D = 1024
HEADS = 16
HEAD_DIM = 64
FF = 3072
C = 768
BUCKET = 256
IMAGES = 64
TOKENS = 16384


def plant(drawn, stream_key, least, largest):
    dims = drawn.shape
    index_at = [jax.random.randint(jax.random.fold_in(stream_key, axis), (), 0, dims[axis]) for axis in range(len(dims))]
    drawn = drawn.at[tuple(index_at)].set(least)
    longest = dims.index(max(dims))
    index_at[longest] = (index_at[longest] + 1) % dims[longest]
    return drawn.at[tuple(index_at)].set(largest)


def block_scale(rng, shape, cuts, smallest, high):
    def one(dim, blocks):
        steps = jax.random.uniform(jax.random.fold_in(jax.random.fold_in(rng, 6), dim), (blocks,), jnp.float32, smallest / len(cuts), high / len(cuts))
        return jnp.repeat(jnp.exp(steps), shape[dim] // blocks).reshape((-1,) + (1,) * (len(shape) - dim - 1))

    gain = one(*cuts[0])
    for cut in cuts[1:]:
        gain = gain * one(*cut)
    return gain


def normal_values(rng, extent, width, reach, cuts=(), held_as=jnp.bfloat16):
    values = jax.random.normal(rng, extent, jnp.float32) * width
    if len(cuts) > 0:
        values = block_scale(rng, extent, cuts, -0.22, 0.18) * values
    return jnp.clip(values, min=-reach, max=reach).astype(held_as)


def setup_inputs(seed: int = 0) -> dict:
    streams_of = jax.random.split(jax.random.key(seed), 12)
    tokens = normal_values(streams_of[0], (TOKENS, D), 1.0, 6.0, ((0, 32),))
    condition = normal_values(streams_of[1], (IMAGES, C), 1.0, 6.0, ((0, 32),))
    buckets = plant(jax.random.randint(streams_of[2], (IMAGES,), 0, 16), jax.random.fold_in(streams_of[2], 1), 0, 15).astype(jnp.int32)
    heads_weight = normal_values(streams_of[3], (D, 3, D), D ** -0.5, 0.1875, ((2, 4),))
    merge_weight = normal_values(streams_of[4], (D, D), (D // 64) ** -0.5, 1.5, ((0, 4),))
    expand_weight = normal_values(streams_of[5], (D, 2, FF), D ** -0.5, 0.1875, ((2, 4),))
    reduce_weight = normal_values(streams_of[6], (FF, D), FF ** -0.5, 0.109375, ((0, 4),))
    adapt_first = normal_values(streams_of[7], (C, D), (4 * C) ** -0.5, 0.109375)
    adapt_second = normal_values(streams_of[8], (C, D), (4 * C) ** -0.5, 0.109375)
    cosine_scale = jnp.clip(jnp.exp(math.log(24.0) - 1.0986123 * jax.random.uniform(streams_of[9], (HEADS,), jnp.float32) ** block_scale(streams_of[9], (HEADS,), ((0, 4),), -0.2, 0.2)), 8.0, 24.0)
    cotangent = normal_values(streams_of[10], (TOKENS, D), 1.0, 6.0, ((0, 32),))
    return {"tokens": tokens, "condition": condition, "buckets": buckets, "heads_weight": heads_weight, "merge_weight": merge_weight, "expand_weight": expand_weight, "reduce_weight": reduce_weight, "adapt_first": adapt_first, "adapt_second": adapt_second, "cosine_scale": cosine_scale, "cotangent": cotangent}


epsilon = 1e-06
highest = lax.Precision.HIGHEST
GRID_ROWS = np.array([16, 12, 21, 14, 18, 12, 16, 10, 20, 8, 24, 11, 22, 8, 32, 13], np.int32)
GRID_COLS = np.array([16, 21, 12, 18, 14, 16, 12, 20, 10, 24, 8, 22, 11, 32, 8, 13], np.int32)

@jax.custom_vjp
def low(v):
    return lax.optimization_barrier(v.astype(jnp.bfloat16)).astype(jnp.float32)

@jax.custom_vjp
def low_back(v):
    return v

def low_keep(v):
    return (low(v), None)

def low_pass(kept, grad):
    return (grad,)

def back_keep(v):
    return (v, None)

def back_low(kept, grad):
    return (low(grad),)
low.defvjp(low_keep, low_pass)
low_back.defvjp(back_keep, back_low)

def grid_lookup(bucket_ids):
    heights = jnp.asarray(GRID_ROWS)[bucket_ids]
    widths = jnp.asarray(GRID_COLS)[bucket_ids]
    places = jnp.arange(BUCKET, dtype=jnp.int32)[None, :]
    row_pos = places // widths[:, None]
    col_pos = places % widths[:, None]
    valid = places < (heights * widths)[:, None]
    quarter = HEAD_DIM // 8
    freqs = 10000.0 ** (-jnp.arange(quarter, dtype=jnp.float32) / quarter)
    angles = jnp.concatenate([row_pos.astype(jnp.float32)[..., None] * freqs, col_pos.astype(jnp.float32)[..., None] * freqs], -1)
    return (jnp.cos(angles), jnp.sin(angles), valid)

def rotate(values, cosines, sines):
    half = HEAD_DIM // 4
    first = values[..., :half]
    second = values[..., half:2 * half]
    return jnp.concatenate([first * cosines - second * sines, first * sines + second * cosines, values[..., 2 * half:]], -1)

def shape_heads(raw, scale, cosines, sines):
    normed = raw * lax.rsqrt(lax.optimization_barrier(jnp.sum(raw * raw, -1, keepdims=True)) + epsilon) * jnp.sqrt(scale)[:, None]
    return rotate(normed, cosines, sines)

def rms_adapt(values, product):
    return values * lax.rsqrt(lax.optimization_barrier(jnp.mean(values * values, -1, keepdims=True)) + epsilon) * (1.0 + product[:, None, :])

def attend_block(inputs):
    queries, key_rows, value_rows, valid = inputs
    scores = low_back(jnp.einsum('ithd,ishd->ihts', queries, key_rows, precision=highest))
    scores = jnp.where(valid[:, None, None, :], scores, -1e+30)
    probs = low(jax.nn.softmax(scores, axis=-1))
    return jnp.einsum('ihts,ishd->ithd', probs, value_rows, precision=highest)

def reference(tokens, condition, buckets, heads_weight, merge_weight, expand_weight, reduce_weight, adapt_first, adapt_second, cosine_scale, cotangent):
    cosines, sines, valid = grid_lookup(buckets)
    cosines = cosines.reshape(TOKENS, 1, -1)
    sines = sines.reshape(TOKENS, 1, -1)
    block_images = 16
    blocks = IMAGES // block_images
    valid_blocks = valid.reshape(blocks, block_images, BUCKET)

    def forward(tokens_f, condition_f, heads_f, merge_f, expand_f, reduce_f, first_f, second_f, scale_f):
        first_adapt = low_back(jnp.dot(condition_f, first_f, precision=highest))
        second_adapt = low_back(jnp.dot(condition_f, second_f, precision=highest))
        normed = low(rms_adapt(tokens_f.reshape(IMAGES, BUCKET, D), first_adapt).reshape(TOKENS, D))
        triple = low_back(jnp.dot(normed, heads_f.reshape(D, 3 * D), precision=highest))
        triple = triple.reshape(TOKENS, 3, HEADS, HEAD_DIM)
        block_shape = (blocks, block_images, BUCKET, HEADS, HEAD_DIM)
        queries = low(shape_heads(triple[:, 0], scale_f, cosines, sines)).reshape(block_shape)
        key_rows = low(shape_heads(triple[:, 1], scale_f, cosines, sines)).reshape(block_shape)
        value_rows = low(triple[:, 2]).reshape(block_shape)
        mixed = lax.map(jax.checkpoint(attend_block), (queries, key_rows, value_rows, valid_blocks))
        mixed = low(low_back(mixed.reshape(TOKENS, D)))
        middle = tokens_f + low_back(jnp.dot(mixed, merge_f, precision=highest))
        second = low(rms_adapt(middle.reshape(IMAGES, BUCKET, D), second_adapt).reshape(TOKENS, D))
        gate_up = low_back(jnp.dot(second, expand_f.reshape(D, 2 * FF), precision=highest)).reshape(TOKENS, 2, FF)
        hidden = low(jax.nn.gelu(gate_up[:, 0], approximate=True) * gate_up[:, 1])
        return middle + low_back(jnp.dot(hidden, reduce_f, precision=highest))
    floats = (tokens.astype(jnp.float32), condition.astype(jnp.float32), heads_weight.astype(jnp.float32), merge_weight.astype(jnp.float32), expand_weight.astype(jnp.float32), reduce_weight.astype(jnp.float32), adapt_first.astype(jnp.float32), adapt_second.astype(jnp.float32), cosine_scale.astype(jnp.float32))
    result, pullback = jax.vjp(forward, *floats)
    grads = pullback(cotangent.astype(jnp.float32))
    return (result, grads[0], grads[1], grads[2], grads[3], grads[4], grads[5], grads[6], grads[7], grads[8])
```

```python
import functools

import jax
import jax.numpy as jnp
import numpy as np
from jax import lax
from jax.experimental import pallas as pl
from jax.experimental.pallas import tpu as pltpu
from jax.sharding import PartitionSpec as P

HEAD_DIM = 64
BUCKET = 256
EPS = 1e-06
NEG = -1e30
GRID_ROWS = np.array([16, 12, 21, 14, 18, 12, 16, 10, 20, 8, 24, 11, 22, 8, 32, 13], np.int32)
GRID_COLS = np.array([16, 21, 12, 18, 14, 16, 12, 20, 10, 24, 8, 22, 11, 32, 8, 13], np.int32)
F32 = jnp.float32
BF16 = jnp.bfloat16
VMEM_LIMIT = 56 * 1024 * 1024
GELU_A = float(np.sqrt(2.0 / np.pi))
GELU_B = 0.044715
CHUNK = 256


def nn(a, b):
    return lax.dot_general(a, b, (((1,), (0,)), ((), ())), preferred_element_type=F32)


def nt(a, b):
    return lax.dot_general(a, b, (((1,), (1,)), ((), ())), preferred_element_type=F32)


def tn(a, b):
    return lax.dot_general(a, b, (((0,), (0,)), ((), ())), preferred_element_type=F32)


def params():
    return pltpu.CompilerParams(vmem_limit_bytes=VMEM_LIMIT, dimension_semantics=("arbitrary",))


def cost(flops, nbytes, trans=0):
    return pl.CostEstimate(flops=int(flops), bytes_accessed=int(nbytes), transcendentals=int(trans))


def whole(shape):
    return pl.BlockSpec(shape, lambda i: (0,) * len(shape))


def rows(block, width):
    return pl.BlockSpec((block, width), lambda i: (i, 0))


def norm_first_kernel(x_ref, s_ref, out_ref):
    x = x_ref[...].astype(F32)
    r = lax.rsqrt(jnp.mean(x * x, -1, keepdims=True) + EPS)
    out_ref[...] = (x * r * s_ref[0]).astype(BF16)


def norm_first(tokens, scale):
    n, d = tokens.shape
    return pl.pallas_call(
        norm_first_kernel,
        grid=(n // BUCKET,),
        in_specs=[rows(BUCKET, d), pl.BlockSpec((1, 1, d), lambda i: (i, 0, 0))],
        out_specs=rows(BUCKET, d),
        out_shape=jax.ShapeDtypeStruct((n, d), BF16),
        compiler_params=params(),
        cost_estimate=cost(8 * n * d, 4 * n * d),
        name="norm_first",
    )(tokens, scale)


def norm_second_kernel(x_ref, part_ref, recv_ref, s_ref, mid_ref, out_ref):
    x = x_ref[...].astype(F32) + (part_ref[...] + recv_ref[...].astype(F32))
    mid_ref[...] = x
    r = lax.rsqrt(jnp.mean(x * x, -1, keepdims=True) + EPS)
    out_ref[...] = (x * r * s_ref[0]).astype(BF16)


def norm_second(tokens, part, recv, scale):
    n, d = tokens.shape
    return pl.pallas_call(
        norm_second_kernel,
        grid=(n // BUCKET,),
        in_specs=[rows(BUCKET, d)] * 3 + [pl.BlockSpec((1, 1, d), lambda i: (i, 0, 0))],
        out_specs=[rows(BUCKET, d)] * 2,
        out_shape=[jax.ShapeDtypeStruct((n, d), F32), jax.ShapeDtypeStruct((n, d), BF16)],
        compiler_params=params(),
        cost_estimate=cost(8 * n * d, 14 * n * d),
        name="norm_second",
    )(tokens, part, recv, scale)


def norm_back_kernel(extra, low, *refs):
    part_ref = refs[0]
    more = refs[1 : 1 + extra]
    x_ref, g_ref, s_ref = refs[1 + extra : 4 + extra]
    outs = refs[4 + extra :]
    grad = part_ref[...]
    for ref in more:
        grad = grad + ref[...].astype(F32)
    x = x_ref[...].astype(F32)
    r = lax.rsqrt(jnp.mean(x * x, -1, keepdims=True) + EPS)
    u = grad * s_ref[0]
    back = g_ref[...].astype(F32) + r * u - x * (r * r * r * jnp.mean(u * x, -1, keepdims=True))
    outs[0][...] = back
    outs[1][0] = jnp.sum(grad * x * r, 0, keepdims=True)
    if low:
        outs[2][...] = back.astype(BF16)


def norm_back(part, more, x, g, scale, low):
    n, d = x.shape
    per_image = pl.BlockSpec((1, 1, d), lambda i: (i, 0, 0))
    outs = [jax.ShapeDtypeStruct((n, d), F32), jax.ShapeDtypeStruct((n // BUCKET, 1, d), F32)]
    specs = [rows(BUCKET, d), per_image]
    if low:
        outs.append(jax.ShapeDtypeStruct((n, d), BF16))
        specs.append(rows(BUCKET, d))
    return pl.pallas_call(
        functools.partial(norm_back_kernel, len(more), low),
        grid=(n // BUCKET,),
        in_specs=[rows(BUCKET, d)] * (3 + len(more)) + [per_image],
        out_specs=specs,
        out_shape=outs,
        compiler_params=params(),
        cost_estimate=cost(16 * n * d, 18 * n * d),
        name="norm_back",
    )(part, *more, x, g, scale)


def head_sums(values, block_ones):
    high = values.astype(BF16)
    low = (values - high.astype(F32)).astype(BF16)
    return nn(high, block_ones) + nn(low, block_ones)


def partner(values):
    parts = []
    for start in range(0, values.shape[1], 128):
        part = values[:, start : start + 128]
        lane = lax.broadcasted_iota(jnp.int32, part.shape, 1) % HEAD_DIM
        parts.append(
            jnp.where(lane < HEAD_DIM // 4, pltpu.roll(part, 128 - 16, 1), pltpu.roll(part, 16, 1))
        )
    return jnp.concatenate(parts, 1)


def twice(table, width):
    return jnp.concatenate([table] * (width // table.shape[1]), 1)


def head_mask(shape, head):
    lane = lax.broadcasted_iota(jnp.int32, shape, 1)
    return (lane >= head * HEAD_DIM) & (lane < (head + 1) * HEAD_DIM)


def attend_forward_kernel(
    merge, heads, n_ref, w_ref, root_ref, ones_ref, cos_ref, sin_ref, bias_ref, *refs
):
    if merge:
        other_ref, m_own_ref, m_ref = refs[:3]
        refs = refs[3:]
    q_ref, k_ref, v_ref, cq_ref, ck_ref, mixed_ref = refs[:6]
    normed = n_ref[...]
    width = heads * HEAD_DIM
    cosines, sines = twice(cos_ref[...], width), twice(sin_ref[...], width)
    ones = ones_ref[...]
    root = root_ref[...]

    def shape_heads(which, c_ref):
        raw = nn(normed, w_ref[which])
        c = lax.rsqrt(head_sums(raw * raw, ones) + EPS) * root
        c_ref[...] = c
        n = raw * c
        return (n * cosines + partner(n) * sines).astype(BF16)

    q = shape_heads(0, cq_ref)
    k = shape_heads(1, ck_ref)
    v = nn(normed, w_ref[2]).astype(BF16)
    q_ref[...] = q
    k_ref[...] = k
    v_ref[...] = v
    bias = bias_ref[0]
    mixed = jnp.zeros((BUCKET, width), F32)
    for head in range(heads):
        mask = head_mask((BUCKET, width), head)
        zero = jnp.zeros_like(q)
        scores = nt(jnp.where(mask, q, zero), k) + bias
        e = jnp.exp(scores)
        probs = e * (1.0 / jnp.sum(e, -1, keepdims=True))
        mixed = mixed + nn(probs.astype(BF16), jnp.where(mask, v, zero))
    mixed = mixed.astype(BF16)
    mixed_ref[...] = mixed
    if merge:
        keep_ref, send_ref = refs[6:]
        part = nn(other_ref[...], m_own_ref[...]) + nn(mixed, m_ref[...])

        @pl.when(pl.program_id(0) < 2)
        def _():
            keep_ref[...] = part

        @pl.when(pl.program_id(0) >= 2)
        def _():
            send_ref[...] = part.astype(BF16)


def attend_forward(normed, weight, root, ones, cosines, sines, bias, merge=None):
    n, d = normed.shape
    width = weight.shape[2]
    images = n // BUCKET
    heads = width // HEAD_DIM
    half = images // 2
    block = rows(BUCKET, width)
    in_specs = [
        rows(BUCKET, d),
        whole(weight.shape),
        whole(root.shape),
        whole(ones.shape),
        rows(BUCKET, 128),
        rows(BUCKET, 128),
        pl.BlockSpec((1, 1, BUCKET), lambda i: (i, 0, 0)),
    ]
    operands = [normed, weight, root, ones, cosines, sines, bias]
    out_specs = [block] * 6
    outs = [jax.ShapeDtypeStruct((n, width), t) for t in (BF16, BF16, BF16, F32, F32, BF16)]
    flops = 2 * n * d * 3 * width + 4 * n * BUCKET * width * heads
    if merge is not None:
        other, own_weight, merge_weight = merge
        in_specs += [block, whole(own_weight.shape), whole(merge_weight.shape)]
        operands += [other, own_weight, merge_weight]
        out_specs += [
            pl.BlockSpec((BUCKET, d), lambda i: (jnp.minimum(i, half - 1), 0)),
            pl.BlockSpec((BUCKET, d), lambda i: (jnp.maximum(i - half, 0), 0)),
        ]
        outs += [
            jax.ShapeDtypeStruct((n // 2, d), F32),
            jax.ShapeDtypeStruct((n // 2, d), BF16),
        ]
        flops += 4 * n * width * d
    return pl.pallas_call(
        functools.partial(attend_forward_kernel, merge is not None, heads),
        grid=(images,),
        in_specs=in_specs,
        out_specs=out_specs,
        out_shape=outs,
        compiler_params=params(),
        cost_estimate=cost(flops * 2, 12 * 1024 * 1024, n * BUCKET * heads),
        name="attend_forward",
    )(*operands)


def attend_backward_kernel(
    second,
    heads,
    n_ref,
    w_ref,
    m_ref,
    inv_ref,
    ones_ref,
    cos_ref,
    sin_ref,
    valid_ref,
    b_ref,
    q_ref,
    k_ref,
    v_ref,
    cq_ref,
    ck_ref,
    mixed_ref,
    *refs,
):
    if second:
        prev_keep_ref, prev_send_ref = refs[:2]
        refs = refs[2:]
    hgrad_ref, mgrad_ref, scale_ref, keep_ref, send_ref, tg_ref, macc_ref = refs
    i = pl.program_id(0)
    width = heads * HEAD_DIM
    cosines, sines = twice(cos_ref[...], width), twice(sin_ref[...], width)
    ones = ones_ref[...]
    inv = inv_ref[...]
    branch = b_ref[...]
    q, k, v = q_ref[...], k_ref[...], v_ref[...]
    mixed = mixed_ref[...]
    dmix = nt(branch, m_ref[...]).astype(BF16)
    prod = (dmix.astype(F32) * mixed.astype(F32)).astype(BF16)
    bias = valid_ref[0]
    zero = jnp.zeros_like(q)
    dq = jnp.zeros((BUCKET, width), F32)
    dk = jnp.zeros((BUCKET, width), F32)
    dv = jnp.zeros((BUCKET, width), F32)
    for head in range(heads):
        mask = head_mask((BUCKET, width), head)
        qh = jnp.where(mask, q, zero)
        kh = jnp.where(mask, k, zero)
        dh = jnp.where(mask, dmix, zero)
        picks = jnp.where(head_mask((16, width), head), 1.0, 0.0).astype(BF16)
        delta = nt(picks, prod)[0:1, :]
        e = jnp.exp(nt(k, qh) + bias)
        probs = e * (1.0 / jnp.sum(e, 0, keepdims=True))
        dprobs = nt(v, dh)
        ds = (probs * (dprobs - delta)).astype(BF16)
        dv = dv + nn(probs.astype(BF16), dh)
        dk = dk + nn(ds, qh)
        dq = dq + tn(ds, kh)

    def back(low, grad, c):
        full = low.astype(F32)
        sums = head_sums(full * grad, ones)
        t = grad - full * (sums * inv)
        return (c * (t * cosines - partner(t) * sines)).astype(BF16), jnp.sum(sums, 0, keepdims=True)

    gq, sq = back(q, dq, cq_ref[...])
    gk, sk = back(k, dk, ck_ref[...])
    gv = dv.astype(BF16)
    part = nt(gq, w_ref[0]) + nt(gk, w_ref[1]) + nt(gv, w_ref[2])
    at = pl.ds(pl.multiple_of(i * BUCKET, BUCKET), BUCKET)
    tg_ref[0, at, :] = gq
    tg_ref[1, at, :] = gk
    tg_ref[2, at, :] = gv
    mg = tn(mixed, branch)

    @pl.when(i == 0)
    def _():
        scale_ref[...] = sq + sk
        macc_ref[...] = mg

    @pl.when(i > 0)
    def _():
        scale_ref[...] += sq + sk
        macc_ref[...] += mg

    if second:

        @pl.when(i < 2)
        def _():
            keep_ref[...] = part + prev_keep_ref[...]

        @pl.when(i >= 2)
        def _():
            send_ref[...] = (part + prev_send_ref[...]).astype(BF16)
    else:

        @pl.when(i < 2)
        def _():
            keep_ref[...] = part

        @pl.when(i >= 2)
        def _():
            send_ref[...] = part

    @pl.when(i == pl.num_programs(0) - 1)
    def _():
        mgrad_ref[...] = macc_ref[...].astype(BF16)
        for which in range(3):
            hgrad_ref[which] = tn(n_ref[...], tg_ref[which]).astype(BF16)


def attend_backward(
    normed, weight, merge_weight, inv, ones, cosines, sines, valid, branch, saved, prev=None
):
    n, d = normed.shape
    width = weight.shape[2]
    images = n // BUCKET
    heads = width // HEAD_DIM
    half = images // 2
    block = rows(BUCKET, width)
    keep_spec = pl.BlockSpec((BUCKET, d), lambda i: (jnp.minimum(i, half - 1), 0))
    send_spec = pl.BlockSpec((BUCKET, d), lambda i: (jnp.maximum(i - half, 0), 0))
    in_specs = [
        whole(normed.shape),
        whole(weight.shape),
        whole(merge_weight.shape),
        whole(inv.shape),
        whole(ones.shape),
        rows(BUCKET, 128),
        rows(BUCKET, 128),
        pl.BlockSpec((1, BUCKET, 1), lambda i: (i, 0, 0)),
        rows(BUCKET, d),
    ] + [block] * 6
    operands = [
        normed, weight, merge_weight, inv, ones, cosines, sines, valid, branch, *saved,
    ]
    if prev is not None:
        in_specs += [keep_spec, send_spec]
        operands += list(prev)
    return pl.pallas_call(
        functools.partial(attend_backward_kernel, prev is not None, heads),
        grid=(images,),
        in_specs=in_specs,
        out_specs=[
            whole(weight.shape),
            whole(merge_weight.shape),
            whole((1, width)),
            keep_spec,
            send_spec,
        ],
        out_shape=[
            jax.ShapeDtypeStruct(weight.shape, BF16),
            jax.ShapeDtypeStruct(merge_weight.shape, BF16),
            jax.ShapeDtypeStruct((1, width), F32),
            jax.ShapeDtypeStruct((n // 2, d), F32),
            jax.ShapeDtypeStruct((n // 2, d), F32 if prev is None else BF16),
        ],
        scratch_shapes=[
            pltpu.VMEM((3, n, width), BF16),
            pltpu.VMEM(merge_weight.shape, F32),
        ],
        compiler_params=params(),
        cost_estimate=cost(
            2 * (16 * n * d * width + 10 * n * BUCKET * width * heads),
            16 * 1024 * 1024,
            n * BUCKET * heads,
        ),
        name="attend_backward",
    )(*operands)


def geglu_kernel(second, na_ref, nb_ref, ga_ref, gb_ref, e_ref, r_ref, *refs):
    if second:
        prev_ref = refs[0]
        refs = refs[1:]
    o_keep_ref, o_send_ref, n_keep_ref, n_send_ref, grad_ref, ob_ref, nb_acc_ref, act_ref = refs
    j = pl.program_id(0)
    e_gate, e_up, red = e_ref[0], e_ref[1], r_ref[...]
    half = na_ref.shape[0]
    tile = 256
    for t in range(2 * half // tile):
        first = t * tile < half
        at = pl.ds((t * tile) % half, tile)
        normed = (na_ref if first else nb_ref)[at, :]
        g = (ga_ref if first else gb_ref)[at, :]
        gate = nn(normed, e_gate)
        up = nn(normed, e_up)
        hgrad = nt(g, red)
        square = gate * gate
        th = jnp.tanh(gate * (GELU_A + (GELU_A * GELU_B) * square))
        act = 0.5 * (1.0 + th)
        gelu = gate * act
        slope = act + (0.5 * gate) * (1.0 - th * th) * (GELU_A + (3.0 * GELU_A * GELU_B) * square)
        hidden = (gelu * up).astype(BF16)
        d_gate = (hgrad * up * slope).astype(BF16)
        d_up = (hgrad * gelu).astype(BF16)
        whole_at = pl.ds(t * tile, tile)
        act_ref[0, whole_at, :] = hidden
        act_ref[1, whole_at, :] = d_gate
        act_ref[2, whole_at, :] = d_up
        o_part = nn(hidden, red)
        n_part = nt(d_gate, e_gate) + nt(d_up, e_up)
        o_ref = o_keep_ref if first else ob_ref
        n_ref = n_keep_ref if first else nb_acc_ref

        @pl.when(j == 0)
        def _():
            o_ref[at, :] = o_part
            n_ref[at, :] = n_part

        @pl.when(j > 0)
        def _():
            o_ref[at, :] += o_part
            n_ref[at, :] += n_part

    for which in range(3):
        left = ga_ref if which == 0 else na_ref
        right = gb_ref if which == 0 else nb_ref
        total = tn(act_ref[which, :half, :], left[...]) + tn(act_ref[which, half:, :], right[...])
        here = pl.ds(which * CHUNK, CHUNK)
        if second:
            total = total + prev_ref[0, here, :].astype(F32)
        grad_ref[0, here, :] = total.astype(BF16)

    @pl.when(j == pl.num_programs(0) - 1)
    def _():
        o_send_ref[...] = ob_ref[...].astype(BF16)
        n_send_ref[...] = nb_acc_ref[...].astype(BF16)


def geglu(normed_a, normed_b, grad_a, grad_b, expand, reduce, prev=None):
    half, d = normed_a.shape
    units = reduce.shape[0]
    steps = units // CHUNK
    grads = pl.BlockSpec((1, 3 * CHUNK, d), lambda j: (j, 0, 0))
    in_specs = [whole((half, d))] * 4 + [
        pl.BlockSpec((2, d, CHUNK), lambda j: (0, 0, j)),
        pl.BlockSpec((CHUNK, d), lambda j: (j, 0)),
    ]
    operands = [normed_a, normed_b, grad_a, grad_b, expand, reduce]
    if prev is not None:
        in_specs.append(grads)
        operands.append(prev)
    return pl.pallas_call(
        functools.partial(geglu_kernel, prev is not None),
        grid=(steps,),
        in_specs=in_specs,
        out_specs=[whole((half, d))] * 4 + [grads],
        out_shape=[
            jax.ShapeDtypeStruct((half, d), F32),
            jax.ShapeDtypeStruct((half, d), BF16),
            jax.ShapeDtypeStruct((half, d), F32),
            jax.ShapeDtypeStruct((half, d), BF16),
            jax.ShapeDtypeStruct((steps, 3 * CHUNK, d), BF16),
        ],
        scratch_shapes=[
            pltpu.VMEM((half, d), F32),
            pltpu.VMEM((half, d), F32),
            pltpu.VMEM((3, 2 * half, CHUNK), BF16),
        ],
        compiler_params=params(),
        cost_estimate=cost(2 * 9 * 2 * half * d * units, 32 * 1024 * 1024, 2 * half * units),
        name="geglu",
    )(*operands)


def swap(values, axis, size, bit):
    return lax.ppermute(values, axis, [(i, i ^ bit) for i in range(size)])


def reduce_over(values, order, size, index):
    x = values
    for bit in order:
        half = x.shape[0] // 2
        mine = (index & bit) != 0
        low, high = x[:half], x[half:]
        sent = jnp.where(mine, low, high)
        kept = jnp.where(mine, high, low)
        got = swap(sent, "dp", size, bit)
        x = (kept.astype(F32) + got.astype(F32)).astype(BF16)
    for bit in reversed(order):
        mine = (index & bit) != 0
        got = swap(x, "dp", size, bit)
        x = jnp.where(mine, jnp.concatenate([got, x], 0), jnp.concatenate([x, got], 0))
    return x


def rope_tables(bucket_ids):
    quarter = HEAD_DIM // 8
    choose = (bucket_ids[:, None] == jnp.arange(16, dtype=jnp.int32)[None, :]).astype(jnp.int32)
    heights = jnp.sum(choose * jnp.asarray(GRID_ROWS)[None, :], axis=1)
    widths = jnp.sum(choose * jnp.asarray(GRID_COLS)[None, :], axis=1)
    places = jnp.arange(BUCKET, dtype=jnp.int32)[None, :]
    row_pos = (places // widths[:, None]).reshape(-1)
    col_pos = (places % widths[:, None]).reshape(-1)
    valid = places < (heights * widths)[:, None]
    lane = np.arange(128) % HEAD_DIM
    freqs = 10000.0 ** (-jnp.arange(quarter, dtype=F32) / quarter)
    freqs = freqs[lane % quarter]
    by_row = jnp.asarray((lane // quarter) % 2 == 0)
    turns = jnp.asarray(lane < HEAD_DIM // 2)
    sign = jnp.asarray(np.where(lane < HEAD_DIM // 4, -1.0, 1.0).astype(np.float32))
    where = jnp.where(by_row[None, :], row_pos[:, None], col_pos[:, None]).astype(F32)
    angles = where * freqs[None, :]
    cosines = jnp.where(turns[None, :], jnp.cos(angles), 1.0)
    sines = jnp.where(turns[None, :], jnp.sin(angles) * sign[None, :], 0.0)
    bias = jnp.where(valid, 0.0, NEG).astype(F32)
    return cosines, sines, bias


def per_device(
    dp,
    mp,
    tokens,
    condition,
    buckets,
    heads_weight,
    merge_weight,
    expand_weight,
    reduce_weight,
    adapt_first,
    adapt_second,
    cosine_scale,
    cotangent,
):
    own_rows, width = tokens.shape
    local_images = buckets.shape[0]
    local_heads = cosine_scale.shape[0]
    local = local_heads * HEAD_DIM
    units = reduce_weight.shape[0]
    index = lax.axis_index("dp")
    core = functools.partial(swap, axis="mp", size=mp, bit=1)
    chip = functools.partial(swap, axis="mp", size=mp, bit=2)

    heads_own = jnp.transpose(heads_weight, (1, 0, 2))
    heads_other = chip(heads_own)
    merge_other = chip(merge_weight)
    scale_other = chip(cosine_scale)
    cot_chip = chip(cotangent)
    cot_core = core(cotangent)
    cot_far = core(cot_chip)

    scale_first = 1.0 + jnp.dot(condition, adapt_first, preferred_element_type=F32)
    scale_second = 1.0 + jnp.dot(condition, adapt_second, preferred_element_type=F32)
    scale_first = scale_first.reshape(local_images, 1, width)
    scale_second = scale_second.reshape(local_images, 1, width)
    normed_own = norm_first(tokens, scale_first)
    normed = jnp.concatenate([normed_own, core(normed_own)], 0)
    cosines, sines, bias = rope_tables(jnp.concatenate([buckets, core(buckets)], 0))
    bias_row = bias[:, None, :]
    bias_column = bias[:, :, None]
    expand_own = jnp.transpose(expand_weight, (1, 0, 2))
    head_of = np.arange(local) // HEAD_DIM
    ones = jnp.asarray((head_of[:, None] == head_of[None, :]).astype(np.float32)).astype(BF16)

    def lanes(values):
        return jnp.repeat(values, HEAD_DIM)[None, :]

    own = attend_forward(
        normed, heads_own, lanes(jnp.sqrt(cosine_scale)), ones, cosines, sines, bias_row
    )
    *other, keep, send = attend_forward(
        normed,
        heads_other,
        lanes(jnp.sqrt(scale_other)),
        ones,
        cosines,
        sines,
        bias_row,
        (own[5], merge_weight, merge_other),
    )
    middle, second_own = norm_second(tokens, keep, core(send), scale_second)
    second_chip = chip(second_own)
    second_core = core(second_own)
    second_far = core(second_chip)

    o_keep, o_send, n_keep, n_send, grads = geglu(
        second_own, second_core, cotangent, cot_core, expand_own, reduce_weight
    )
    o_chip, o_far, n_chip, n_far, grads = geglu(
        second_chip, second_far, cot_chip, cot_far, expand_own, reduce_weight, grads
    )

    n_sum = chip((n_chip + core(n_far).astype(F32)).astype(BF16))
    n_near = core(n_send)
    middle_grad, adapt_second_grad, branch_own = norm_back(
        n_keep, (n_near, n_sum), middle, cotangent, scale_second, True
    )
    o_sum = chip((o_chip + core(o_far).astype(F32)).astype(BF16))
    layer_out = middle + (o_keep + core(o_send).astype(F32) + o_sum.astype(F32))

    branch = jnp.concatenate([branch_own, core(branch_own)], 0)
    heads_far, merge_far, turn_far, keep, send = attend_backward(
        normed,
        heads_other,
        merge_other,
        lanes(1.0 / scale_other),
        ones,
        cosines,
        sines,
        bias_column,
        branch,
        other,
    )
    heads_got, merge_got = chip(heads_far), chip(merge_far)
    heads_near, merge_near, turn_own, keep, send = attend_backward(
        normed,
        heads_own,
        merge_weight,
        lanes(1.0 / cosine_scale),
        ones,
        cosines,
        sines,
        bias_column,
        branch,
        own,
        (keep, send),
    )
    tokens_grad, adapt_first_grad = norm_back(
        keep, (core(send),), tokens, middle_grad, scale_first, False
    )

    bits = [1 << b for b in range(dp.bit_length() - 1)]
    turned = bits[1:2] + bits[:1] + bits[2:]
    blocks = [
        reduce_over(grads[j], turned if j == 2 else bits, dp, index) for j in range(grads.shape[0])
    ]
    merge_sum = reduce_over(
        (merge_near.astype(F32) + merge_got.astype(F32)).astype(BF16), turned, dp, index
    )
    heads_sum = [
        reduce_over(
            (heads_near[c].astype(F32) + heads_got[c].astype(F32)).astype(BF16), bits, dp, index
        )
        for c in range(3)
    ]
    blocks = jnp.stack(blocks).astype(F32).reshape(-1, 3, CHUNK, width)
    reduce_total = blocks[:, 0].reshape(units, width)
    expand_total = jnp.transpose(blocks[:, 1:], (3, 1, 0, 2)).reshape(width, 2, units)
    heads_total = jnp.transpose(jnp.stack(heads_sum).astype(F32), (1, 0, 2))
    merge_total = merge_sum.astype(F32)

    first_low = adapt_first_grad.reshape(local_images, width).astype(BF16)
    second_low = adapt_second_grad.reshape(local_images, width).astype(BF16)
    condition_grad = nt(first_low, adapt_first) + nt(second_low, adapt_second)
    pad = ((0, 0), (0, width - condition.shape[1]))
    turn_far_got = chip(turn_far)
    turn = jnp.pad(turn_own + turn_far_got, ((0, 0), (0, width - local)))
    payload = jnp.concatenate(
        [
            first_low.astype(F32),
            second_low.astype(F32),
            jnp.pad(condition.astype(F32), pad),
            turn,
            jnp.zeros((1, width), F32),
        ],
        0,
    )[None]
    for bit in bits:
        payload = jnp.concatenate([payload, swap(payload, "dp", dp, bit)], 0)
    turn_total = jnp.sum(payload[:, 3 * local_images, :local], 0)
    for bit in (1, 2):
        payload = jnp.concatenate([payload, swap(payload, "mp", mp, bit)], 0)
    n = local_images
    first_all = payload[:, :n].reshape(-1, width).astype(BF16)
    second_all = payload[:, n : 2 * n].reshape(-1, width).astype(BF16)
    condition_all = payload[:, 2 * n : 3 * n, : condition.shape[1]]
    condition_all = condition_all.reshape(-1, condition.shape[1]).astype(BF16)
    first_total = tn(condition_all, first_all)
    second_total = tn(condition_all, second_all)
    scale_total = turn_total[::HEAD_DIM] / (2.0 * cosine_scale)
    return (
        layer_out,
        tokens_grad,
        condition_grad,
        heads_total,
        merge_total,
        expand_total,
        reduce_total,
        first_total,
        second_total,
        scale_total,
    )


def solution(mesh):
    split = P(("dp", "mp"), None)
    return jax.shard_map(
        functools.partial(per_device, mesh.shape["dp"], mesh.shape["mp"]),
        mesh=mesh,
        in_specs=(
            split,
            split,
            P(("dp", "mp")),
            P(None, None, "mp"),
            P("mp", None),
            P(None, None, "mp"),
            P("mp", None),
            P(),
            P(),
            P("mp"),
            split,
        ),
        out_specs=(
            split,
            split,
            split,
            P(None, None, "mp"),
            P("mp", None),
            P(None, None, "mp"),
            P("mp", None),
            P(),
            P(),
            P("mp"),
        ),
        check_vma=False,
    )
```

```python
import functools

import jax
import jax.numpy as jnp
import numpy as np
from jax import lax
from jax.experimental import pallas as pl
from jax.experimental.pallas import tpu as pltpu
from jax.sharding import PartitionSpec as P

HEAD_DIM = 64
BUCKET = 256
EPS = 1e-06
NEG = -1e30
GRID_ROWS = np.array([16, 12, 21, 14, 18, 12, 16, 10, 20, 8, 24, 11, 22, 8, 32, 13], np.int32)
GRID_COLS = np.array([16, 21, 12, 18, 14, 16, 12, 20, 10, 24, 8, 22, 11, 32, 8, 13], np.int32)
F32 = jnp.float32
BF16 = jnp.bfloat16
VMEM_LIMIT = 56 * 1024 * 1024
GELU_A = float(np.sqrt(2.0 / np.pi))
GELU_B = 0.044715
CHUNK = 256


def nn(a, b):
    return lax.dot_general(a, b, (((1,), (0,)), ((), ())), preferred_element_type=F32)


def nt(a, b):
    return lax.dot_general(a, b, (((1,), (1,)), ((), ())), preferred_element_type=F32)


def tn(a, b):
    return lax.dot_general(a, b, (((0,), (0,)), ((), ())), preferred_element_type=F32)


def params():
    return pltpu.CompilerParams(vmem_limit_bytes=VMEM_LIMIT, dimension_semantics=("arbitrary",))


def cost():
    return pl.CostEstimate(flops=1000, bytes_accessed=1000, transcendentals=0)


def whole(shape):
    return pl.BlockSpec(shape, lambda i: (0,) * len(shape))


def rows(block, width):
    return pl.BlockSpec((block, width), lambda i: (i, 0))


def norm_first_kernel(x_ref, s_ref, out_ref):
    x = x_ref[...].astype(F32)
    r = lax.rsqrt(jnp.mean(x * x, -1, keepdims=True) + EPS)
    out_ref[...] = (x * r * s_ref[0]).astype(BF16)


def norm_first(tokens, scale):
    n, d = tokens.shape
    return pl.pallas_call(
        norm_first_kernel,
        grid=(n // BUCKET,),
        in_specs=[rows(BUCKET, d), pl.BlockSpec((1, 1, d), lambda i: (i, 0, 0))],
        out_specs=rows(BUCKET, d),
        out_shape=jax.ShapeDtypeStruct((n, d), BF16),
        compiler_params=params(),
        cost_estimate=cost(),
        name="norm_first",
    )(tokens, scale)


def norm_second_kernel(x_ref, part_ref, recv_ref, s_ref, mid_ref, out_ref):
    x = x_ref[...].astype(F32) + (part_ref[...] + recv_ref[...].astype(F32))
    mid_ref[...] = x
    r = lax.rsqrt(jnp.mean(x * x, -1, keepdims=True) + EPS)
    out_ref[...] = (x * r * s_ref[0]).astype(BF16)


def norm_second(tokens, part, recv, scale):
    n, d = tokens.shape
    return pl.pallas_call(
        norm_second_kernel,
        grid=(n // BUCKET,),
        in_specs=[rows(BUCKET, d)] * 3 + [pl.BlockSpec((1, 1, d), lambda i: (i, 0, 0))],
        out_specs=[rows(BUCKET, d)] * 2,
        out_shape=[jax.ShapeDtypeStruct((n, d), F32), jax.ShapeDtypeStruct((n, d), BF16)],
        compiler_params=params(),
        cost_estimate=cost(),
        name="norm_second",
    )(tokens, part, recv, scale)


def norm_back_kernel(extra, low, *refs):
    part_ref = refs[0]
    more = refs[1 : 1 + extra]
    x_ref, g_ref, s_ref = refs[1 + extra : 4 + extra]
    outs = refs[4 + extra :]
    grad = part_ref[...]
    for ref in more:
        grad = grad + ref[...].astype(F32)
    x = x_ref[...].astype(F32)
    r = lax.rsqrt(jnp.mean(x * x, -1, keepdims=True) + EPS)
    u = grad * s_ref[0]
    back = g_ref[...].astype(F32) + r * u - x * (r * r * r * jnp.mean(u * x, -1, keepdims=True))
    outs[0][...] = back
    outs[1][0] = jnp.sum(grad * x * r, 0, keepdims=True)
    if low:
        outs[2][...] = back.astype(BF16)


def norm_back(part, more, x, g, scale, low):
    n, d = x.shape
    per_image = pl.BlockSpec((1, 1, d), lambda i: (i, 0, 0))
    outs = [jax.ShapeDtypeStruct((n, d), F32), jax.ShapeDtypeStruct((n // BUCKET, 1, d), F32)]
    specs = [rows(BUCKET, d), per_image]
    if low:
        outs.append(jax.ShapeDtypeStruct((n, d), BF16))
        specs.append(rows(BUCKET, d))
    return pl.pallas_call(
        functools.partial(norm_back_kernel, len(more), low),
        grid=(n // BUCKET,),
        in_specs=[rows(BUCKET, d)] * (3 + len(more)) + [per_image],
        out_specs=specs,
        out_shape=outs,
        compiler_params=params(),
        cost_estimate=cost(),
        name="norm_back",
    )(part, *more, x, g, scale)


def head_sums(values, block_ones):
    high = values.astype(BF16)
    low = (values - high.astype(F32)).astype(BF16)
    return nn(high, block_ones) + nn(low, block_ones)


def partner(values):
    parts = []
    for start in range(0, values.shape[1], 128):
        part = values[:, start : start + 128]
        lane = lax.broadcasted_iota(jnp.int32, part.shape, 1) % HEAD_DIM
        parts.append(
            jnp.where(lane < HEAD_DIM // 4, pltpu.roll(part, 128 - 16, 1), pltpu.roll(part, 16, 1))
        )
    return jnp.concatenate(parts, 1)


def head_mask(shape, head):
    lane = lax.broadcasted_iota(jnp.int32, shape, 1)
    return (lane >= head * HEAD_DIM) & (lane < (head + 1) * HEAD_DIM)


def by_head(scale_ref, heads):
    row = jnp.zeros((1, heads * HEAD_DIM), F32)
    for head in range(heads):
        row = jnp.where(head_mask(row.shape, head), scale_ref[head], row)
    return row


def block_of_ones(width):
    a = lax.broadcasted_iota(jnp.int32, (width, width), 0) // HEAD_DIM
    b = lax.broadcasted_iota(jnp.int32, (width, width), 1) // HEAD_DIM
    return jnp.where(a == b, 1.0, 0.0).astype(BF16)


PLACES = 32


def turn_table():
    lane = np.arange(128) % HEAD_DIM
    quarter = HEAD_DIM // 8
    freqs = 10000.0 ** (-np.arange(quarter) / quarter)
    angles = np.arange(PLACES)[:, None] * freqs[lane % quarter][None, :]
    turns = lane < HEAD_DIM // 2
    by_row = (lane // quarter) % 2 == 0
    sign = np.where(lane < HEAD_DIM // 4, -1.0, 1.0)
    cosines = np.where(turns, np.cos(angles), 1.0)
    sines = np.where(turns, np.sin(angles) * sign, 0.0)
    both = np.concatenate([cosines, sines], 1)
    by_row = np.concatenate([by_row, by_row])
    table = np.concatenate([np.where(by_row, both, 0.0), np.where(by_row, 0.0, both)], 0)
    table = table.astype(np.float32)
    high = table.astype(jnp.bfloat16)
    rest = table - high.astype(np.float32)
    mid = rest.astype(jnp.bfloat16)
    low = (rest - mid.astype(np.float32)).astype(jnp.bfloat16)
    return np.stack([high, mid, low])


def turns_of(grid_rows, grid_cols, table_ref, width):
    place = lax.broadcasted_iota(jnp.int32, (BUCKET, 2 * PLACES), 0).astype(F32)
    lane = lax.broadcasted_iota(jnp.int32, (BUCKET, 2 * PLACES), 1).astype(F32)
    cols = jnp.full((1, 1), grid_cols, jnp.int32).astype(F32)
    row = jnp.floor((place + 0.5) / cols)
    col = place - row * cols
    hot = (lane == row) | (lane - PLACES == col)
    hot = jnp.where(hot, 1.0, 0.0).astype(BF16)
    both = nn(hot, table_ref[0]) + nn(hot, table_ref[1]) + nn(hot, table_ref[2])
    cosines, sines = both[:, :128], both[:, 128:]
    copies = width // 128
    return jnp.concatenate([cosines] * copies, 1), jnp.concatenate([sines] * copies, 1)


def grid_of(bucket_ref, dims_ref, image):
    bucket = bucket_ref[image]
    return dims_ref[0, bucket], dims_ref[1, bucket]


def smem():
    return pl.BlockSpec(memory_space=pltpu.SMEM)


def attend_forward_kernel(
    merge, heads, step, bucket_ref, dims_ref, scale_ref, table_ref, n_ref, w_ref, *refs
):
    if merge:
        other_ref, m_own_ref, m_ref = refs[:3]
        refs = refs[3:]
    q_ref, k_ref, v_ref, cq_ref, ck_ref, mixed_ref = refs[:6]
    width = heads * HEAD_DIM
    ones = block_of_ones(width)
    root = jnp.sqrt(by_head(scale_ref, heads))
    first = pl.program_id(0) * step
    normed = n_ref[...]

    raw = [nn(normed, w_ref[which]) for which in range(3)]
    v_ref[...] = raw[2].astype(BF16)
    tables = []
    for image in range(step):
        grid_rows, grid_cols = grid_of(bucket_ref, dims_ref, first + image)
        tables.append((*turns_of(grid_rows, grid_cols, table_ref, width), grid_rows * grid_cols))
    cosines = jnp.concatenate([t[0] for t in tables], 0)
    sines = jnp.concatenate([t[1] for t in tables], 0)
    for which, (out_ref, c_ref) in enumerate(((q_ref, cq_ref), (k_ref, ck_ref))):
        c = lax.rsqrt(head_sums(raw[which] * raw[which], ones) + EPS) * root
        c_ref[...] = c.astype(BF16)
        n = raw[which] * c
        out_ref[...] = (n * cosines + partner(n) * sines).astype(BF16)
    for image in range(step):
        at = pl.ds(image * BUCKET, BUCKET)
        q, k, v = q_ref[at, :], k_ref[at, :], v_ref[at, :]
        key = lax.broadcasted_iota(jnp.int32, (1, BUCKET), 1)
        bias = jnp.where(key < tables[image][2], 0.0, NEG)
        zero = jnp.zeros_like(q)
        probs, values = [], []
        for head in range(heads):
            mask = head_mask((BUCKET, width), head)
            e = jnp.exp(nt(jnp.where(mask, q, zero), k) + bias)
            probs.append((e * (1.0 / jnp.sum(e, -1, keepdims=True))).astype(BF16))
            values.append(jnp.where(mask, v, zero))
        mixed = nn(jnp.concatenate(probs, 1), jnp.concatenate(values, 0)).astype(BF16)
        mixed_ref[at, :] = mixed
    if merge:
        keep_ref, send_ref = refs[6:]
        part = nn(other_ref[...], m_own_ref[...]) + nn(mixed_ref[...], m_ref[...])
        half = pl.num_programs(0) // 2

        @pl.when(pl.program_id(0) < half)
        def _():
            keep_ref[...] = part

        @pl.when(pl.program_id(0) >= half)
        def _():
            send_ref[...] = part.astype(BF16)


def attend_forward(buckets, scale, table, normed, weight, merge=None, step=2):
    n, d = normed.shape
    width = weight.shape[2]
    images = n // BUCKET
    heads = width // HEAD_DIM
    count = images // step
    half = count // 2
    tile = step * BUCKET
    block = rows(tile, width)
    dims = jnp.asarray(np.stack([GRID_ROWS, GRID_COLS]))
    in_specs = [smem()] * 3 + [whole(table.shape), rows(tile, d), whole(weight.shape)]
    operands = [buckets, dims, scale, table, normed, weight]
    out_specs = [block] * 6
    outs = [jax.ShapeDtypeStruct((n, width), t) for t in (BF16,) * 6]
    if merge is not None:
        other, own_weight, merge_weight = merge
        in_specs += [block, whole(own_weight.shape), whole(merge_weight.shape)]
        operands += [other, own_weight, merge_weight]
        out_specs += [
            pl.BlockSpec((tile, d), lambda i: (jnp.minimum(i, half - 1), 0)),
            pl.BlockSpec((tile, d), lambda i: (jnp.maximum(i - half, 0), 0)),
        ]
        outs += [
            jax.ShapeDtypeStruct((n // 2, d), F32),
            jax.ShapeDtypeStruct((n // 2, d), BF16),
        ]
    return pl.pallas_call(
        functools.partial(attend_forward_kernel, merge is not None, heads, step),
        grid=(count,),
        in_specs=in_specs,
        out_specs=out_specs,
        out_shape=outs,
        compiler_params=params(),
        cost_estimate=cost(),
        name="attend_forward",
    )(*operands)


def attend_backward_kernel(
    second,
    heads,
    bucket_ref,
    dims_ref,
    scale_ref,
    table_ref,
    n_ref,
    m_ref,
    b_own_ref,
    b_core_ref,
    q_ref,
    k_ref,
    v_ref,
    cq_ref,
    ck_ref,
    mixed_ref,
    *refs,
):
    if second:
        w_ref, w_far_ref, far_ref = refs[:3]
        grad_ref, rest_ref, turn_ref, keep_ref, send_ref, tg_ref, all_ref, macc_ref = refs[3:]
    else:
        grad_ref, rest_ref, turn_ref, out_ref, tg_ref, all_ref, macc_ref = refs
    i = pl.program_id(0)
    images = pl.num_programs(0) - 1
    width = heads * HEAD_DIM

    @pl.when(i < images)
    def _():
        grid_rows, grid_cols = grid_of(bucket_ref, dims_ref, i)
        cosines, sines = turns_of(grid_rows, grid_cols, table_ref, width)
        ones = block_of_ones(width)
        inv = 1.0 / by_head(scale_ref, heads)
        key = lax.broadcasted_iota(jnp.int32, (BUCKET, 1), 0)
        bias = jnp.where(key < grid_rows * grid_cols, 0.0, NEG)
        branch = jnp.where(i < images // 2, b_own_ref[...], b_core_ref[...])
        q, k, v = q_ref[...], k_ref[...], v_ref[...]
        mixed = mixed_ref[...]
        dmix = nt(branch, m_ref[...]).astype(BF16)
        prod = (dmix.astype(F32) * mixed.astype(F32)).astype(BF16)
        lane_head = lax.broadcasted_iota(jnp.int32, (16, width), 1) // HEAD_DIM
        picks = lax.broadcasted_iota(jnp.int32, (16, width), 0) == lane_head
        deltas = nt(jnp.where(picks, 1.0, 0.0).astype(BF16), prod)
        zero = jnp.zeros_like(q)
        masks = [head_mask((BUCKET, width), head) for head in range(heads)]
        qs = [jnp.where(mask, q, zero) for mask in masks]
        ks = [jnp.where(mask, k, zero) for mask in masks]
        dhs = [jnp.where(mask, dmix, zero) for mask in masks]
        probs_all, ds_all = [], []
        for head in range(heads):
            e = jnp.exp(nt(k, qs[head]) + bias)
            probs = e * (1.0 / jnp.sum(e, 0, keepdims=True))
            dprobs = nt(v, dhs[head])
            probs_all.append(probs.astype(BF16))
            ds_all.append((probs * (dprobs - deltas[head : head + 1, :])).astype(BF16))
        dv = nn(jnp.concatenate(probs_all, 1), jnp.concatenate(dhs, 0))
        dk = nn(jnp.concatenate(ds_all, 1), jnp.concatenate(qs, 0))
        dq = tn(jnp.concatenate(ds_all, 0), jnp.concatenate(ks, 0))

        def back(low, grad, c):
            full = low.astype(F32)
            sums = head_sums(full * grad, ones)
            t = grad - full * (sums * inv)
            out = (c * (t * cosines - partner(t) * sines)).astype(BF16)
            return out, jnp.sum(sums, 0, keepdims=True)

        gq, sq = back(q, dq, cq_ref[...].astype(F32))
        gk, sk = back(k, dk, ck_ref[...].astype(F32))
        gv = dv.astype(BF16)
        at = pl.ds(pl.multiple_of(i * BUCKET, BUCKET), BUCKET)
        tg_ref[at, :width] = gq
        tg_ref[at, width : 2 * width] = gk
        tg_ref[at, 2 * width :] = gv
        all_ref[at, :] = n_ref[...]
        mg = tn(mixed, branch)

        @pl.when(i == 0)
        def _():
            turn_ref[...] = sq + sk
            macc_ref[...] = mg

        @pl.when(i > 0)
        def _():
            turn_ref[...] += sq + sk
            macc_ref[...] += mg

        if not second:
            out_ref[:, :width] = gq
            out_ref[:, width : 2 * width] = gk
            out_ref[:, 2 * width :] = gv
        else:
            part = nt(gq, w_ref[0]) + nt(gk, w_ref[1]) + nt(gv, w_ref[2])
            for which in range(3):
                part = part + nt(far_ref[:, which * width : (which + 1) * width], w_far_ref[which])

            @pl.when(i < images // 2)
            def _():
                keep_ref[...] = part

            @pl.when(i >= images // 2)
            def _():
                send_ref[...] = part.astype(BF16)

    @pl.when(i == images)
    def _():
        grad_ref[...] = tn(tg_ref[:, : 2 * width], all_ref[...]).astype(BF16)
        rest_ref[:width, :] = tn(tg_ref[:, 2 * width :], all_ref[...]).astype(BF16)
        rest_ref[width:, :] = macc_ref[...].astype(BF16)


def attend_backward(buckets, scale, table, normed, merge_weight, branch, saved, weights=None):
    n, d = normed.shape
    width = merge_weight.shape[0]
    images = n // BUCKET
    heads = width // HEAD_DIM
    half = images // 2

    def clip(i, low, high):
        return jnp.minimum(jnp.maximum(i - low, 0), high)

    image = pl.BlockSpec((BUCKET, width), lambda i: (clip(i, 0, images - 1), 0))
    triple = pl.BlockSpec((BUCKET, 3 * width), lambda i: (clip(i, 0, images - 1), 0))
    wide = pl.BlockSpec((BUCKET, d), lambda i: (clip(i, 0, images - 1), 0))
    keep_spec = pl.BlockSpec((BUCKET, d), lambda i: (clip(i, 0, half - 1), 0))
    send_spec = pl.BlockSpec((BUCKET, d), lambda i: (clip(i, half, half - 1), 0))
    dims = jnp.asarray(np.stack([GRID_ROWS, GRID_COLS]))
    in_specs = [smem()] * 3 + [
        whole(table.shape),
        wide,
        whole(merge_weight.shape),
        keep_spec,
        send_spec,
    ] + [image] * 6
    operands = [buckets, dims, scale, table, normed, merge_weight, *branch, *saved]
    out_specs = [whole((2 * width, d))] * 2 + [whole((1, width))]
    outs = [jax.ShapeDtypeStruct((2 * width, d), BF16)] * 2 + [jax.ShapeDtypeStruct((1, width), F32)]
    if weights is not None:
        in_specs += [whole(weights[0].shape)] * 2 + [triple]
        operands += list(weights)
        out_specs += [keep_spec, send_spec]
        outs += [jax.ShapeDtypeStruct((n // 2, d), F32), jax.ShapeDtypeStruct((n // 2, d), BF16)]
    else:
        out_specs.append(triple)
        outs.append(jax.ShapeDtypeStruct((n, 3 * width), BF16))
    return pl.pallas_call(
        functools.partial(attend_backward_kernel, weights is not None, heads),
        grid=(images + 1,),
        in_specs=in_specs,
        out_specs=out_specs,
        out_shape=outs,
        scratch_shapes=[
            pltpu.VMEM((n, 3 * width), BF16),
            pltpu.VMEM((n, d), BF16),
            pltpu.VMEM((width, d), F32),
        ],
        compiler_params=params(),
        cost_estimate=cost(),
        name="attend_backward",
    )(*operands)


def geglu_kernel(second, tile, na_ref, nb_ref, ga_ref, gb_ref, e_ref, r_ref, *refs):
    if second:
        prev_ref = refs[0]
        refs = refs[1:]
    o_keep_ref, o_send_ref, n_keep_ref, n_send_ref, grad_ref = refs[:5]
    n_all, g_all, e_all, r_all, act, o_keep, o_send, n_keep, n_send, grad = refs[5:15]
    sems = refs[-1]
    half = na_ref.shape[0]
    units = r_ref.shape[0]
    count = [0]

    def copy(source, target):
        made = pltpu.make_async_copy(source, target, sems.at[count[0]])
        count[0] += 1
        made.start()
        return made

    waits = {}
    starts = range(0, units, CHUNK)
    waits["na"] = copy(na_ref, n_all.at[:half])
    for u in starts:
        waits["e", u] = copy(e_ref.at[:, :, u : u + CHUNK], e_all.at[:, :, u : u + CHUNK])
    waits["ga"] = copy(ga_ref, g_all.at[:half])
    waits["r"] = copy(r_ref, r_all)
    waits["nb"] = copy(nb_ref, n_all.at[half:])
    waits["gb"] = copy(gb_ref, g_all.at[half:])
    if second:
        waits["prev"] = copy(prev_ref, refs[15])

    def ready(*keys):
        for key in keys:
            if key in waits:
                waits.pop(key).wait()

    outs = []
    for t in range(0, 2 * half, tile):
        first = t < half
        ready("na" if first else "nb")
        at = slice(t, t + tile)
        normed = n_all[at, :]
        for u in starts:
            here = slice(u, u + CHUNK)
            ready(("e", u))
            gate = nn(normed, e_all[0, :, here])
            up = nn(normed, e_all[1, :, here])
            ready("ga" if first else "gb", "r")
            hgrad = nt(g_all[at, :], r_all[here, :])
            square = gate * gate
            th = jnp.tanh(gate * (GELU_A + (GELU_A * GELU_B) * square))
            slant = 0.5 * (1.0 + th)
            gelu = gate * slant
            bend = (0.5 * GELU_A) + (1.5 * GELU_A * GELU_B) * square
            slope = slant + gate * (1.0 - th * th) * bend
            act[0, at, here] = (gelu * up).astype(BF16)
            act[1, at, here] = (hgrad * up * slope).astype(BF16)
            act[2, at, here] = (hgrad * gelu).astype(BF16)
        o_part = nn(act[0, at, :], r_all[...])
        n_part = nt(act[1, at, :], e_all[0]) + nt(act[2, at, :], e_all[1])
        local = slice(t % half, t % half + tile)
        if first:
            n_keep[local, :] = n_part
            o_keep[local, :] = o_part
        else:
            n_send[local, :] = n_part.astype(BF16)
            o_send[local, :] = o_part.astype(BF16)
        for source, target in (
            (n_keep, n_keep_ref) if first else (n_send, n_send_ref),
            (o_keep, o_keep_ref) if first else (o_send, o_send_ref),
        ):
            outs.append(copy(source.at[local, :], target.at[local, :]))
    ready("prev")
    for which in range(3):
        total = tn(act[which], (g_all if which == 0 else n_all)[...])
        here = slice(which * units, (which + 1) * units)
        if second:
            total = total + refs[15][here, :].astype(F32)
        grad[here, :] = total.astype(BF16)
        outs.append(copy(grad.at[here, :], grad_ref.at[here, :]))
    for out in outs:
        out.wait()


def geglu(normed_a, normed_b, grad_a, grad_b, expand, reduce, prev=None):
    half, d = normed_a.shape
    units = reduce.shape[0]
    tile = min(half, 256)
    operands = [normed_a, normed_b, grad_a, grad_b, expand, reduce]
    if prev is not None:
        operands.append(prev)
    anywhere = pl.BlockSpec(memory_space=pl.ANY)
    copies = 6 + units // CHUNK + 4 * half // tile + 3
    scratch = [
        pltpu.VMEM((2 * half, d), BF16),
        pltpu.VMEM((2 * half, d), BF16),
        pltpu.VMEM(expand.shape, BF16),
        pltpu.VMEM(reduce.shape, BF16),
        pltpu.VMEM((3, 2 * half, units), BF16),
        pltpu.VMEM((half, d), F32),
        pltpu.VMEM((half, d), BF16),
        pltpu.VMEM((half, d), F32),
        pltpu.VMEM((half, d), BF16),
        pltpu.VMEM((3 * units, d), BF16),
    ]
    if prev is not None:
        scratch.append(pltpu.VMEM((3 * units, d), BF16))
    scratch.append(pltpu.SemaphoreType.DMA((copies,)))
    return pl.pallas_call(
        functools.partial(geglu_kernel, prev is not None, tile),
        in_specs=[anywhere] * len(operands),
        out_specs=[anywhere] * 5,
        out_shape=[
            jax.ShapeDtypeStruct((half, d), F32),
            jax.ShapeDtypeStruct((half, d), BF16),
            jax.ShapeDtypeStruct((half, d), F32),
            jax.ShapeDtypeStruct((half, d), BF16),
            jax.ShapeDtypeStruct((3 * units, d), BF16),
        ],
        scratch_shapes=scratch,
        compiler_params=pltpu.CompilerParams(vmem_limit_bytes=VMEM_LIMIT),
        cost_estimate=cost(),
        name="geglu",
    )(*operands)


def finish_geglu_kernel(mine_ref, x_ref, x_got_ref, y_ref, *refs):
    *y_got_refs, reduce_ref, expand_ref = refs
    def order(which, own, got):
        mine = mine_ref[which] != 0
        return jnp.where(mine, got, own), jnp.where(mine, own, got)

    y_got = jnp.concatenate([ref[...] for ref in y_got_refs], 0)
    parts = [*order(0, x_ref[...], x_got_ref[...]), *order(1, y_ref[...], y_got)]
    units = reduce_ref.shape[0]
    rows = jnp.concatenate(parts, 0).astype(F32)
    reduce_ref[...] = rows[:units]
    expand_ref[:, 0, :] = rows[units : 2 * units].T
    expand_ref[:, 1, :] = rows[2 * units :].T


def finish_geglu(mine, halves, units):
    d = halves[0].shape[1]
    block = min(d, 256)
    return pl.pallas_call(
        finish_geglu_kernel,
        grid=(d // block,),
        in_specs=[smem()]
        + [pl.BlockSpec((half.shape[0], block), lambda i: (0, i)) for half in halves],
        out_specs=[
            pl.BlockSpec((units, block), lambda i: (0, i)),
            pl.BlockSpec((block, 2, units), lambda i: (i, 0, 0)),
        ],
        out_shape=[
            jax.ShapeDtypeStruct((units, d), F32),
            jax.ShapeDtypeStruct((d, 2, units), F32),
        ],
        compiler_params=params(),
        cost_estimate=cost(),
        name="finish_geglu",
    )(mine, *halves)


def finish_attend_kernel(mine_ref, x_ref, x_got_ref, y_ref, y_got_ref, heads_ref, merge_ref):
    def order(which, own, got):
        mine = mine_ref[which] != 0
        return jnp.where(mine, got, own), jnp.where(mine, own, got)

    q, k = order(0, x_ref[...], x_got_ref[...])
    v, merge = order(0, y_ref[...], y_got_ref[...])
    for which, part in enumerate((q, k, v)):
        heads_ref[which] = part.astype(F32).T
    merge_ref[...] = merge.astype(F32)


def finish_attend(mine, halves):
    count, d = halves[0].shape
    block = min(d, 256)
    part = pl.BlockSpec((count, block), lambda i: (0, i))
    return pl.pallas_call(
        finish_attend_kernel,
        grid=(d // block,),
        in_specs=[smem()] + [part] * 4,
        out_specs=[pl.BlockSpec((3, block, count), lambda i: (0, i, 0)), part],
        out_shape=[
            jax.ShapeDtypeStruct((3, d, count), F32),
            jax.ShapeDtypeStruct((count, d), F32),
        ],
        compiler_params=params(),
        cost_estimate=cost(),
        name="finish_attend",
    )(mine, *halves)


def swap(values, axis, size, bit):
    return lax.ppermute(values, axis, [(i, i ^ bit) for i in range(size)])


def after(values, *before):
    return lax.optimization_barrier((values, *before))[0]


def fetch_parts(values, dp, index):
    if dp < 4:
        return (values,)
    part = values.shape[1] // 4
    place = index & 3
    return tuple(
        lax.dynamic_slice_in_dim(values, which * part, part, 1) for which in (place, place ^ 3)
    )


def split_terms(values):
    high = lax.reduce_precision(values, 8, 7)
    mid = lax.reduce_precision(values - high, 8, 7)
    return [term.astype(BF16) for term in (high, mid, values - high - mid)]


def pack_row(values, width):
    rows = jnp.stack(split_terms(values))
    return jnp.pad(rows, ((0, 13), (0, width - values.shape[0])))


def unpack_row(block, count):
    return jnp.sum(block[:3, :count].astype(F32), 0)


def relay_parts(near, dp):
    return [] if dp < 4 else [swap(near, "dp", dp, 1), swap(near, "dp", dp, 2)]


def assemble_parts(near, others, dp, index):
    if dp < 4:
        return near
    pieces = [near, *others]
    low, high = (index & 1) != 0, (index & 2) != 0
    a, b = jnp.where(low, pieces[1], pieces[0]), jnp.where(low, pieces[0], pieces[1])
    c, d = jnp.where(low, pieces[3], pieces[2]), jnp.where(low, pieces[2], pieces[3])
    first, last = jnp.where(high, c, a), jnp.where(high, a, c)
    second, third = jnp.where(high, d, b), jnp.where(high, b, d)
    return jnp.concatenate([first, second, last, third], 1)


ORDER = "mMgGaAbBm12aAgGbB@3aAgGbB!@4gb%B@"


class Reduction:
    def __init__(self, x, order, size, index, short=False):
        self.x, self.size, self.index = x, size, index
        down = order[:-1] if short else order
        self.steps = [(bit, "half") for bit in down]
        self.steps += [(bit, "add") for bit in order[len(down) :]]
        self.steps += [(bit, "double") for bit in reversed(down)]
        self.flying = None

    def split(self, *before):
        bit, kind = self.steps[0]
        if kind != "half":
            if before:
                self.x = after(self.x, *before)
            return self.x
        mine = (self.index & bit) != 0
        half = self.x.shape[0] // 2
        low, high = self.x[:half], self.x[half:]
        self.x = jnp.where(mine, high, low)
        return jnp.where(mine, low, high)

    def start(self, *before):
        bit = self.steps[0][0]
        sent = self.split(*before)
        self.flying = swap(sent, "dp", self.size, bit)

    def start_piece(self, which, count, *before):
        bit = self.steps[0][0]
        part = self.x.shape[0] // count
        sent = after(self.x[which * part : (which + 1) * part], *before)
        self.flying = (self.flying if which else []) + [swap(sent, "dp", self.size, bit)]

    def end(self, *before):
        bit, kind = self.steps.pop(0)
        mine = (self.index & bit) != 0
        got = after(self.flying, *before) if before else self.flying
        if kind == "double":
            parts = jnp.where(mine, got, self.x), jnp.where(mine, self.x, got)
            self.x = jnp.concatenate(parts, 0)
        else:
            self.x = (self.x.astype(F32) + got.astype(F32)).astype(BF16)

    def halves(self, *before):
        got = self.flying if isinstance(self.flying, list) else [self.flying]
        return [self.x, *(after(part, *before) for part in got)]


class Pair:
    def __init__(self, first, second, bits, turned, size, index):
        self.parts = Reduction(first, bits, size, index), Reduction(second, turned, size, index)
        self.size, self.both = size, None

    @property
    def x(self):
        return tuple(part.x for part in self.parts)

    def start(self):
        one, two = self.parts
        bit = one.steps[0][0]
        if bit != two.steps[0][0]:
            one.start()
            two.start()
            return
        self.both = swap(jnp.stack([one.split(), two.split()]), "dp", self.size, bit)

    def end(self, *before):
        one, two = self.parts
        if self.both is not None:
            both = after(self.both, *before)
            one.flying, two.flying, self.both = both[0], both[1], None
            before = ()
        one.end(*before)
        two.end(*before)


class Gather:
    def __init__(self, x, steps):
        self.x, self.steps = x, steps

    def start(self):
        axis, size, bit = self.steps[0]
        self.flying = swap(self.x, axis, size, bit)

    def end(self, *before):
        self.steps.pop(0)
        self.x = jnp.concatenate([self.x, after(self.flying, *before)], 0)


def per_device(
    dp,
    mp,
    tokens,
    condition,
    buckets,
    heads_weight,
    merge_weight,
    expand_weight,
    reduce_weight,
    adapt_first,
    adapt_second,
    cosine_scale,
    cotangent,
):
    own_rows, width = tokens.shape
    local_images = buckets.shape[0]
    local = cosine_scale.shape[0] * HEAD_DIM
    units = reduce_weight.shape[0]
    index = lax.axis_index("dp")
    core = functools.partial(swap, axis="mp", size=mp, bit=1)
    chip = functools.partial(swap, axis="mp", size=mp, bit=2)

    heads_own = jnp.transpose(heads_weight, (1, 0, 2))
    heads_parts = fetch_parts(heads_own, dp, index)
    tokens, *heads_parts = lax.optimization_barrier((tokens, *heads_parts))

    scale_first = 1.0 + jnp.dot(condition, adapt_first, preferred_element_type=F32)
    scale_first = scale_first.reshape(local_images, 1, width)
    normed_own = norm_first(tokens, scale_first)
    heads_near = chip(heads_parts[0])
    merge_packed = jnp.concatenate(
        [after(merge_weight, normed_own), pack_row(cosine_scale, width)], 0
    )
    buckets_chip = jnp.concatenate([buckets, core(buckets)], 0)
    normed = jnp.concatenate([normed_own, core(normed_own)], 0)
    normed, heads_near, cotangent_late, merge_packed, *cross = lax.optimization_barrier(
        (normed, heads_near, cotangent, merge_packed, *heads_parts[1:])
    )
    cross = [chip(part) for part in cross]
    relayed = relay_parts(heads_near, dp)
    merge_other = chip(merge_packed)
    cot_core = core(cotangent_late)
    table = jnp.asarray(turn_table())
    own = attend_forward(buckets_chip, cosine_scale, table, normed, heads_own)

    expand_own = jnp.transpose(after(expand_weight, own[5]), (1, 0, 2))
    scale_second = 1.0 + jnp.dot(
        after(condition, own[5]), adapt_second, preferred_element_type=F32
    )
    scale_second = scale_second.reshape(local_images, 1, width)
    expand_own = lax.optimization_barrier((expand_own, scale_second))[0]
    cot_first = chip(after(cotangent_late[: own_rows // 2], expand_own))
    *pieces, merge_other = lax.optimization_barrier(
        (*relayed, *cross, merge_other, expand_own)
    )[:-1]
    heads_other = assemble_parts(heads_near, pieces, dp, index)
    scale_other = unpack_row(merge_other[local:], cosine_scale.shape[0])
    merge_other = merge_other[:local]
    heads_other, expand_own, scale_second, merge_other, scale_other = lax.optimization_barrier(
        (heads_other, expand_own, scale_second, merge_other, scale_other)
    )
    cot_last = chip(after(cotangent_late[own_rows // 2 :], heads_other))
    *other, keep, send = attend_forward(
        buckets_chip, scale_other, table, normed, heads_other, (own[5], merge_weight, merge_other)
    )
    send, cot_first, cot_last, cot_core = lax.optimization_barrier(
        (send, cot_first, cot_last, cot_core)
    )
    middle, second_own = norm_second(tokens, keep, core(send), scale_second)
    second_chip = chip(second_own)
    second_core = core(second_own)
    cot_chip = jnp.concatenate([after(cot_first, second_own), cot_last], 0)
    cot_far = core(cot_chip)

    o_keep, o_send, n_keep, n_send, grads = geglu(
        second_own, second_core, cotangent, cot_core, expand_own, reduce_weight
    )
    second_chip, cot_far, grads = lax.optimization_barrier((second_chip, cot_far, grads))
    second_far = core(second_chip)
    o_near, n_near = core(o_send), core(n_send)
    o_chip, o_far, n_chip, n_far, grads = geglu(
        second_chip, second_far, cot_chip, cot_far, expand_own, reduce_weight, grads
    )

    bits = [1 << b for b in range(dp.bit_length() - 1)]
    turned = bits[1:2] + bits[:1] + bits[2:]
    n_pair = (n_chip + core(n_far).astype(F32)).astype(BF16)
    n_pair, grads = lax.optimization_barrier((n_pair, grads))
    n_sum = chip(n_pair)
    cut = 3 * units // 2
    mlp = Pair(grads[:cut], grads[cut:], bits, turned, dp, index)
    mlp.start()
    middle_grad, adapt_second_grad, branch_own = norm_back(
        after(n_keep, *mlp.x), (n_near, n_sum), middle, cotangent, scale_second, True
    )
    branch_core = core(branch_own)
    o_pair = (o_chip + after(core(after(o_far, n_pair)), branch_own).astype(F32)).astype(BF16)
    o_sum = chip(o_pair)
    mlp.end(branch_own)
    mlp.start()
    branch = lax.optimization_barrier((branch_own, branch_core, o_pair, *mlp.x))[:2]

    far_a, far_b, turn_far, triple_far = attend_backward(
        buckets_chip, scale_other, table, normed, merge_other, branch, other
    )
    got_a, got_b = chip(far_a), chip(far_b)
    o_sum = after(o_sum, far_a)
    mlp.end(far_a, o_sum)
    mlp.start()
    branch = lax.optimization_barrier((*branch, *mlp.x))[:2]
    near_a, near_b, turn_own, keep, send = attend_backward(
        buckets_chip,
        cosine_scale,
        table,
        normed,
        merge_weight,
        branch,
        own,
        (heads_own, heads_other, triple_far),
    )
    near_a, near_b, send, got_a, mlp.both = lax.optimization_barrier(
        (near_a, near_b, send, got_a, mlp.both)
    )
    attend_a = Reduction(
        (near_a.astype(F32) + got_a.astype(F32)).astype(BF16), bits, dp, index, True
    )
    attend_a.start()
    mlp.end(attend_a.x)
    mlp.start()
    tokens_grad, adapt_first_grad = norm_back(
        after(keep, *mlp.x), (core(send),), tokens, middle_grad, scale_first, False
    )
    n = local_images
    first_low = adapt_first_grad.reshape(n, width).astype(BF16)
    second_low = adapt_second_grad.reshape(n, width).astype(BF16)
    turn = split_terms(jnp.concatenate([turn_own, turn_far], 1))
    payload = jnp.concatenate(
        [
            first_low,
            second_low,
            jnp.pad(condition, ((0, 0), (0, width - condition.shape[1]))),
            jnp.concatenate([turn[0], turn[1]], 1),
            jnp.concatenate([turn[2], jnp.zeros_like(turn[2])], 1),
        ],
        0,
    )[None]
    adapters = Gather(
        payload, [("dp", dp, bit) for bit in bits] + [("mp", mp, bit) for bit in (1, 2)]
    )
    adapters.start()
    attend_a.end(tokens_grad)
    attend_a.start()
    attend_b = Reduction(
        (near_b.astype(F32) + after(got_b, attend_a.x).astype(F32)).astype(BF16),
        bits,
        dp,
        index,
        True,
    )
    attend_b.start()
    adapters.end(attend_b.x)
    adapters.start()
    middle, first_late = lax.optimization_barrier((middle, first_low, attend_b.x))[:2]
    layer_out = middle + (o_keep + o_near.astype(F32) + o_sum.astype(F32))
    condition_grad = nt(first_late, adapt_first) + nt(second_low, adapt_second)
    last = [adapters.x, layer_out, condition_grad]

    def end(one):
        one.end(*last)
        last.clear()
        last.extend(one.x if isinstance(one.x, tuple) else [one.x])

    def land(one):
        if isinstance(one.flying, list):
            one.flying[-1] = after(one.flying[-1], *last)
            last[:] = one.flying[-1:]
        else:
            one.flying = after(one.flying, *last)
            last[:] = [one.flying]

    names = {"a": attend_a, "b": attend_b, "m": mlp, "g": adapters}
    for name in ORDER if dp == 8 else "":
        if name in "!@%":
            land({"!": mlp.parts[0], "@": mlp.parts[1], "%": attend_a}[name])
        elif name == "1":
            mlp.parts[0].start(*last)
        elif name in "234":
            mlp.parts[1].start_piece(int(name) - 2, 3, *last)
        elif name.islower():
            end(names[name])
        else:
            names[name.lower()].start()
    if dp != 8:
        for one in (mlp, attend_a, attend_b):
            part = one.parts[0] if one is mlp else one
            while len(part.steps) > 1:
                end(one)
                one.start()
        while adapters.steps:
            end(adapters)
            if adapters.steps:
                adapters.start()
    everyone = adapters.x
    first_all = everyone[:, :n].reshape(-1, width)
    second_all = everyone[:, n : 2 * n].reshape(-1, width)
    condition_all = everyone[:, 2 * n : 3 * n, : condition.shape[1]]
    condition_all = condition_all.reshape(-1, condition.shape[1])
    first_total = tn(condition_all, first_all)
    second_total = tn(condition_all, second_all)
    turns = everyone[:, 3 * n :].astype(F32)
    turns = turns[:, 0, : 2 * local] + turns[:, 0, 2 * local : 4 * local] + turns[:, 1, : 2 * local]
    turn_total = jnp.sum(turns[:dp, :local], 0) + jnp.sum(turns[2 * dp : 3 * dp, local:], 0)
    scale_total = turn_total[::HEAD_DIM] / (2.0 * cosine_scale)
    mine = jnp.stack([index & 1, (index >> 1) & 1])
    reduce_total, expand_total = finish_geglu(
        mine, [half for part in mlp.parts for half in part.halves(*last, first_total)], units
    )
    heads_total, merge_total = finish_attend(
        mine,
        [half for part in (attend_a, attend_b) for half in part.halves(reduce_total)],
    )
    heads_total = jnp.transpose(heads_total, (1, 0, 2))
    return (
        layer_out,
        tokens_grad,
        condition_grad,
        heads_total,
        merge_total,
        expand_total,
        reduce_total,
        first_total,
        second_total,
        scale_total,
    )


def solution(mesh):
    split = P(("dp", "mp"), None)
    return jax.shard_map(
        functools.partial(per_device, mesh.shape["dp"], mesh.shape["mp"]),
        mesh=mesh,
        in_specs=(
            split,
            split,
            P(("dp", "mp")),
            P(None, None, "mp"),
            P("mp", None),
            P(None, None, "mp"),
            P("mp", None),
            P(),
            P(),
            P("mp"),
            split,
        ),
        out_specs=(
            split,
            split,
            split,
            P(None, None, "mp"),
            P("mp", None),
            P(None, None, "mp"),
            P("mp", None),
            P(),
            P(),
            P("mp"),
        ),
        check_vma=False,
    )
```

```python
import functools

import jax
import jax.numpy as jnp
import numpy as np
from jax import lax
from jax.experimental import pallas as pl
from jax.experimental.pallas import tpu as pltpu
from jax.sharding import PartitionSpec as P

HEAD_DIM = 64
BUCKET = 256
EPS = 1e-06
NEG = -1e30
GRID_ROWS = np.array([16, 12, 21, 14, 18, 12, 16, 10, 20, 8, 24, 11, 22, 8, 32, 13], np.int32)
GRID_COLS = np.array([16, 21, 12, 18, 14, 16, 12, 20, 10, 24, 8, 22, 11, 32, 8, 13], np.int32)
F32 = jnp.float32
BF16 = jnp.bfloat16
VMEM_LIMIT = 56 * 1024 * 1024
GELU_A = float(np.sqrt(2.0 / np.pi))
GELU_B = 0.044715
CHUNK = 256


def nn(a, b):
    return lax.dot_general(a, b, (((1,), (0,)), ((), ())), preferred_element_type=F32)


def nt(a, b):
    return lax.dot_general(a, b, (((1,), (1,)), ((), ())), preferred_element_type=F32)


def tn(a, b):
    return lax.dot_general(a, b, (((0,), (0,)), ((), ())), preferred_element_type=F32)


def params():
    return pltpu.CompilerParams(vmem_limit_bytes=VMEM_LIMIT, dimension_semantics=("arbitrary",))


def cost():
    return pl.CostEstimate(flops=1000, bytes_accessed=1000, transcendentals=0)


def whole(shape):
    return pl.BlockSpec(shape, lambda i: (0,) * len(shape))


def rows(block, width):
    return pl.BlockSpec((block, width), lambda i: (i, 0))


def norm_first_kernel(x_ref, s_ref, out_ref):
    x = x_ref[...].astype(F32)
    r = lax.rsqrt(jnp.mean(x * x, -1, keepdims=True) + EPS)
    out_ref[...] = (x * r * s_ref[0]).astype(BF16)


def norm_first(tokens, scale):
    n, d = tokens.shape
    return pl.pallas_call(
        norm_first_kernel,
        grid=(n // BUCKET,),
        in_specs=[rows(BUCKET, d), pl.BlockSpec((1, 1, d), lambda i: (i, 0, 0))],
        out_specs=rows(BUCKET, d),
        out_shape=jax.ShapeDtypeStruct((n, d), BF16),
        compiler_params=params(),
        cost_estimate=cost(),
        name="norm_first",
    )(tokens, scale)


def norm_second_kernel(x_ref, part_ref, recv_ref, s_ref, mid_ref, out_ref):
    x = x_ref[...].astype(F32) + (part_ref[...] + recv_ref[...].astype(F32))
    mid_ref[...] = x
    r = lax.rsqrt(jnp.mean(x * x, -1, keepdims=True) + EPS)
    out_ref[...] = (x * r * s_ref[0]).astype(BF16)


def norm_second(tokens, part, recv, scale):
    n, d = tokens.shape
    return pl.pallas_call(
        norm_second_kernel,
        grid=(n // BUCKET,),
        in_specs=[rows(BUCKET, d)] * 3 + [pl.BlockSpec((1, 1, d), lambda i: (i, 0, 0))],
        out_specs=[rows(BUCKET, d)] * 2,
        out_shape=[jax.ShapeDtypeStruct((n, d), F32), jax.ShapeDtypeStruct((n, d), BF16)],
        compiler_params=params(),
        cost_estimate=cost(),
        name="norm_second",
    )(tokens, part, recv, scale)


def norm_back_kernel(extra, low, *refs):
    part_ref = refs[0]
    more = refs[1 : 1 + extra]
    x_ref, g_ref, s_ref = refs[1 + extra : 4 + extra]
    outs = refs[4 + extra :]
    grad = part_ref[...]
    for ref in more:
        grad = grad + ref[...].astype(F32)
    x = x_ref[...].astype(F32)
    r = lax.rsqrt(jnp.mean(x * x, -1, keepdims=True) + EPS)
    u = grad * s_ref[0]
    back = g_ref[...].astype(F32) + r * u - x * (r * r * r * jnp.mean(u * x, -1, keepdims=True))
    outs[0][...] = back
    outs[1][0] = jnp.sum(grad * x * r, 0, keepdims=True)
    if low:
        outs[2][...] = back.astype(BF16)


def norm_back(part, more, x, g, scale, low):
    n, d = x.shape
    per_image = pl.BlockSpec((1, 1, d), lambda i: (i, 0, 0))
    outs = [jax.ShapeDtypeStruct((n, d), F32), jax.ShapeDtypeStruct((n // BUCKET, 1, d), F32)]
    specs = [rows(BUCKET, d), per_image]
    if low:
        outs.append(jax.ShapeDtypeStruct((n, d), BF16))
        specs.append(rows(BUCKET, d))
    return pl.pallas_call(
        functools.partial(norm_back_kernel, len(more), low),
        grid=(n // BUCKET,),
        in_specs=[rows(BUCKET, d)] * (3 + len(more)) + [per_image],
        out_specs=specs,
        out_shape=outs,
        compiler_params=params(),
        cost_estimate=cost(),
        name="norm_back",
    )(part, *more, x, g, scale)


def head_sums(values, block_ones):
    high = values.astype(BF16)
    low = (values - high.astype(F32)).astype(BF16)
    return nn(high, block_ones) + nn(low, block_ones)


def partner(values):
    parts = []
    for start in range(0, values.shape[1], 128):
        part = values[:, start : start + 128]
        lane = lax.broadcasted_iota(jnp.int32, part.shape, 1) % HEAD_DIM
        parts.append(
            jnp.where(lane < HEAD_DIM // 4, pltpu.roll(part, 128 - 16, 1), pltpu.roll(part, 16, 1))
        )
    return jnp.concatenate(parts, 1)


def head_mask(shape, head):
    lane = lax.broadcasted_iota(jnp.int32, shape, 1)
    return (lane >= head * HEAD_DIM) & (lane < (head + 1) * HEAD_DIM)


def by_head(scale_ref, heads):
    row = jnp.zeros((1, heads * HEAD_DIM), F32)
    for head in range(heads):
        row = jnp.where(head_mask(row.shape, head), scale_ref[head], row)
    return row


def block_of_ones(width):
    a = lax.broadcasted_iota(jnp.int32, (width, width), 0) // HEAD_DIM
    b = lax.broadcasted_iota(jnp.int32, (width, width), 1) // HEAD_DIM
    return jnp.where(a == b, 1.0, 0.0).astype(BF16)


PLACES = 32


def turn_table():
    lane = np.arange(128) % HEAD_DIM
    quarter = HEAD_DIM // 8
    freqs = 10000.0 ** (-np.arange(quarter) / quarter)
    angles = np.arange(PLACES)[:, None] * freqs[lane % quarter][None, :]
    turns = lane < HEAD_DIM // 2
    by_row = (lane // quarter) % 2 == 0
    sign = np.where(lane < HEAD_DIM // 4, -1.0, 1.0)
    cosines = np.where(turns, np.cos(angles), 1.0)
    sines = np.where(turns, np.sin(angles) * sign, 0.0)
    both = np.concatenate([cosines, sines], 1)
    by_row = np.concatenate([by_row, by_row])
    table = np.concatenate([np.where(by_row, both, 0.0), np.where(by_row, 0.0, both)], 0)
    table = table.astype(np.float32)
    high = table.astype(jnp.bfloat16)
    rest = table - high.astype(np.float32)
    mid = rest.astype(jnp.bfloat16)
    low = (rest - mid.astype(np.float32)).astype(jnp.bfloat16)
    return np.stack([high, mid, low])


def turns_of(grid_rows, grid_cols, table_ref, width):
    place = lax.broadcasted_iota(jnp.int32, (BUCKET, 2 * PLACES), 0).astype(F32)
    lane = lax.broadcasted_iota(jnp.int32, (BUCKET, 2 * PLACES), 1).astype(F32)
    cols = jnp.full((1, 1), grid_cols, jnp.int32).astype(F32)
    row = jnp.floor((place + 0.5) / cols)
    col = place - row * cols
    hot = (lane == row) | (lane - PLACES == col)
    hot = jnp.where(hot, 1.0, 0.0).astype(BF16)
    both = nn(hot, table_ref[0]) + nn(hot, table_ref[1]) + nn(hot, table_ref[2])
    cosines, sines = both[:, :128], both[:, 128:]
    copies = width // 128
    return jnp.concatenate([cosines] * copies, 1), jnp.concatenate([sines] * copies, 1)


def grid_of(bucket_ref, dims_ref, image):
    bucket = bucket_ref[image]
    return dims_ref[0, bucket], dims_ref[1, bucket]


def smem():
    return pl.BlockSpec(memory_space=pltpu.SMEM)


def attend_forward_kernel(
    merge, heads, step, bucket_ref, dims_ref, scale_ref, table_ref, n_ref, w_ref, *refs
):
    if merge:
        other_ref, m_own_ref, m_ref = refs[:3]
        refs = refs[3:]
    q_ref, k_ref, v_ref, cq_ref, ck_ref, mixed_ref = refs[:6]
    width = heads * HEAD_DIM
    ones = block_of_ones(width)
    root = jnp.sqrt(by_head(scale_ref, heads))
    first = pl.program_id(0) * step
    normed = n_ref[...]

    raw = [nn(normed, w_ref[which]) for which in range(3)]
    v_ref[...] = raw[2].astype(BF16)
    tables = []
    for image in range(step):
        grid_rows, grid_cols = grid_of(bucket_ref, dims_ref, first + image)
        tables.append((*turns_of(grid_rows, grid_cols, table_ref, width), grid_rows * grid_cols))
    cosines = jnp.concatenate([t[0] for t in tables], 0)
    sines = jnp.concatenate([t[1] for t in tables], 0)
    for which, (out_ref, c_ref) in enumerate(((q_ref, cq_ref), (k_ref, ck_ref))):
        c = lax.rsqrt(head_sums(raw[which] * raw[which], ones) + EPS) * root
        c_ref[...] = c.astype(BF16)
        n = raw[which] * c
        out_ref[...] = (n * cosines + partner(n) * sines).astype(BF16)
    for image in range(step):
        at = pl.ds(image * BUCKET, BUCKET)
        q, k, v = q_ref[at, :], k_ref[at, :], v_ref[at, :]
        key = lax.broadcasted_iota(jnp.int32, (1, BUCKET), 1)
        bias = jnp.where(key < tables[image][2], 0.0, NEG)
        zero = jnp.zeros_like(q)
        probs, values = [], []
        for head in range(heads):
            mask = head_mask((BUCKET, width), head)
            e = jnp.exp(nt(jnp.where(mask, q, zero), k) + bias)
            probs.append((e * (1.0 / jnp.sum(e, -1, keepdims=True))).astype(BF16))
            values.append(jnp.where(mask, v, zero))
        mixed = nn(jnp.concatenate(probs, 1), jnp.concatenate(values, 0)).astype(BF16)
        mixed_ref[at, :] = mixed
    if merge:
        keep_ref, send_ref = refs[6:]
        part = nn(other_ref[...], m_own_ref[...]) + nn(mixed_ref[...], m_ref[...])
        half = pl.num_programs(0) // 2

        @pl.when(pl.program_id(0) < half)
        def _():
            keep_ref[...] = part

        @pl.when(pl.program_id(0) >= half)
        def _():
            send_ref[...] = part.astype(BF16)


def attend_forward(buckets, scale, table, normed, weight, merge=None, step=2):
    n, d = normed.shape
    width = weight.shape[2]
    images = n // BUCKET
    heads = width // HEAD_DIM
    count = images // step
    half = count // 2
    tile = step * BUCKET
    block = rows(tile, width)
    dims = jnp.asarray(np.stack([GRID_ROWS, GRID_COLS]))
    in_specs = [smem()] * 3 + [whole(table.shape), rows(tile, d), whole(weight.shape)]
    operands = [buckets, dims, scale, table, normed, weight]
    out_specs = [block] * 6
    outs = [jax.ShapeDtypeStruct((n, width), t) for t in (BF16,) * 6]
    if merge is not None:
        other, own_weight, merge_weight = merge
        in_specs += [block, whole(own_weight.shape), whole(merge_weight.shape)]
        operands += [other, own_weight, merge_weight]
        out_specs += [
            pl.BlockSpec((tile, d), lambda i: (jnp.minimum(i, half - 1), 0)),
            pl.BlockSpec((tile, d), lambda i: (jnp.maximum(i - half, 0), 0)),
        ]
        outs += [
            jax.ShapeDtypeStruct((n // 2, d), F32),
            jax.ShapeDtypeStruct((n // 2, d), BF16),
        ]
    return pl.pallas_call(
        functools.partial(attend_forward_kernel, merge is not None, heads, step),
        grid=(count,),
        in_specs=in_specs,
        out_specs=out_specs,
        out_shape=outs,
        compiler_params=params(),
        cost_estimate=cost(),
        name="attend_forward",
    )(*operands)


def attend_backward_kernel(
    second,
    heads,
    bucket_ref,
    dims_ref,
    scale_ref,
    table_ref,
    n_ref,
    m_ref,
    b_own_ref,
    b_core_ref,
    q_ref,
    k_ref,
    v_ref,
    cq_ref,
    ck_ref,
    mixed_ref,
    *refs,
):
    if second:
        w_ref, w_far_ref, far_ref = refs[:3]
        grad_ref, rest_ref, turn_ref, keep_ref, send_ref, tg_ref, all_ref, macc_ref = refs[3:]
    else:
        grad_ref, rest_ref, turn_ref, out_ref, tg_ref, all_ref, macc_ref = refs
    i = pl.program_id(0)
    images = pl.num_programs(0) - 1
    width = heads * HEAD_DIM

    @pl.when(i < images)
    def _():
        grid_rows, grid_cols = grid_of(bucket_ref, dims_ref, i)
        cosines, sines = turns_of(grid_rows, grid_cols, table_ref, width)
        ones = block_of_ones(width)
        inv = 1.0 / by_head(scale_ref, heads)
        key = lax.broadcasted_iota(jnp.int32, (BUCKET, 1), 0)
        bias = jnp.where(key < grid_rows * grid_cols, 0.0, NEG)
        branch = jnp.where(i < images // 2, b_own_ref[...], b_core_ref[...])
        q, k, v = q_ref[...], k_ref[...], v_ref[...]
        mixed = mixed_ref[...]
        dmix = nt(branch, m_ref[...]).astype(BF16)
        prod = (dmix.astype(F32) * mixed.astype(F32)).astype(BF16)
        lane_head = lax.broadcasted_iota(jnp.int32, (16, width), 1) // HEAD_DIM
        picks = lax.broadcasted_iota(jnp.int32, (16, width), 0) == lane_head
        deltas = nt(jnp.where(picks, 1.0, 0.0).astype(BF16), prod)
        zero = jnp.zeros_like(q)
        masks = [head_mask((BUCKET, width), head) for head in range(heads)]
        qs = [jnp.where(mask, q, zero) for mask in masks]
        ks = [jnp.where(mask, k, zero) for mask in masks]
        dhs = [jnp.where(mask, dmix, zero) for mask in masks]
        probs_all, ds_all = [], []
        for head in range(heads):
            e = jnp.exp(nt(k, qs[head]) + bias)
            probs = e * (1.0 / jnp.sum(e, 0, keepdims=True))
            dprobs = nt(v, dhs[head])
            probs_all.append(probs.astype(BF16))
            ds_all.append((probs * (dprobs - deltas[head : head + 1, :])).astype(BF16))
        dv = nn(jnp.concatenate(probs_all, 1), jnp.concatenate(dhs, 0))
        dk = nn(jnp.concatenate(ds_all, 1), jnp.concatenate(qs, 0))
        dq = tn(jnp.concatenate(ds_all, 0), jnp.concatenate(ks, 0))

        def back(low, grad, c):
            full = low.astype(F32)
            sums = head_sums(full * grad, ones)
            t = grad - full * (sums * inv)
            out = (c * (t * cosines - partner(t) * sines)).astype(BF16)
            return out, jnp.sum(sums, 0, keepdims=True)

        gq, sq = back(q, dq, cq_ref[...].astype(F32))
        gk, sk = back(k, dk, ck_ref[...].astype(F32))
        gv = dv.astype(BF16)
        at = pl.ds(pl.multiple_of(i * BUCKET, BUCKET), BUCKET)
        tg_ref[at, :width] = gq
        tg_ref[at, width : 2 * width] = gk
        tg_ref[at, 2 * width :] = gv
        all_ref[at, :] = n_ref[...]
        mg = tn(mixed, branch)

        @pl.when(i == 0)
        def _():
            turn_ref[...] = sq + sk
            macc_ref[...] = mg

        @pl.when(i > 0)
        def _():
            turn_ref[...] += sq + sk
            macc_ref[...] += mg

        if not second:
            out_ref[:, :width] = gq
            out_ref[:, width : 2 * width] = gk
            out_ref[:, 2 * width :] = gv
        else:
            part = nt(gq, w_ref[0]) + nt(gk, w_ref[1]) + nt(gv, w_ref[2])
            for which in range(3):
                part = part + nt(far_ref[:, which * width : (which + 1) * width], w_far_ref[which])

            @pl.when(i < images // 2)
            def _():
                keep_ref[...] = part

            @pl.when(i >= images // 2)
            def _():
                send_ref[...] = part.astype(BF16)

    @pl.when(i == images)
    def _():
        grad_ref[...] = tn(tg_ref[:, : 2 * width], all_ref[...]).astype(BF16)
        rest_ref[:width, :] = tn(tg_ref[:, 2 * width :], all_ref[...]).astype(BF16)
        rest_ref[width:, :] = macc_ref[...].astype(BF16)


def attend_backward(buckets, scale, table, normed, merge_weight, branch, saved, weights=None):
    n, d = normed.shape
    width = merge_weight.shape[0]
    images = n // BUCKET
    heads = width // HEAD_DIM
    half = images // 2

    def clip(i, low, high):
        return jnp.minimum(jnp.maximum(i - low, 0), high)

    image = pl.BlockSpec((BUCKET, width), lambda i: (clip(i, 0, images - 1), 0))
    triple = pl.BlockSpec((BUCKET, 3 * width), lambda i: (clip(i, 0, images - 1), 0))
    wide = pl.BlockSpec((BUCKET, d), lambda i: (clip(i, 0, images - 1), 0))
    keep_spec = pl.BlockSpec((BUCKET, d), lambda i: (clip(i, 0, half - 1), 0))
    send_spec = pl.BlockSpec((BUCKET, d), lambda i: (clip(i, half, half - 1), 0))
    dims = jnp.asarray(np.stack([GRID_ROWS, GRID_COLS]))
    in_specs = [smem()] * 3 + [
        whole(table.shape),
        wide,
        whole(merge_weight.shape),
        keep_spec,
        send_spec,
    ] + [image] * 6
    operands = [buckets, dims, scale, table, normed, merge_weight, *branch, *saved]
    out_specs = [whole((2 * width, d))] * 2 + [whole((1, width))]
    outs = [jax.ShapeDtypeStruct((2 * width, d), BF16)] * 2 + [jax.ShapeDtypeStruct((1, width), F32)]
    if weights is not None:
        in_specs += [whole(weights[0].shape)] * 2 + [triple]
        operands += list(weights)
        out_specs += [keep_spec, send_spec]
        outs += [jax.ShapeDtypeStruct((n // 2, d), F32), jax.ShapeDtypeStruct((n // 2, d), BF16)]
    else:
        out_specs.append(triple)
        outs.append(jax.ShapeDtypeStruct((n, 3 * width), BF16))
    return pl.pallas_call(
        functools.partial(attend_backward_kernel, weights is not None, heads),
        grid=(images + 1,),
        in_specs=in_specs,
        out_specs=out_specs,
        out_shape=outs,
        scratch_shapes=[
            pltpu.VMEM((n, 3 * width), BF16),
            pltpu.VMEM((n, d), BF16),
            pltpu.VMEM((width, d), F32),
        ],
        compiler_params=params(),
        cost_estimate=cost(),
        name="attend_backward",
    )(*operands)


def geglu_kernel(second, tile, na_ref, nb_ref, ga_ref, gb_ref, e_ref, r_ref, *refs):
    if second:
        prev_ref = refs[0]
        refs = refs[1:]
    o_keep_ref, o_send_ref, n_keep_ref, n_send_ref, grad_ref = refs[:5]
    n_all, g_all, e_all, r_all, act, o_keep, o_send, n_keep, n_send, grad = refs[5:15]
    sems = refs[-1]
    half = na_ref.shape[0]
    units = r_ref.shape[0]
    count = [0]

    def copy(source, target):
        made = pltpu.make_async_copy(source, target, sems.at[count[0]])
        count[0] += 1
        made.start()
        return made

    waits = {}
    starts = range(0, units, CHUNK)
    waits["na"] = copy(na_ref, n_all.at[:half])
    for u in starts:
        waits["e", u] = copy(e_ref.at[:, :, u : u + CHUNK], e_all.at[:, :, u : u + CHUNK])
    waits["ga"] = copy(ga_ref, g_all.at[:half])
    waits["r"] = copy(r_ref, r_all)
    waits["nb"] = copy(nb_ref, n_all.at[half:])
    waits["gb"] = copy(gb_ref, g_all.at[half:])
    if second:
        waits["prev"] = copy(prev_ref, refs[15])

    def ready(*keys):
        for key in keys:
            if key in waits:
                waits.pop(key).wait()

    outs = []
    for t in range(0, 2 * half, tile):
        first = t < half
        ready("na" if first else "nb")
        at = slice(t, t + tile)
        normed = n_all[at, :]
        for u in starts:
            here = slice(u, u + CHUNK)
            ready(("e", u))
            gate = nn(normed, e_all[0, :, here])
            up = nn(normed, e_all[1, :, here])
            ready("ga" if first else "gb", "r")
            hgrad = nt(g_all[at, :], r_all[here, :])
            square = gate * gate
            th = jnp.tanh(gate * (GELU_A + (GELU_A * GELU_B) * square))
            slant = 0.5 * (1.0 + th)
            gelu = gate * slant
            bend = (0.5 * GELU_A) + (1.5 * GELU_A * GELU_B) * square
            slope = slant + gate * (1.0 - th * th) * bend
            act[0, at, here] = (gelu * up).astype(BF16)
            act[1, at, here] = (hgrad * up * slope).astype(BF16)
            act[2, at, here] = (hgrad * gelu).astype(BF16)
        o_part = nn(act[0, at, :], r_all[...])
        n_part = nt(act[1, at, :], e_all[0]) + nt(act[2, at, :], e_all[1])
        local = slice(t % half, t % half + tile)
        if first:
            n_keep[local, :] = n_part
            o_keep[local, :] = o_part
        else:
            n_send[local, :] = n_part.astype(BF16)
            o_send[local, :] = o_part.astype(BF16)
        for source, target in (
            (n_keep, n_keep_ref) if first else (n_send, n_send_ref),
            (o_keep, o_keep_ref) if first else (o_send, o_send_ref),
        ):
            outs.append(copy(source.at[local, :], target.at[local, :]))
    ready("prev")
    for which in range(3):
        total = tn(act[which], (g_all if which == 0 else n_all)[...])
        here = slice(which * units, (which + 1) * units)
        if second:
            total = total + refs[15][here, :].astype(F32)
        grad[here, :] = total.astype(BF16)
        outs.append(copy(grad.at[here, :], grad_ref.at[here, :]))
    for out in outs:
        out.wait()


def geglu(normed_a, normed_b, grad_a, grad_b, expand, reduce, prev=None):
    half, d = normed_a.shape
    units = reduce.shape[0]
    tile = min(half, 256)
    operands = [normed_a, normed_b, grad_a, grad_b, expand, reduce]
    if prev is not None:
        operands.append(prev)
    anywhere = pl.BlockSpec(memory_space=pl.ANY)
    copies = 6 + units // CHUNK + 4 * half // tile + 3
    scratch = [
        pltpu.VMEM((2 * half, d), BF16),
        pltpu.VMEM((2 * half, d), BF16),
        pltpu.VMEM(expand.shape, BF16),
        pltpu.VMEM(reduce.shape, BF16),
        pltpu.VMEM((3, 2 * half, units), BF16),
        pltpu.VMEM((half, d), F32),
        pltpu.VMEM((half, d), BF16),
        pltpu.VMEM((half, d), F32),
        pltpu.VMEM((half, d), BF16),
        pltpu.VMEM((3 * units, d), BF16),
    ]
    if prev is not None:
        scratch.append(pltpu.VMEM((3 * units, d), BF16))
    scratch.append(pltpu.SemaphoreType.DMA((copies,)))
    return pl.pallas_call(
        functools.partial(geglu_kernel, prev is not None, tile),
        in_specs=[anywhere] * len(operands),
        out_specs=[anywhere] * 5,
        out_shape=[
            jax.ShapeDtypeStruct((half, d), F32),
            jax.ShapeDtypeStruct((half, d), BF16),
            jax.ShapeDtypeStruct((half, d), F32),
            jax.ShapeDtypeStruct((half, d), BF16),
            jax.ShapeDtypeStruct((3 * units, d), BF16),
        ],
        scratch_shapes=scratch,
        compiler_params=pltpu.CompilerParams(vmem_limit_bytes=VMEM_LIMIT),
        cost_estimate=cost(),
        name="geglu",
    )(*operands)


def finish_geglu_kernel(mine_ref, x_ref, x_got_ref, y_ref, *refs):
    *y_got_refs, reduce_ref, expand_ref = refs
    def order(which, own, got):
        mine = mine_ref[which] != 0
        return jnp.where(mine, got, own), jnp.where(mine, own, got)

    y_got = jnp.concatenate([ref[...] for ref in y_got_refs], 0)
    parts = [*order(0, x_ref[...], x_got_ref[...]), *order(1, y_ref[...], y_got)]
    units = reduce_ref.shape[0]
    rows = jnp.concatenate(parts, 0).astype(F32)
    reduce_ref[...] = rows[:units]
    expand_ref[:, 0, :] = rows[units : 2 * units].T
    expand_ref[:, 1, :] = rows[2 * units :].T


def finish_geglu(mine, halves, units):
    d = halves[0].shape[1]
    block = min(d, 512)
    return pl.pallas_call(
        finish_geglu_kernel,
        grid=(d // block,),
        in_specs=[smem()]
        + [pl.BlockSpec((half.shape[0], block), lambda i: (0, i)) for half in halves],
        out_specs=[
            pl.BlockSpec((units, block), lambda i: (0, i)),
            pl.BlockSpec((block, 2, units), lambda i: (i, 0, 0)),
        ],
        out_shape=[
            jax.ShapeDtypeStruct((units, d), F32),
            jax.ShapeDtypeStruct((d, 2, units), F32),
        ],
        compiler_params=params(),
        cost_estimate=cost(),
        name="finish_geglu",
    )(mine, *halves)


def finish_attend_kernel(mine_ref, x_ref, x_got_ref, y_ref, y_got_ref, heads_ref, merge_ref):
    def order(which, own, got):
        mine = mine_ref[which] != 0
        return jnp.where(mine, got, own), jnp.where(mine, own, got)

    q, k = order(0, x_ref[...], x_got_ref[...])
    v, merge = order(0, y_ref[...], y_got_ref[...])
    for which, part in enumerate((q, k, v)):
        heads_ref[which] = part.astype(F32).T
    merge_ref[...] = merge.astype(F32)


def finish_attend(mine, halves):
    count, d = halves[0].shape
    block = min(d, 512)
    part = pl.BlockSpec((count, block), lambda i: (0, i))
    return pl.pallas_call(
        finish_attend_kernel,
        grid=(d // block,),
        in_specs=[smem()] + [part] * 4,
        out_specs=[pl.BlockSpec((3, block, count), lambda i: (0, i, 0)), part],
        out_shape=[
            jax.ShapeDtypeStruct((3, d, count), F32),
            jax.ShapeDtypeStruct((count, d), F32),
        ],
        compiler_params=params(),
        cost_estimate=cost(),
        name="finish_attend",
    )(mine, *halves)


def swap(values, axis, size, bit):
    return lax.ppermute(values, axis, [(i, i ^ bit) for i in range(size)])


def after(values, *before):
    return lax.optimization_barrier((values, *before))[0]


def fetch_parts(values, dp, index):
    if dp < 4:
        return (values,)
    part = values.shape[1] // 4
    place = index & 3
    return tuple(
        lax.dynamic_slice_in_dim(values, which * part, part, 1) for which in (place, place ^ 3)
    )


def split_terms(values):
    high = lax.reduce_precision(values, 8, 7)
    mid = lax.reduce_precision(values - high, 8, 7)
    return [term.astype(BF16) for term in (high, mid, values - high - mid)]


def pack_row(values, width):
    rows = jnp.stack(split_terms(values))
    return jnp.pad(rows, ((0, 13), (0, width - values.shape[0])))


def unpack_row(block, count):
    return jnp.sum(block[:3, :count].astype(F32), 0)


def relay_parts(near, dp):
    return [] if dp < 4 else [swap(near, "dp", dp, 1), swap(near, "dp", dp, 2)]


def assemble_parts(near, others, dp, index):
    if dp < 4:
        return near
    pieces = [near, *others]
    low, high = (index & 1) != 0, (index & 2) != 0
    a, b = jnp.where(low, pieces[1], pieces[0]), jnp.where(low, pieces[0], pieces[1])
    c, d = jnp.where(low, pieces[3], pieces[2]), jnp.where(low, pieces[2], pieces[3])
    first, last = jnp.where(high, c, a), jnp.where(high, a, c)
    second, third = jnp.where(high, d, b), jnp.where(high, b, d)
    return jnp.concatenate([first, second, last, third], 1)


ORDER = "mMgGaAbBm21aAbBgG@3aAbB@4gGb!%BgC"


class Reduction:
    def __init__(self, x, order, size, index, short=False):
        self.x, self.size, self.index = x, size, index
        down = order[:-1] if short else order
        self.steps = [(bit, "half") for bit in down]
        self.steps += [(bit, "add") for bit in order[len(down) :]]
        self.steps += [(bit, "double") for bit in reversed(down)]
        self.flying = None

    def split(self, *before):
        bit, kind = self.steps[0]
        if kind != "half":
            if before:
                self.x = after(self.x, *before)
            return self.x
        mine = (self.index & bit) != 0
        half = self.x.shape[0] // 2
        low, high = self.x[:half], self.x[half:]
        self.x = jnp.where(mine, high, low)
        return jnp.where(mine, low, high)

    def start(self, *before):
        bit = self.steps[0][0]
        sent = self.split(*before)
        self.flying = swap(sent, "dp", self.size, bit)

    def start_piece(self, which, count, *before):
        bit = self.steps[0][0]
        part = self.x.shape[0] // count
        sent = after(self.x[which * part : (which + 1) * part], *before)
        self.flying = (self.flying if which else []) + [swap(sent, "dp", self.size, bit)]

    def end(self, *before):
        bit, kind = self.steps.pop(0)
        mine = (self.index & bit) != 0
        got = after(self.flying, *before) if before else self.flying
        if kind == "double":
            parts = jnp.where(mine, got, self.x), jnp.where(mine, self.x, got)
            self.x = jnp.concatenate(parts, 0)
        else:
            self.x = (self.x.astype(F32) + got.astype(F32)).astype(BF16)

    def halves(self, *before):
        got = self.flying if isinstance(self.flying, list) else [self.flying]
        return [self.x, *(after(part, *before) for part in got)]


class Pair:
    def __init__(self, first, second, bits, turned, size, index):
        self.parts = Reduction(first, bits, size, index), Reduction(second, turned, size, index)
        self.size, self.both = size, None

    @property
    def x(self):
        return tuple(part.x for part in self.parts)

    def start(self):
        one, two = self.parts
        bit = one.steps[0][0]
        if bit != two.steps[0][0]:
            one.start()
            two.start()
            return
        self.both = swap(jnp.stack([one.split(), two.split()]), "dp", self.size, bit)

    def end(self, *before):
        one, two = self.parts
        if self.both is not None:
            both = after(self.both, *before)
            one.flying, two.flying, self.both = both[0], both[1], None
            before = ()
        one.end(*before)
        two.end(*before)


class Gather:
    def __init__(self, x, steps):
        self.x, self.steps = x, steps

    def start(self):
        axis, size, bit = self.steps[0]
        self.flying = swap(self.x, axis, size, bit)

    def end(self, *before):
        self.steps.pop(0)
        self.x = jnp.concatenate([self.x, after(self.flying, *before)], 0)


def per_device(
    dp,
    mp,
    tokens,
    condition,
    buckets,
    heads_weight,
    merge_weight,
    expand_weight,
    reduce_weight,
    adapt_first,
    adapt_second,
    cosine_scale,
    cotangent,
):
    own_rows, width = tokens.shape
    local_images = buckets.shape[0]
    local = cosine_scale.shape[0] * HEAD_DIM
    units = reduce_weight.shape[0]
    index = lax.axis_index("dp")
    core = functools.partial(swap, axis="mp", size=mp, bit=1)
    chip = functools.partial(swap, axis="mp", size=mp, bit=2)

    heads_own = jnp.transpose(heads_weight, (1, 0, 2))
    heads_parts = fetch_parts(heads_own, dp, index)
    tokens, *heads_parts = lax.optimization_barrier((tokens, *heads_parts))

    scale_first = 1.0 + jnp.dot(condition, adapt_first, preferred_element_type=F32)
    scale_first = scale_first.reshape(local_images, 1, width)
    normed_own = norm_first(tokens, scale_first)
    heads_near = chip(heads_parts[0])
    merge_packed = jnp.concatenate(
        [after(merge_weight, normed_own), pack_row(cosine_scale, width)], 0
    )
    buckets_chip = jnp.concatenate([buckets, core(buckets)], 0)
    normed = jnp.concatenate([normed_own, core(normed_own)], 0)
    normed, heads_near, cotangent_late, merge_packed, *cross = lax.optimization_barrier(
        (normed, heads_near, cotangent, merge_packed, *heads_parts[1:])
    )
    cross = [chip(part) for part in cross]
    relayed = relay_parts(heads_near, dp)
    merge_other = chip(merge_packed)
    cot_core = core(cotangent_late)
    table = jnp.asarray(turn_table())
    own = attend_forward(buckets_chip, cosine_scale, table, normed, heads_own)

    expand_own = jnp.transpose(after(expand_weight, own[5]), (1, 0, 2))
    scale_second = 1.0 + jnp.dot(
        after(condition, own[5]), adapt_second, preferred_element_type=F32
    )
    scale_second = scale_second.reshape(local_images, 1, width)
    expand_own = lax.optimization_barrier((expand_own, scale_second))[0]
    cot_first = chip(after(cotangent_late[: own_rows // 2], expand_own))
    *pieces, merge_other = lax.optimization_barrier(
        (*relayed, *cross, merge_other, expand_own)
    )[:-1]
    heads_other = assemble_parts(heads_near, pieces, dp, index)
    scale_other = unpack_row(merge_other[local:], cosine_scale.shape[0])
    merge_other = merge_other[:local]
    heads_other, expand_own, scale_second, merge_other, scale_other = lax.optimization_barrier(
        (heads_other, expand_own, scale_second, merge_other, scale_other)
    )
    cot_last = chip(after(cotangent_late[own_rows // 2 :], heads_other))
    *other, keep, send = attend_forward(
        buckets_chip, scale_other, table, normed, heads_other, (own[5], merge_weight, merge_other)
    )
    send, cot_first, cot_last, cot_core = lax.optimization_barrier(
        (send, cot_first, cot_last, cot_core)
    )
    middle, second_own = norm_second(tokens, keep, core(send), scale_second)
    second_chip = chip(second_own)
    second_core = core(second_own)
    cot_chip = jnp.concatenate([after(cot_first, second_own), cot_last], 0)
    cot_far = core(cot_chip)

    o_keep, o_send, n_keep, n_send, grads = geglu(
        second_own, second_core, cotangent, cot_core, expand_own, reduce_weight
    )
    second_chip, cot_far, grads = lax.optimization_barrier((second_chip, cot_far, grads))
    second_far = core(second_chip)
    o_near, n_near = core(o_send), core(n_send)
    o_chip, o_far, n_chip, n_far, grads = geglu(
        second_chip, second_far, cot_chip, cot_far, expand_own, reduce_weight, grads
    )

    bits = [1 << b for b in range(dp.bit_length() - 1)]
    turned = bits[1:2] + bits[:1] + bits[2:]
    n_pair = (n_chip + core(n_far).astype(F32)).astype(BF16)
    n_pair, grads = lax.optimization_barrier((n_pair, grads))
    n_sum = chip(n_pair)
    cut = 3 * units // 2
    mlp = Pair(grads[:cut], grads[cut:], bits, turned, dp, index)
    mlp.start()
    middle_grad, adapt_second_grad, branch_own = norm_back(
        after(n_keep, *mlp.x), (n_near, n_sum), middle, cotangent, scale_second, True
    )
    branch_core = core(branch_own)
    o_pair = (o_chip + after(core(after(o_far, n_pair)), branch_own).astype(F32)).astype(BF16)
    o_sum = chip(o_pair)
    mlp.end(branch_own)
    mlp.start()
    branch = lax.optimization_barrier((branch_own, branch_core, o_pair, *mlp.x))[:2]

    far_a, far_b, turn_far, triple_far = attend_backward(
        buckets_chip, scale_other, table, normed, merge_other, branch, other
    )
    got_a, got_b = chip(far_a), chip(far_b)
    o_sum = after(o_sum, far_a)
    mlp.end(far_a, o_sum)
    mlp.start()
    branch = lax.optimization_barrier((*branch, *mlp.x))[:2]
    near_a, near_b, turn_own, keep, send = attend_backward(
        buckets_chip,
        cosine_scale,
        table,
        normed,
        merge_weight,
        branch,
        own,
        (heads_own, heads_other, triple_far),
    )
    near_a, near_b, send, got_a, mlp.both = lax.optimization_barrier(
        (near_a, near_b, send, got_a, mlp.both)
    )
    attend_a = Reduction(
        (near_a.astype(F32) + got_a.astype(F32)).astype(BF16), bits, dp, index, True
    )
    attend_a.start()
    mlp.end(attend_a.x)
    mlp.start()
    tokens_grad, adapt_first_grad = norm_back(
        after(keep, *mlp.x), (core(send),), tokens, middle_grad, scale_first, False
    )
    n = local_images
    first_low = adapt_first_grad.reshape(n, width).astype(BF16)
    second_low = adapt_second_grad.reshape(n, width).astype(BF16)
    turn = split_terms(jnp.concatenate([turn_own, turn_far], 1))
    payload = jnp.concatenate(
        [
            first_low,
            second_low,
            jnp.pad(condition, ((0, 0), (0, width - condition.shape[1]))),
            jnp.concatenate([turn[0], turn[1]], 1),
            jnp.concatenate([turn[2], jnp.zeros_like(turn[2])], 1),
        ],
        0,
    )[None]
    adapters = Gather(
        payload, [("dp", dp, bit) for bit in bits] + [("mp", mp, bit) for bit in (1, 2)]
    )
    adapters.start()
    attend_a.end(tokens_grad)
    attend_a.start()
    attend_b = Reduction(
        (near_b.astype(F32) + after(got_b, attend_a.x).astype(F32)).astype(BF16),
        bits,
        dp,
        index,
        True,
    )
    attend_b.start()
    adapters.end(attend_b.x)
    adapters.start()
    middle, first_late = lax.optimization_barrier((middle, first_low, attend_b.x))[:2]
    layer_out = middle + (o_keep + o_near.astype(F32) + o_sum.astype(F32))
    condition_grad = nt(first_late, adapt_first) + nt(second_low, adapt_second)
    last = [adapters.x, layer_out, condition_grad]

    def end(one):
        one.end(*last)
        last.clear()
        last.extend(one.x if isinstance(one.x, tuple) else [one.x])

    def land(one):
        if isinstance(one.flying, list):
            one.flying[-1] = after(one.flying[-1], *last)
            last[:] = one.flying[-1:]
        else:
            one.flying = after(one.flying, *last)
            last[:] = [one.flying]

    def products():
        everyone = adapters.x
        first_all = everyone[:, :n].reshape(-1, width)
        second_all = everyone[:, n : 2 * n].reshape(-1, width)
        condition_all = everyone[:, 2 * n : 3 * n, : condition.shape[1]]
        condition_all = condition_all.reshape(-1, condition.shape[1])
        first_total = tn(condition_all, first_all)
        second_total = tn(condition_all, second_all)
        turns = everyone[:, 3 * n :].astype(F32)
        turns = turns[:, 0, : 2 * local] + turns[:, 0, 2 * local : 4 * local] + turns[:, 1, : 2 * local]
        turn_total = jnp.sum(turns[:dp, :local], 0) + jnp.sum(turns[2 * dp : 3 * dp, local:], 0)
        scale_total = turn_total[::HEAD_DIM] / (2.0 * cosine_scale)
        return first_total, second_total, scale_total

    names = {"a": attend_a, "b": attend_b, "m": mlp, "g": adapters}
    for name in ORDER if dp == 8 else "":
        if name == "C":
            first_total, second_total, scale_total = products()
            last[:] = [first_total, second_total]
            continue
        if name in "!@%":
            land({"!": mlp.parts[0], "@": mlp.parts[1], "%": attend_a}[name])
        elif name == "1":
            mlp.parts[0].start(*last)
        elif name in "234":
            mlp.parts[1].start_piece(int(name) - 2, 3, *last)
        elif name.islower():
            end(names[name])
        else:
            names[name.lower()].start()
    if dp != 8:
        for one in (mlp, attend_a, attend_b):
            part = one.parts[0] if one is mlp else one
            while len(part.steps) > 1:
                end(one)
                one.start()
        while adapters.steps:
            end(adapters)
            if adapters.steps:
                adapters.start()
        first_total, second_total, scale_total = products()
    if dp == 8 and "C" not in ORDER:
        first_total, second_total, scale_total = products()
    mine = jnp.stack([index & 1, (index >> 1) & 1])
    reduce_total, expand_total = finish_geglu(
        mine, [half for part in mlp.parts for half in part.halves(*last)], units
    )
    heads_total, merge_total = finish_attend(
        mine,
        [half for part in (attend_a, attend_b) for half in part.halves(reduce_total)],
    )
    heads_total = jnp.transpose(heads_total, (1, 0, 2))
    return (
        layer_out,
        tokens_grad,
        condition_grad,
        heads_total,
        merge_total,
        expand_total,
        reduce_total,
        first_total,
        second_total,
        scale_total,
    )


def solution(mesh):
    split = P(("dp", "mp"), None)
    return jax.shard_map(
        functools.partial(per_device, mesh.shape["dp"], mesh.shape["mp"]),
        mesh=mesh,
        in_specs=(
            split,
            split,
            P(("dp", "mp")),
            P(None, None, "mp"),
            P("mp", None),
            P(None, None, "mp"),
            P("mp", None),
            P(),
            P(),
            P("mp"),
            split,
        ),
        out_specs=(
            split,
            split,
            split,
            P(None, None, "mp"),
            P("mp", None),
            P(None, None, "mp"),
            P("mp", None),
            P(),
            P(),
            P("mp"),
        ),
        check_vma=False,
    )
```

```python
import functools

import jax
import jax.numpy as jnp
import numpy as np
from jax import lax
from jax.experimental import pallas as pl
from jax.experimental.pallas import tpu as pltpu
from jax.sharding import PartitionSpec as P

HEAD_DIM = 64
BUCKET = 256
EPS = 1e-06
NEG = -1e30
GRID_ROWS = np.array([16, 12, 21, 14, 18, 12, 16, 10, 20, 8, 24, 11, 22, 8, 32, 13], np.int32)
GRID_COLS = np.array([16, 21, 12, 18, 14, 16, 12, 20, 10, 24, 8, 22, 11, 32, 8, 13], np.int32)
F32 = jnp.float32
BF16 = jnp.bfloat16
VMEM_LIMIT = 56 * 1024 * 1024
GELU_A = float(np.sqrt(2.0 / np.pi))
GELU_B = 0.044715
CHUNK = 256


def nn(a, b):
    return lax.dot_general(a, b, (((1,), (0,)), ((), ())), preferred_element_type=F32)


def nt(a, b):
    return lax.dot_general(a, b, (((1,), (1,)), ((), ())), preferred_element_type=F32)


def tn(a, b):
    return lax.dot_general(a, b, (((0,), (0,)), ((), ())), preferred_element_type=F32)


def params():
    return pltpu.CompilerParams(vmem_limit_bytes=VMEM_LIMIT, dimension_semantics=("arbitrary",))


def cost():
    return pl.CostEstimate(flops=20_000_000_000, bytes_accessed=30_000_000, transcendentals=0)


def whole(shape):
    return pl.BlockSpec(shape, lambda i: (0,) * len(shape))


def rows(block, width):
    return pl.BlockSpec((block, width), lambda i: (i, 0))


def norm_first_kernel(x_ref, s_ref, out_ref):
    x = x_ref[...].astype(F32)
    r = lax.rsqrt(jnp.mean(x * x, -1, keepdims=True) + EPS)
    out_ref[...] = (x * r * s_ref[0]).astype(BF16)


def norm_first(tokens, scale):
    n, d = tokens.shape
    return pl.pallas_call(
        norm_first_kernel,
        grid=(n // BUCKET,),
        in_specs=[rows(BUCKET, d), pl.BlockSpec((1, 1, d), lambda i: (i, 0, 0))],
        out_specs=rows(BUCKET, d),
        out_shape=jax.ShapeDtypeStruct((n, d), BF16),
        compiler_params=params(),
        cost_estimate=cost(),
        name="norm_first",
    )(tokens, scale)


def norm_second_kernel(x_ref, part_ref, recv_ref, s_ref, mid_ref, out_ref):
    x = x_ref[...].astype(F32) + (part_ref[...] + recv_ref[...].astype(F32))
    mid_ref[...] = x
    r = lax.rsqrt(jnp.mean(x * x, -1, keepdims=True) + EPS)
    out_ref[...] = (x * r * s_ref[0]).astype(BF16)


def norm_second(tokens, part, recv, scale):
    n, d = tokens.shape
    return pl.pallas_call(
        norm_second_kernel,
        grid=(n // BUCKET,),
        in_specs=[rows(BUCKET, d)] * 3 + [pl.BlockSpec((1, 1, d), lambda i: (i, 0, 0))],
        out_specs=[rows(BUCKET, d)] * 2,
        out_shape=[jax.ShapeDtypeStruct((n, d), F32), jax.ShapeDtypeStruct((n, d), BF16)],
        compiler_params=params(),
        cost_estimate=cost(),
        name="norm_second",
    )(tokens, part, recv, scale)


def norm_back_kernel(extra, low, *refs):
    part_ref = refs[0]
    more = refs[1 : 1 + extra]
    x_ref, g_ref, s_ref = refs[1 + extra : 4 + extra]
    outs = refs[4 + extra :]
    grad = part_ref[...]
    for ref in more:
        grad = grad + ref[...].astype(F32)
    x = x_ref[...].astype(F32)
    r = lax.rsqrt(jnp.mean(x * x, -1, keepdims=True) + EPS)
    u = grad * s_ref[0]
    back = g_ref[...].astype(F32) + r * u - x * (r * r * r * jnp.mean(u * x, -1, keepdims=True))
    outs[0][...] = back
    outs[1][0] = jnp.sum(grad * x * r, 0, keepdims=True)
    if low:
        outs[2][...] = back.astype(BF16)


def norm_back(part, more, x, g, scale, low):
    n, d = x.shape
    per_image = pl.BlockSpec((1, 1, d), lambda i: (i, 0, 0))
    outs = [jax.ShapeDtypeStruct((n, d), F32), jax.ShapeDtypeStruct((n // BUCKET, 1, d), F32)]
    specs = [rows(BUCKET, d), per_image]
    if low:
        outs.append(jax.ShapeDtypeStruct((n, d), BF16))
        specs.append(rows(BUCKET, d))
    return pl.pallas_call(
        functools.partial(norm_back_kernel, len(more), low),
        grid=(n // BUCKET,),
        in_specs=[rows(BUCKET, d)] * (3 + len(more)) + [per_image],
        out_specs=specs,
        out_shape=outs,
        compiler_params=params(),
        cost_estimate=cost(),
        name="norm_back",
    )(part, *more, x, g, scale)


def head_sums(values, block_ones):
    high = values.astype(BF16)
    low = (values - high.astype(F32)).astype(BF16)
    return nn(high, block_ones) + nn(low, block_ones)


def partner(values):
    parts = []
    for start in range(0, values.shape[1], 128):
        part = values[:, start : start + 128]
        lane = lax.broadcasted_iota(jnp.int32, part.shape, 1) % HEAD_DIM
        parts.append(
            jnp.where(lane < HEAD_DIM // 4, pltpu.roll(part, 128 - 16, 1), pltpu.roll(part, 16, 1))
        )
    return jnp.concatenate(parts, 1)


def head_mask(shape, head):
    lane = lax.broadcasted_iota(jnp.int32, shape, 1)
    return (lane >= head * HEAD_DIM) & (lane < (head + 1) * HEAD_DIM)


def by_head(scale_ref, heads):
    row = jnp.zeros((1, heads * HEAD_DIM), F32)
    for head in range(heads):
        row = jnp.where(head_mask(row.shape, head), scale_ref[head], row)
    return row


def block_of_ones(width):
    a = lax.broadcasted_iota(jnp.int32, (width, width), 0) // HEAD_DIM
    b = lax.broadcasted_iota(jnp.int32, (width, width), 1) // HEAD_DIM
    return jnp.where(a == b, 1.0, 0.0).astype(BF16)


PLACES = 32


def turn_table():
    lane = np.arange(128) % HEAD_DIM
    quarter = HEAD_DIM // 8
    freqs = 10000.0 ** (-np.arange(quarter) / quarter)
    angles = np.arange(PLACES)[:, None] * freqs[lane % quarter][None, :]
    turns = lane < HEAD_DIM // 2
    by_row = (lane // quarter) % 2 == 0
    sign = np.where(lane < HEAD_DIM // 4, -1.0, 1.0)
    cosines = np.where(turns, np.cos(angles), 1.0)
    sines = np.where(turns, np.sin(angles) * sign, 0.0)
    both = np.concatenate([cosines, sines], 1)
    by_row = np.concatenate([by_row, by_row])
    table = np.concatenate([np.where(by_row, both, 0.0), np.where(by_row, 0.0, both)], 0)
    table = table.astype(np.float32)
    high = table.astype(jnp.bfloat16)
    rest = table - high.astype(np.float32)
    mid = rest.astype(jnp.bfloat16)
    low = (rest - mid.astype(np.float32)).astype(jnp.bfloat16)
    return np.stack([high, mid, low])


def turns_of(grid_rows, grid_cols, table_ref, width):
    place = lax.broadcasted_iota(jnp.int32, (BUCKET, 2 * PLACES), 0).astype(F32)
    lane = lax.broadcasted_iota(jnp.int32, (BUCKET, 2 * PLACES), 1).astype(F32)
    cols = jnp.full((1, 1), grid_cols, jnp.int32).astype(F32)
    row = jnp.floor((place + 0.5) / cols)
    col = place - row * cols
    hot = (lane == row) | (lane - PLACES == col)
    hot = jnp.where(hot, 1.0, 0.0).astype(BF16)
    both = nn(hot, table_ref[0]) + nn(hot, table_ref[1]) + nn(hot, table_ref[2])
    cosines, sines = both[:, :128], both[:, 128:]
    copies = width // 128
    return jnp.concatenate([cosines] * copies, 1), jnp.concatenate([sines] * copies, 1)


def grid_of(bucket_ref, dims_ref, image):
    bucket = bucket_ref[image]
    return dims_ref[0, bucket], dims_ref[1, bucket]


def smem():
    return pl.BlockSpec(memory_space=pltpu.SMEM)


def attend_forward_kernel(
    merge, heads, step, bucket_ref, dims_ref, scale_ref, table_ref, n_ref, w_ref, *refs
):
    if merge:
        other_ref, m_own_ref, m_ref = refs[:3]
        refs = refs[3:]
    q_ref, k_ref, v_ref, cq_ref, ck_ref, mixed_ref = refs[:6]
    width = heads * HEAD_DIM
    ones = block_of_ones(width)
    root = jnp.sqrt(by_head(scale_ref, heads))
    first = pl.program_id(0) * step
    normed = n_ref[...]

    raw = [nn(normed, w_ref[which]) for which in range(3)]
    v_ref[...] = raw[2].astype(BF16)
    tables = []
    for image in range(step):
        grid_rows, grid_cols = grid_of(bucket_ref, dims_ref, first + image)
        tables.append((*turns_of(grid_rows, grid_cols, table_ref, width), grid_rows * grid_cols))
    cosines = jnp.concatenate([t[0] for t in tables], 0)
    sines = jnp.concatenate([t[1] for t in tables], 0)
    for which, (out_ref, c_ref) in enumerate(((q_ref, cq_ref), (k_ref, ck_ref))):
        c = lax.rsqrt(head_sums(raw[which] * raw[which], ones) + EPS) * root
        c_ref[...] = c.astype(BF16)
        n = raw[which] * c
        out_ref[...] = (n * cosines + partner(n) * sines).astype(BF16)
    for image in range(step):
        at = pl.ds(image * BUCKET, BUCKET)
        q, k, v = q_ref[at, :], k_ref[at, :], v_ref[at, :]
        key = lax.broadcasted_iota(jnp.int32, (1, BUCKET), 1)
        bias = jnp.where(key < tables[image][2], 0.0, NEG)
        zero = jnp.zeros_like(q)
        probs, values = [], []
        for head in range(heads):
            mask = head_mask((BUCKET, width), head)
            e = jnp.exp(nt(jnp.where(mask, q, zero), k) + bias)
            probs.append((e * (1.0 / jnp.sum(e, -1, keepdims=True))).astype(BF16))
            values.append(jnp.where(mask, v, zero))
        mixed = nn(jnp.concatenate(probs, 1), jnp.concatenate(values, 0)).astype(BF16)
        mixed_ref[at, :] = mixed
    if merge:
        keep_ref, send_ref = refs[6:]
        part = nn(other_ref[...], m_own_ref[...]) + nn(mixed_ref[...], m_ref[...])
        half = pl.num_programs(0) // 2

        @pl.when(pl.program_id(0) < half)
        def _():
            keep_ref[...] = part

        @pl.when(pl.program_id(0) >= half)
        def _():
            send_ref[...] = part.astype(BF16)


def attend_forward(buckets, scale, table, normed, weight, merge=None, step=2):
    n, d = normed.shape
    width = weight.shape[2]
    images = n // BUCKET
    heads = width // HEAD_DIM
    count = images // step
    half = count // 2
    tile = step * BUCKET
    block = rows(tile, width)
    dims = jnp.asarray(np.stack([GRID_ROWS, GRID_COLS]))
    in_specs = [smem()] * 3 + [whole(table.shape), rows(tile, d), whole(weight.shape)]
    operands = [buckets, dims, scale, table, normed, weight]
    out_specs = [block] * 6
    outs = [jax.ShapeDtypeStruct((n, width), t) for t in (BF16,) * 6]
    if merge is not None:
        other, own_weight, merge_weight = merge
        in_specs += [block, whole(own_weight.shape), whole(merge_weight.shape)]
        operands += [other, own_weight, merge_weight]
        out_specs += [
            pl.BlockSpec((tile, d), lambda i: (jnp.minimum(i, half - 1), 0)),
            pl.BlockSpec((tile, d), lambda i: (jnp.maximum(i - half, 0), 0)),
        ]
        outs += [
            jax.ShapeDtypeStruct((n // 2, d), F32),
            jax.ShapeDtypeStruct((n // 2, d), BF16),
        ]
    return pl.pallas_call(
        functools.partial(attend_forward_kernel, merge is not None, heads, step),
        grid=(count,),
        in_specs=in_specs,
        out_specs=out_specs,
        out_shape=outs,
        compiler_params=params(),
        cost_estimate=cost(),
        name="attend_forward",
    )(*operands)


def attend_backward_kernel(
    second,
    heads,
    bucket_ref,
    dims_ref,
    scale_ref,
    table_ref,
    n_ref,
    m_ref,
    b_own_ref,
    b_core_ref,
    q_ref,
    k_ref,
    v_ref,
    cq_ref,
    ck_ref,
    mixed_ref,
    *refs,
):
    if second:
        w_ref, w_far_ref, far_ref = refs[:3]
        grad_ref, rest_ref, turn_ref, keep_ref, send_ref, tg_ref, all_ref, macc_ref = refs[3:]
    else:
        grad_ref, rest_ref, turn_ref, out_ref, tg_ref, all_ref, macc_ref = refs
    i = pl.program_id(0)
    images = pl.num_programs(0) - 1
    width = heads * HEAD_DIM

    @pl.when(i < images)
    def _():
        grid_rows, grid_cols = grid_of(bucket_ref, dims_ref, i)
        cosines, sines = turns_of(grid_rows, grid_cols, table_ref, width)
        ones = block_of_ones(width)
        inv = 1.0 / by_head(scale_ref, heads)
        key = lax.broadcasted_iota(jnp.int32, (BUCKET, 1), 0)
        bias = jnp.where(key < grid_rows * grid_cols, 0.0, NEG)
        branch = jnp.where(i < images // 2, b_own_ref[...], b_core_ref[...])
        q, k, v = q_ref[...], k_ref[...], v_ref[...]
        mixed = mixed_ref[...]
        dmix = nt(branch, m_ref[...]).astype(BF16)
        prod = (dmix.astype(F32) * mixed.astype(F32)).astype(BF16)
        lane_head = lax.broadcasted_iota(jnp.int32, (16, width), 1) // HEAD_DIM
        picks = lax.broadcasted_iota(jnp.int32, (16, width), 0) == lane_head
        deltas = nt(jnp.where(picks, 1.0, 0.0).astype(BF16), prod)
        zero = jnp.zeros_like(q)
        masks = [head_mask((BUCKET, width), head) for head in range(heads)]
        qs = [jnp.where(mask, q, zero) for mask in masks]
        ks = [jnp.where(mask, k, zero) for mask in masks]
        dhs = [jnp.where(mask, dmix, zero) for mask in masks]
        probs_all, ds_all = [], []
        for head in range(heads):
            e = jnp.exp(nt(k, qs[head]) + bias)
            probs = e * (1.0 / jnp.sum(e, 0, keepdims=True))
            dprobs = nt(v, dhs[head])
            probs_all.append(probs.astype(BF16))
            ds_all.append((probs * (dprobs - deltas[head : head + 1, :])).astype(BF16))
        dv = nn(jnp.concatenate(probs_all, 1), jnp.concatenate(dhs, 0))
        dk = nn(jnp.concatenate(ds_all, 1), jnp.concatenate(qs, 0))
        dq = tn(jnp.concatenate(ds_all, 0), jnp.concatenate(ks, 0))

        def back(low, grad, c):
            full = low.astype(F32)
            sums = head_sums(full * grad, ones)
            t = grad - full * (sums * inv)
            out = (c * (t * cosines - partner(t) * sines)).astype(BF16)
            return out, jnp.sum(sums, 0, keepdims=True)

        gq, sq = back(q, dq, cq_ref[...].astype(F32))
        gk, sk = back(k, dk, ck_ref[...].astype(F32))
        gv = dv.astype(BF16)
        at = pl.ds(pl.multiple_of(i * BUCKET, BUCKET), BUCKET)
        tg_ref[at, :width] = gq
        tg_ref[at, width : 2 * width] = gk
        tg_ref[at, 2 * width :] = gv
        all_ref[at, :] = n_ref[...]
        mg = tn(mixed, branch)

        @pl.when(i == 0)
        def _():
            turn_ref[...] = sq + sk
            macc_ref[...] = mg

        @pl.when(i > 0)
        def _():
            turn_ref[...] += sq + sk
            macc_ref[...] += mg

        if not second:
            out_ref[:, :width] = gq
            out_ref[:, width : 2 * width] = gk
            out_ref[:, 2 * width :] = gv
        else:
            part = nt(gq, w_ref[0]) + nt(gk, w_ref[1]) + nt(gv, w_ref[2])
            for which in range(3):
                part = part + nt(far_ref[:, which * width : (which + 1) * width], w_far_ref[which])

            @pl.when(i < images // 2)
            def _():
                keep_ref[...] = part

            @pl.when(i >= images // 2)
            def _():
                send_ref[...] = part.astype(BF16)

    @pl.when(i == images)
    def _():
        grad_ref[...] = tn(tg_ref[:, : 2 * width], all_ref[...]).astype(BF16)
        rest_ref[:width, :] = tn(tg_ref[:, 2 * width :], all_ref[...]).astype(BF16)
        rest_ref[width:, :] = macc_ref[...].astype(BF16)


def attend_backward(buckets, scale, table, normed, merge_weight, branch, saved, weights=None):
    n, d = normed.shape
    width = merge_weight.shape[0]
    images = n // BUCKET
    heads = width // HEAD_DIM
    half = images // 2

    def clip(i, low, high):
        return jnp.minimum(jnp.maximum(i - low, 0), high)

    image = pl.BlockSpec((BUCKET, width), lambda i: (clip(i, 0, images - 1), 0))
    triple = pl.BlockSpec((BUCKET, 3 * width), lambda i: (clip(i, 0, images - 1), 0))
    wide = pl.BlockSpec((BUCKET, d), lambda i: (clip(i, 0, images - 1), 0))
    keep_spec = pl.BlockSpec((BUCKET, d), lambda i: (clip(i, 0, half - 1), 0))
    send_spec = pl.BlockSpec((BUCKET, d), lambda i: (clip(i, half, half - 1), 0))
    dims = jnp.asarray(np.stack([GRID_ROWS, GRID_COLS]))
    in_specs = [smem()] * 3 + [
        whole(table.shape),
        wide,
        whole(merge_weight.shape),
        keep_spec,
        send_spec,
    ] + [image] * 6
    operands = [buckets, dims, scale, table, normed, merge_weight, *branch, *saved]
    out_specs = [whole((2 * width, d))] * 2 + [whole((1, width))]
    outs = [jax.ShapeDtypeStruct((2 * width, d), BF16)] * 2 + [jax.ShapeDtypeStruct((1, width), F32)]
    if weights is not None:
        in_specs += [whole(weights[0].shape)] * 2 + [triple]
        operands += list(weights)
        out_specs += [keep_spec, send_spec]
        outs += [jax.ShapeDtypeStruct((n // 2, d), F32), jax.ShapeDtypeStruct((n // 2, d), BF16)]
    else:
        out_specs.append(triple)
        outs.append(jax.ShapeDtypeStruct((n, 3 * width), BF16))
    return pl.pallas_call(
        functools.partial(attend_backward_kernel, weights is not None, heads),
        grid=(images + 1,),
        in_specs=in_specs,
        out_specs=out_specs,
        out_shape=outs,
        scratch_shapes=[
            pltpu.VMEM((n, 3 * width), BF16),
            pltpu.VMEM((n, d), BF16),
            pltpu.VMEM((width, d), F32),
        ],
        compiler_params=params(),
        cost_estimate=cost(),
        name="attend_backward",
    )(*operands)


def geglu_kernel(second, tile, na_ref, nb_ref, ga_ref, gb_ref, e_ref, r_ref, *refs):
    if second:
        prev_ref = refs[0]
        refs = refs[1:]
    o_keep_ref, o_send_ref, n_keep_ref, n_send_ref, grad_ref = refs[:5]
    n_all, g_all, e_all, r_all, act, o_keep, o_send, n_keep, n_send, grad = refs[5:15]
    sems = refs[-1]
    half = na_ref.shape[0]
    units = r_ref.shape[0]
    count = [0]

    def copy(source, target):
        made = pltpu.make_async_copy(source, target, sems.at[count[0]])
        count[0] += 1
        made.start()
        return made

    waits = {}
    starts = range(0, units, CHUNK)
    waits["na"] = copy(na_ref, n_all.at[:half])
    for u in starts:
        waits["e", u] = copy(e_ref.at[:, :, u : u + CHUNK], e_all.at[:, :, u : u + CHUNK])
    waits["ga"] = copy(ga_ref, g_all.at[:half])
    waits["r"] = copy(r_ref, r_all)
    waits["nb"] = copy(nb_ref, n_all.at[half:])
    waits["gb"] = copy(gb_ref, g_all.at[half:])
    if second:
        waits["prev"] = copy(prev_ref, refs[15])

    def ready(*keys):
        for key in keys:
            if key in waits:
                waits.pop(key).wait()

    outs = []
    for t in range(0, 2 * half, tile):
        first = t < half
        ready("na" if first else "nb")
        at = slice(t, t + tile)
        normed = n_all[at, :]
        for u in starts:
            here = slice(u, u + CHUNK)
            ready(("e", u))
            gate = nn(normed, e_all[0, :, here])
            up = nn(normed, e_all[1, :, here])
            ready("ga" if first else "gb", "r")
            hgrad = nt(g_all[at, :], r_all[here, :])
            square = gate * gate
            th = jnp.tanh(gate * (GELU_A + (GELU_A * GELU_B) * square))
            slant = 0.5 * (1.0 + th)
            gelu = gate * slant
            bend = (0.5 * GELU_A) + (1.5 * GELU_A * GELU_B) * square
            slope = slant + gate * (1.0 - th * th) * bend
            act[0, at, here] = (gelu * up).astype(BF16)
            act[1, at, here] = (hgrad * up * slope).astype(BF16)
            act[2, at, here] = (hgrad * gelu).astype(BF16)
        o_part = nn(act[0, at, :], r_all[...])
        n_part = nt(act[1, at, :], e_all[0]) + nt(act[2, at, :], e_all[1])
        local = slice(t % half, t % half + tile)
        if first:
            n_keep[local, :] = n_part
            o_keep[local, :] = o_part
        else:
            n_send[local, :] = n_part.astype(BF16)
            o_send[local, :] = o_part.astype(BF16)
        for source, target in (
            (n_keep, n_keep_ref) if first else (n_send, n_send_ref),
            (o_keep, o_keep_ref) if first else (o_send, o_send_ref),
        ):
            outs.append(copy(source.at[local, :], target.at[local, :]))
    ready("prev")
    for which in range(3):
        total = tn(act[which], (g_all if which == 0 else n_all)[...])
        here = slice(which * units, (which + 1) * units)
        if second:
            total = total + refs[15][here, :].astype(F32)
        grad[here, :] = total.astype(BF16)
        outs.append(copy(grad.at[here, :], grad_ref.at[here, :]))
    for out in outs:
        out.wait()


def geglu(normed_a, normed_b, grad_a, grad_b, expand, reduce, prev=None):
    half, d = normed_a.shape
    units = reduce.shape[0]
    tile = min(half, 256)
    operands = [normed_a, normed_b, grad_a, grad_b, expand, reduce]
    if prev is not None:
        operands.append(prev)
    anywhere = pl.BlockSpec(memory_space=pl.ANY)
    copies = 6 + units // CHUNK + 4 * half // tile + 3
    scratch = [
        pltpu.VMEM((2 * half, d), BF16),
        pltpu.VMEM((2 * half, d), BF16),
        pltpu.VMEM(expand.shape, BF16),
        pltpu.VMEM(reduce.shape, BF16),
        pltpu.VMEM((3, 2 * half, units), BF16),
        pltpu.VMEM((half, d), F32),
        pltpu.VMEM((half, d), BF16),
        pltpu.VMEM((half, d), F32),
        pltpu.VMEM((half, d), BF16),
        pltpu.VMEM((3 * units, d), BF16),
    ]
    if prev is not None:
        scratch.append(pltpu.VMEM((3 * units, d), BF16))
    scratch.append(pltpu.SemaphoreType.DMA((copies,)))
    return pl.pallas_call(
        functools.partial(geglu_kernel, prev is not None, tile),
        in_specs=[anywhere] * len(operands),
        out_specs=[anywhere] * 5,
        out_shape=[
            jax.ShapeDtypeStruct((half, d), F32),
            jax.ShapeDtypeStruct((half, d), BF16),
            jax.ShapeDtypeStruct((half, d), F32),
            jax.ShapeDtypeStruct((half, d), BF16),
            jax.ShapeDtypeStruct((3 * units, d), BF16),
        ],
        scratch_shapes=scratch,
        compiler_params=pltpu.CompilerParams(vmem_limit_bytes=VMEM_LIMIT),
        cost_estimate=cost(),
        name="geglu",
    )(*operands)


def finish_geglu_kernel(mine_ref, x_ref, x_got_ref, y_ref, *refs):
    *y_got_refs, reduce_ref, expand_ref = refs
    def order(which, own, got):
        mine = mine_ref[which] != 0
        return jnp.where(mine, got, own), jnp.where(mine, own, got)

    y_got = jnp.concatenate([ref[...] for ref in y_got_refs], 0)
    parts = [*order(0, x_ref[...], x_got_ref[...]), *order(1, y_ref[...], y_got)]
    units = reduce_ref.shape[0]
    rows = jnp.concatenate(parts, 0).astype(F32)
    reduce_ref[...] = rows[:units]
    expand_ref[:, 0, :] = rows[units : 2 * units].T
    expand_ref[:, 1, :] = rows[2 * units :].T


def finish_geglu(mine, halves, units):
    d = halves[0].shape[1]
    block = min(d, 512)
    return pl.pallas_call(
        finish_geglu_kernel,
        grid=(d // block,),
        in_specs=[smem()]
        + [pl.BlockSpec((half.shape[0], block), lambda i: (0, i)) for half in halves],
        out_specs=[
            pl.BlockSpec((units, block), lambda i: (0, i)),
            pl.BlockSpec((block, 2, units), lambda i: (i, 0, 0)),
        ],
        out_shape=[
            jax.ShapeDtypeStruct((units, d), F32),
            jax.ShapeDtypeStruct((d, 2, units), F32),
        ],
        compiler_params=params(),
        cost_estimate=cost(),
        name="finish_geglu",
    )(mine, *halves)


def finish_attend_kernel(mine_ref, x_ref, x_got_ref, y_ref, y_got_ref, heads_ref, merge_ref):
    def order(which, own, got):
        mine = mine_ref[which] != 0
        return jnp.where(mine, got, own), jnp.where(mine, own, got)

    q, k = order(0, x_ref[...], x_got_ref[...])
    v, merge = order(0, y_ref[...], y_got_ref[...])
    for which, part in enumerate((q, k, v)):
        heads_ref[which] = part.astype(F32).T
    merge_ref[...] = merge.astype(F32)


def finish_attend(mine, halves):
    count, d = halves[0].shape
    block = min(d, 512)
    part = pl.BlockSpec((count, block), lambda i: (0, i))
    return pl.pallas_call(
        finish_attend_kernel,
        grid=(d // block,),
        in_specs=[smem()] + [part] * 4,
        out_specs=[pl.BlockSpec((3, block, count), lambda i: (0, i, 0)), part],
        out_shape=[
            jax.ShapeDtypeStruct((3, d, count), F32),
            jax.ShapeDtypeStruct((count, d), F32),
        ],
        compiler_params=params(),
        cost_estimate=cost(),
        name="finish_attend",
    )(mine, *halves)


def swap(values, axis, size, bit):
    return lax.ppermute(values, axis, [(i, i ^ bit) for i in range(size)])


def after(values, *before):
    return lax.optimization_barrier((values, *before))[0]


def fetch_parts(values, dp, index):
    if dp < 4:
        return (values,)
    part = values.shape[1] // 4
    place = index & 3
    return tuple(
        lax.dynamic_slice_in_dim(values, which * part, part, 1) for which in (place, place ^ 3)
    )


def split_terms(values):
    high = lax.reduce_precision(values, 8, 7)
    mid = lax.reduce_precision(values - high, 8, 7)
    return [term.astype(BF16) for term in (high, mid, values - high - mid)]


def pack_row(values, width):
    rows = jnp.stack(split_terms(values))
    return jnp.pad(rows, ((0, 13), (0, width - values.shape[0])))


def unpack_row(block, count):
    return jnp.sum(block[:3, :count].astype(F32), 0)


def relay_parts(near, dp):
    return [] if dp < 4 else [swap(near, "dp", dp, 1), swap(near, "dp", dp, 2)]


def assemble_parts(near, others, dp, index):
    if dp < 4:
        return near
    pieces = [near, *others]
    low, high = (index & 1) != 0, (index & 2) != 0
    a, b = jnp.where(low, pieces[1], pieces[0]), jnp.where(low, pieces[0], pieces[1])
    c, d = jnp.where(low, pieces[3], pieces[2]), jnp.where(low, pieces[2], pieces[3])
    first, last = jnp.where(high, c, a), jnp.where(high, a, c)
    second, third = jnp.where(high, d, b), jnp.where(high, b, d)
    return jnp.concatenate([first, second, last, third], 1)


ORDER = "mMgGaAbBm21aAbBgG@3aAbB@4gGb!%BgC"


class Reduction:
    def __init__(self, x, order, size, index, short=False):
        self.x, self.size, self.index = x, size, index
        down = order[:-1] if short else order
        self.steps = [(bit, "half") for bit in down]
        self.steps += [(bit, "add") for bit in order[len(down) :]]
        self.steps += [(bit, "double") for bit in reversed(down)]
        self.flying = None

    def split(self, *before):
        bit, kind = self.steps[0]
        if kind != "half":
            if before:
                self.x = after(self.x, *before)
            return self.x
        mine = (self.index & bit) != 0
        half = self.x.shape[0] // 2
        low, high = self.x[:half], self.x[half:]
        self.x = jnp.where(mine, high, low)
        return jnp.where(mine, low, high)

    def start(self, *before):
        bit = self.steps[0][0]
        sent = self.split(*before)
        self.flying = swap(sent, "dp", self.size, bit)

    def start_piece(self, which, count, *before):
        bit = self.steps[0][0]
        part = self.x.shape[0] // count
        sent = after(self.x[which * part : (which + 1) * part], *before)
        self.flying = (self.flying if which else []) + [swap(sent, "dp", self.size, bit)]

    def end(self, *before):
        bit, kind = self.steps.pop(0)
        mine = (self.index & bit) != 0
        got = after(self.flying, *before) if before else self.flying
        if kind == "double":
            parts = jnp.where(mine, got, self.x), jnp.where(mine, self.x, got)
            self.x = jnp.concatenate(parts, 0)
        else:
            self.x = (self.x.astype(F32) + got.astype(F32)).astype(BF16)

    def halves(self, *before):
        got = self.flying if isinstance(self.flying, list) else [self.flying]
        return [self.x, *(after(part, *before) for part in got)]


class Pair:
    def __init__(self, first, second, bits, turned, size, index):
        self.parts = Reduction(first, bits, size, index), Reduction(second, turned, size, index)
        self.size, self.both = size, None

    @property
    def x(self):
        return tuple(part.x for part in self.parts)

    def start(self):
        one, two = self.parts
        bit = one.steps[0][0]
        if bit != two.steps[0][0]:
            one.start()
            two.start()
            return
        self.both = swap(jnp.stack([one.split(), two.split()]), "dp", self.size, bit)

    def end(self, *before):
        one, two = self.parts
        if self.both is not None:
            both = after(self.both, *before)
            one.flying, two.flying, self.both = both[0], both[1], None
            before = ()
        one.end(*before)
        two.end(*before)


class Gather:
    def __init__(self, x, steps):
        self.x, self.steps = x, steps

    def start(self):
        axis, size, bit = self.steps[0]
        self.flying = swap(self.x, axis, size, bit)

    def end(self, *before):
        self.steps.pop(0)
        self.x = jnp.concatenate([self.x, after(self.flying, *before)], 0)


def per_device(
    dp,
    mp,
    tokens,
    condition,
    buckets,
    heads_weight,
    merge_weight,
    expand_weight,
    reduce_weight,
    adapt_first,
    adapt_second,
    cosine_scale,
    cotangent,
):
    own_rows, width = tokens.shape
    local_images = buckets.shape[0]
    local = cosine_scale.shape[0] * HEAD_DIM
    units = reduce_weight.shape[0]
    index = lax.axis_index("dp")
    core = functools.partial(swap, axis="mp", size=mp, bit=1)
    chip = functools.partial(swap, axis="mp", size=mp, bit=2)

    heads_own = jnp.transpose(heads_weight, (1, 0, 2))
    heads_parts = fetch_parts(heads_own, dp, index)
    tokens, *heads_parts = lax.optimization_barrier((tokens, *heads_parts))

    scale_first = 1.0 + jnp.dot(condition, adapt_first, preferred_element_type=F32)
    scale_first = scale_first.reshape(local_images, 1, width)
    normed_own = norm_first(tokens, scale_first)
    heads_near = chip(heads_parts[0])
    merge_packed = jnp.concatenate(
        [after(merge_weight, normed_own), pack_row(cosine_scale, width)], 0
    )
    buckets_chip = jnp.concatenate([buckets, core(buckets)], 0)
    normed = jnp.concatenate([normed_own, core(normed_own)], 0)
    normed, heads_near, cotangent_late, merge_packed, *cross = lax.optimization_barrier(
        (normed, heads_near, cotangent, merge_packed, *heads_parts[1:])
    )
    cross = [chip(part) for part in cross]
    relayed = relay_parts(heads_near, dp)
    merge_other = chip(merge_packed)
    cot_core = core(cotangent_late)
    table = jnp.asarray(turn_table())
    own = attend_forward(buckets_chip, cosine_scale, table, normed, heads_own)

    expand_own = jnp.transpose(after(expand_weight, own[5]), (1, 0, 2))
    scale_second = 1.0 + jnp.dot(
        after(condition, own[5]), adapt_second, preferred_element_type=F32
    )
    scale_second = scale_second.reshape(local_images, 1, width)
    expand_own = lax.optimization_barrier((expand_own, scale_second))[0]
    cot_first = chip(after(cotangent_late[: own_rows // 2], expand_own))
    *pieces, merge_other = lax.optimization_barrier(
        (*relayed, *cross, merge_other, expand_own)
    )[:-1]
    heads_other = assemble_parts(heads_near, pieces, dp, index)
    scale_other = unpack_row(merge_other[local:], cosine_scale.shape[0])
    merge_other = merge_other[:local]
    heads_other, expand_own, scale_second, merge_other, scale_other = lax.optimization_barrier(
        (heads_other, expand_own, scale_second, merge_other, scale_other)
    )
    cot_last = chip(after(cotangent_late[own_rows // 2 :], heads_other))
    *other, keep, send = attend_forward(
        buckets_chip, scale_other, table, normed, heads_other, (own[5], merge_weight, merge_other)
    )
    send, cot_first, cot_last, cot_core = lax.optimization_barrier(
        (send, cot_first, cot_last, cot_core)
    )
    middle, second_own = norm_second(tokens, keep, core(send), scale_second)
    second_chip = chip(second_own)
    second_core = core(second_own)
    cot_chip = jnp.concatenate([after(cot_first, second_own), cot_last], 0)
    cot_far = core(cot_chip)

    o_keep, o_send, n_keep, n_send, grads = geglu(
        second_own, second_core, cotangent, cot_core, expand_own, reduce_weight
    )
    second_chip, cot_far, grads = lax.optimization_barrier((second_chip, cot_far, grads))
    second_far = core(second_chip)
    o_near, n_near = core(o_send), core(n_send)
    o_chip, o_far, n_chip, n_far, grads = geglu(
        second_chip, second_far, cot_chip, cot_far, expand_own, reduce_weight, grads
    )

    bits = [1 << b for b in range(dp.bit_length() - 1)]
    turned = bits[1:2] + bits[:1] + bits[2:]
    n_pair = (n_chip + core(n_far).astype(F32)).astype(BF16)
    n_pair, grads = lax.optimization_barrier((n_pair, grads))
    n_sum = chip(n_pair)
    cut = 3 * units // 2
    mlp = Pair(grads[:cut], grads[cut:], bits, turned, dp, index)
    mlp.start()
    middle_grad, adapt_second_grad, branch_own = norm_back(
        after(n_keep, *mlp.x), (n_near, n_sum), middle, cotangent, scale_second, True
    )
    branch_core = core(branch_own)
    o_pair = (o_chip + after(core(after(o_far, n_pair)), branch_own).astype(F32)).astype(BF16)
    o_sum = chip(o_pair)
    mlp.end(branch_own)
    mlp.start()
    branch = lax.optimization_barrier((branch_own, branch_core, o_pair, *mlp.x))[:2]

    far_a, far_b, turn_far, triple_far = attend_backward(
        buckets_chip, scale_other, table, normed, merge_other, branch, other
    )
    got_a, got_b = chip(far_a), chip(far_b)
    o_sum = after(o_sum, far_a)
    mlp.end(far_a, o_sum)
    mlp.start()
    branch = lax.optimization_barrier((*branch, *mlp.x))[:2]
    near_a, near_b, turn_own, keep, send = attend_backward(
        buckets_chip,
        cosine_scale,
        table,
        normed,
        merge_weight,
        branch,
        own,
        (heads_own, heads_other, triple_far),
    )
    near_a, near_b, send, got_a, mlp.both = lax.optimization_barrier(
        (near_a, near_b, send, got_a, mlp.both)
    )
    attend_a = Reduction(
        (near_a.astype(F32) + got_a.astype(F32)).astype(BF16), bits, dp, index, True
    )
    attend_a.start()
    mlp.end(attend_a.x)
    mlp.start()
    tokens_grad, adapt_first_grad = norm_back(
        after(keep, *mlp.x), (core(send),), tokens, middle_grad, scale_first, False
    )
    n = local_images
    first_low = adapt_first_grad.reshape(n, width).astype(BF16)
    second_low = adapt_second_grad.reshape(n, width).astype(BF16)
    turn = split_terms(jnp.concatenate([turn_own, turn_far], 1))
    payload = jnp.concatenate(
        [
            first_low,
            second_low,
            jnp.pad(condition, ((0, 0), (0, width - condition.shape[1]))),
            jnp.concatenate([turn[0], turn[1]], 1),
            jnp.concatenate([turn[2], jnp.zeros_like(turn[2])], 1),
        ],
        0,
    )[None]
    adapters = Gather(
        payload, [("dp", dp, bit) for bit in bits] + [("mp", mp, bit) for bit in (1, 2)]
    )
    adapters.start()
    attend_a.end(tokens_grad)
    attend_a.start()
    attend_b = Reduction(
        (near_b.astype(F32) + after(got_b, attend_a.x).astype(F32)).astype(BF16),
        bits,
        dp,
        index,
        True,
    )
    attend_b.start()
    adapters.end(attend_b.x)
    adapters.start()
    middle, first_late = lax.optimization_barrier((middle, first_low, attend_b.x))[:2]
    layer_out = middle + (o_keep + o_near.astype(F32) + o_sum.astype(F32))
    condition_grad = nt(first_late, adapt_first) + nt(second_low, adapt_second)
    last = [adapters.x, layer_out, condition_grad]

    def end(one):
        one.end(*last)
        last.clear()
        last.extend(one.x if isinstance(one.x, tuple) else [one.x])

    def land(one):
        if isinstance(one.flying, list):
            one.flying[-1] = after(one.flying[-1], *last)
            last[:] = one.flying[-1:]
        else:
            one.flying = after(one.flying, *last)
            last[:] = [one.flying]

    def products():
        everyone = adapters.x
        first_all = everyone[:, :n].reshape(-1, width)
        second_all = everyone[:, n : 2 * n].reshape(-1, width)
        condition_all = everyone[:, 2 * n : 3 * n, : condition.shape[1]]
        condition_all = condition_all.reshape(-1, condition.shape[1])
        first_total = tn(condition_all, first_all)
        second_total = tn(condition_all, second_all)
        turns = everyone[:, 3 * n :].astype(F32)
        turns = turns[:, 0, : 2 * local] + turns[:, 0, 2 * local : 4 * local] + turns[:, 1, : 2 * local]
        turn_total = jnp.sum(turns[:dp, :local], 0) + jnp.sum(turns[2 * dp : 3 * dp, local:], 0)
        scale_total = turn_total[::HEAD_DIM] / (2.0 * cosine_scale)
        return first_total, second_total, scale_total

    names = {"a": attend_a, "b": attend_b, "m": mlp, "g": adapters}
    for name in ORDER if dp == 8 else "":
        if name == "C":
            first_total, second_total, scale_total = products()
            last[:] = [first_total, second_total]
            continue
        if name in "!@%":
            land({"!": mlp.parts[0], "@": mlp.parts[1], "%": attend_a}[name])
        elif name == "1":
            mlp.parts[0].start(*last)
        elif name in "234":
            mlp.parts[1].start_piece(int(name) - 2, 3, *last)
        elif name.islower():
            end(names[name])
        else:
            names[name.lower()].start()
    if dp != 8:
        for one in (mlp, attend_a, attend_b):
            part = one.parts[0] if one is mlp else one
            while len(part.steps) > 1:
                end(one)
                one.start()
        while adapters.steps:
            end(adapters)
            if adapters.steps:
                adapters.start()
        first_total, second_total, scale_total = products()
    if dp == 8 and "C" not in ORDER:
        first_total, second_total, scale_total = products()
    mine = jnp.stack([index & 1, (index >> 1) & 1])
    reduce_total, expand_total = finish_geglu(
        mine, [half for part in mlp.parts for half in part.halves(*last)], units
    )
    heads_total, merge_total = finish_attend(
        mine,
        [half for part in (attend_a, attend_b) for half in part.halves(reduce_total)],
    )
    heads_total = jnp.transpose(heads_total, (1, 0, 2))
    return (
        layer_out,
        tokens_grad,
        condition_grad,
        heads_total,
        merge_total,
        expand_total,
        reduce_total,
        first_total,
        second_total,
        scale_total,
    )


def solution(mesh):
    split = P(("dp", "mp"), None)
    return jax.shard_map(
        functools.partial(per_device, mesh.shape["dp"], mesh.shape["mp"]),
        mesh=mesh,
        in_specs=(
            split,
            split,
            P(("dp", "mp")),
            P(None, None, "mp"),
            P("mp", None),
            P(None, None, "mp"),
            P("mp", None),
            P(),
            P(),
            P("mp"),
            split,
        ),
        out_specs=(
            split,
            split,
            split,
            P(None, None, "mp"),
            P("mp", None),
            P(None, None, "mp"),
            P("mp", None),
            P(),
            P(),
            P("mp"),
        ),
        check_vma=False,
    )
```

```python
import functools

import jax
import jax.numpy as jnp
import numpy as np
from jax import lax
from jax.experimental import pallas as pl
from jax.experimental.pallas import tpu as pltpu
from jax.sharding import PartitionSpec as P

HEAD_DIM = 64
BUCKET = 256
EPS = 1e-06
NEG = -1e30
GRID_ROWS = np.array([16, 12, 21, 14, 18, 12, 16, 10, 20, 8, 24, 11, 22, 8, 32, 13], np.int32)
GRID_COLS = np.array([16, 21, 12, 18, 14, 16, 12, 20, 10, 24, 8, 22, 11, 32, 8, 13], np.int32)
F32 = jnp.float32
BF16 = jnp.bfloat16
VMEM_LIMIT = 56 * 1024 * 1024
GELU_A = float(np.sqrt(2.0 / np.pi))
GELU_B = 0.044715
CHUNK = 256


def nn(a, b):
    return lax.dot_general(a, b, (((1,), (0,)), ((), ())), preferred_element_type=F32)


def nt(a, b):
    return lax.dot_general(a, b, (((1,), (1,)), ((), ())), preferred_element_type=F32)


def tn(a, b):
    return lax.dot_general(a, b, (((0,), (0,)), ((), ())), preferred_element_type=F32)


def params():
    return pltpu.CompilerParams(vmem_limit_bytes=VMEM_LIMIT, dimension_semantics=("arbitrary",))


def cost(us=17):
    return pl.CostEstimate(flops=us * 1_176_000_000, bytes_accessed=us * 1_764_000, transcendentals=0)


def whole(shape):
    return pl.BlockSpec(shape, lambda i: (0,) * len(shape))


def rows(block, width):
    return pl.BlockSpec((block, width), lambda i: (i, 0))


def norm_first_kernel(x_ref, s_ref, out_ref):
    x = x_ref[...].astype(F32)
    r = lax.rsqrt(jnp.mean(x * x, -1, keepdims=True) + EPS)
    out_ref[...] = (x * r * s_ref[0]).astype(BF16)


def norm_first(tokens, scale):
    n, d = tokens.shape
    return pl.pallas_call(
        norm_first_kernel,
        grid=(n // BUCKET,),
        in_specs=[rows(BUCKET, d), pl.BlockSpec((1, 1, d), lambda i: (i, 0, 0))],
        out_specs=rows(BUCKET, d),
        out_shape=jax.ShapeDtypeStruct((n, d), BF16),
        compiler_params=params(),
        cost_estimate=cost(3),
        name="norm_first",
    )(tokens, scale)


def norm_second_kernel(x_ref, part_ref, recv_ref, s_ref, mid_ref, out_ref):
    x = x_ref[...].astype(F32) + (part_ref[...] + recv_ref[...].astype(F32))
    mid_ref[...] = x
    r = lax.rsqrt(jnp.mean(x * x, -1, keepdims=True) + EPS)
    out_ref[...] = (x * r * s_ref[0]).astype(BF16)


def norm_second(tokens, part, recv, scale):
    n, d = tokens.shape
    return pl.pallas_call(
        norm_second_kernel,
        grid=(n // BUCKET,),
        in_specs=[rows(BUCKET, d)] * 3 + [pl.BlockSpec((1, 1, d), lambda i: (i, 0, 0))],
        out_specs=[rows(BUCKET, d)] * 2,
        out_shape=[jax.ShapeDtypeStruct((n, d), F32), jax.ShapeDtypeStruct((n, d), BF16)],
        compiler_params=params(),
        cost_estimate=cost(4),
        name="norm_second",
    )(tokens, part, recv, scale)


def norm_back_kernel(extra, low, *refs):
    part_ref = refs[0]
    more = refs[1 : 1 + extra]
    x_ref, g_ref, s_ref = refs[1 + extra : 4 + extra]
    outs = refs[4 + extra :]
    grad = part_ref[...]
    for ref in more:
        grad = grad + ref[...].astype(F32)
    x = x_ref[...].astype(F32)
    r = lax.rsqrt(jnp.mean(x * x, -1, keepdims=True) + EPS)
    u = grad * s_ref[0]
    back = g_ref[...].astype(F32) + r * u - x * (r * r * r * jnp.mean(u * x, -1, keepdims=True))
    outs[0][...] = back
    outs[1][0] = jnp.sum(grad * x * r, 0, keepdims=True)
    if low:
        outs[2][...] = back.astype(BF16)


def norm_back(part, more, x, g, scale, low):
    n, d = x.shape
    per_image = pl.BlockSpec((1, 1, d), lambda i: (i, 0, 0))
    outs = [jax.ShapeDtypeStruct((n, d), F32), jax.ShapeDtypeStruct((n // BUCKET, 1, d), F32)]
    specs = [rows(BUCKET, d), per_image]
    if low:
        outs.append(jax.ShapeDtypeStruct((n, d), BF16))
        specs.append(rows(BUCKET, d))
    return pl.pallas_call(
        functools.partial(norm_back_kernel, len(more), low),
        grid=(n // BUCKET,),
        in_specs=[rows(BUCKET, d)] * (3 + len(more)) + [per_image],
        out_specs=specs,
        out_shape=outs,
        compiler_params=params(),
        cost_estimate=cost(5),
        name="norm_back",
    )(part, *more, x, g, scale)


def head_sums(values, block_ones):
    high = values.astype(BF16)
    low = (values - high.astype(F32)).astype(BF16)
    return nn(high, block_ones) + nn(low, block_ones)


def partner(values):
    parts = []
    for start in range(0, values.shape[1], 128):
        part = values[:, start : start + 128]
        lane = lax.broadcasted_iota(jnp.int32, part.shape, 1) % HEAD_DIM
        parts.append(
            jnp.where(lane < HEAD_DIM // 4, pltpu.roll(part, 128 - 16, 1), pltpu.roll(part, 16, 1))
        )
    return jnp.concatenate(parts, 1)


def head_mask(shape, head):
    lane = lax.broadcasted_iota(jnp.int32, shape, 1)
    return (lane >= head * HEAD_DIM) & (lane < (head + 1) * HEAD_DIM)


def by_head(scale_ref, heads):
    row = jnp.zeros((1, heads * HEAD_DIM), F32)
    for head in range(heads):
        row = jnp.where(head_mask(row.shape, head), scale_ref[head], row)
    return row


def block_of_ones(width):
    a = lax.broadcasted_iota(jnp.int32, (width, width), 0) // HEAD_DIM
    b = lax.broadcasted_iota(jnp.int32, (width, width), 1) // HEAD_DIM
    return jnp.where(a == b, 1.0, 0.0).astype(BF16)


PLACES = 32


def turn_table():
    lane = np.arange(128) % HEAD_DIM
    quarter = HEAD_DIM // 8
    freqs = 10000.0 ** (-np.arange(quarter) / quarter)
    angles = np.arange(PLACES)[:, None] * freqs[lane % quarter][None, :]
    turns = lane < HEAD_DIM // 2
    by_row = (lane // quarter) % 2 == 0
    sign = np.where(lane < HEAD_DIM // 4, -1.0, 1.0)
    cosines = np.where(turns, np.cos(angles), 1.0)
    sines = np.where(turns, np.sin(angles) * sign, 0.0)
    both = np.concatenate([cosines, sines], 1)
    by_row = np.concatenate([by_row, by_row])
    table = np.concatenate([np.where(by_row, both, 0.0), np.where(by_row, 0.0, both)], 0)
    table = table.astype(np.float32)
    high = table.astype(jnp.bfloat16)
    rest = table - high.astype(np.float32)
    mid = rest.astype(jnp.bfloat16)
    low = (rest - mid.astype(np.float32)).astype(jnp.bfloat16)
    return np.stack([high, mid, low])


def turns_of(grid_rows, grid_cols, table_ref, width):
    place = lax.broadcasted_iota(jnp.int32, (BUCKET, 2 * PLACES), 0).astype(F32)
    lane = lax.broadcasted_iota(jnp.int32, (BUCKET, 2 * PLACES), 1).astype(F32)
    cols = jnp.full((1, 1), grid_cols, jnp.int32).astype(F32)
    row = jnp.floor((place + 0.5) / cols)
    col = place - row * cols
    hot = (lane == row) | (lane - PLACES == col)
    hot = jnp.where(hot, 1.0, 0.0).astype(BF16)
    both = nn(hot, table_ref[0]) + nn(hot, table_ref[1]) + nn(hot, table_ref[2])
    cosines, sines = both[:, :128], both[:, 128:]
    copies = width // 128
    return jnp.concatenate([cosines] * copies, 1), jnp.concatenate([sines] * copies, 1)


def grid_of(bucket_ref, dims_ref, image):
    bucket = bucket_ref[image]
    return dims_ref[0, bucket], dims_ref[1, bucket]


def smem():
    return pl.BlockSpec(memory_space=pltpu.SMEM)


def attend_forward_kernel(
    merge, heads, step, bucket_ref, dims_ref, scale_ref, table_ref, n_ref, w_ref, *refs
):
    if merge:
        other_ref, m_own_ref, m_ref = refs[:3]
        refs = refs[3:]
    q_ref, k_ref, v_ref, cq_ref, ck_ref, mixed_ref = refs[:6]
    width = heads * HEAD_DIM
    ones = block_of_ones(width)
    root = jnp.sqrt(by_head(scale_ref, heads))
    first = pl.program_id(0) * step
    normed = n_ref[...]

    raw = [nn(normed, w_ref[which]) for which in range(3)]
    v_ref[...] = raw[2].astype(BF16)
    tables = []
    for image in range(step):
        grid_rows, grid_cols = grid_of(bucket_ref, dims_ref, first + image)
        tables.append((*turns_of(grid_rows, grid_cols, table_ref, width), grid_rows * grid_cols))
    cosines = jnp.concatenate([t[0] for t in tables], 0)
    sines = jnp.concatenate([t[1] for t in tables], 0)
    for which, (out_ref, c_ref) in enumerate(((q_ref, cq_ref), (k_ref, ck_ref))):
        c = lax.rsqrt(head_sums(raw[which] * raw[which], ones) + EPS) * root
        c_ref[...] = c.astype(BF16)
        n = raw[which] * c
        out_ref[...] = (n * cosines + partner(n) * sines).astype(BF16)
    for image in range(step):
        at = pl.ds(image * BUCKET, BUCKET)
        q, k, v = q_ref[at, :], k_ref[at, :], v_ref[at, :]
        key = lax.broadcasted_iota(jnp.int32, (1, BUCKET), 1)
        bias = jnp.where(key < tables[image][2], 0.0, NEG)
        zero = jnp.zeros_like(q)
        probs, values = [], []
        for head in range(heads):
            mask = head_mask((BUCKET, width), head)
            e = jnp.exp(nt(jnp.where(mask, q, zero), k) + bias)
            probs.append((e * (1.0 / jnp.sum(e, -1, keepdims=True))).astype(BF16))
            values.append(jnp.where(mask, v, zero))
        mixed = nn(jnp.concatenate(probs, 1), jnp.concatenate(values, 0)).astype(BF16)
        mixed_ref[at, :] = mixed
    if merge:
        keep_ref, send_ref = refs[6:]
        part = nn(other_ref[...], m_own_ref[...]) + nn(mixed_ref[...], m_ref[...])
        half = pl.num_programs(0) // 2

        @pl.when(pl.program_id(0) < half)
        def _():
            keep_ref[...] = part

        @pl.when(pl.program_id(0) >= half)
        def _():
            send_ref[...] = part.astype(BF16)


def attend_forward(buckets, scale, table, normed, weight, merge=None, step=2):
    n, d = normed.shape
    width = weight.shape[2]
    images = n // BUCKET
    heads = width // HEAD_DIM
    count = images // step
    half = count // 2
    tile = step * BUCKET
    block = rows(tile, width)
    dims = jnp.asarray(np.stack([GRID_ROWS, GRID_COLS]))
    in_specs = [smem()] * 3 + [whole(table.shape), rows(tile, d), whole(weight.shape)]
    operands = [buckets, dims, scale, table, normed, weight]
    out_specs = [block] * 6
    outs = [jax.ShapeDtypeStruct((n, width), t) for t in (BF16,) * 6]
    if merge is not None:
        other, own_weight, merge_weight = merge
        in_specs += [block, whole(own_weight.shape), whole(merge_weight.shape)]
        operands += [other, own_weight, merge_weight]
        out_specs += [
            pl.BlockSpec((tile, d), lambda i: (jnp.minimum(i, half - 1), 0)),
            pl.BlockSpec((tile, d), lambda i: (jnp.maximum(i - half, 0), 0)),
        ]
        outs += [
            jax.ShapeDtypeStruct((n // 2, d), F32),
            jax.ShapeDtypeStruct((n // 2, d), BF16),
        ]
    return pl.pallas_call(
        functools.partial(attend_forward_kernel, merge is not None, heads, step),
        grid=(count,),
        in_specs=in_specs,
        out_specs=out_specs,
        out_shape=outs,
        compiler_params=params(),
        cost_estimate=cost(),
        name="attend_forward",
    )(*operands)


def attend_backward_kernel(
    second,
    heads,
    bucket_ref,
    dims_ref,
    scale_ref,
    table_ref,
    n_ref,
    m_ref,
    b_own_ref,
    b_core_ref,
    q_ref,
    k_ref,
    v_ref,
    cq_ref,
    ck_ref,
    mixed_ref,
    *refs,
):
    if second:
        w_ref, w_far_ref, far_ref = refs[:3]
        grad_ref, rest_ref, turn_ref, keep_ref, send_ref, tg_ref, all_ref, macc_ref = refs[3:]
    else:
        grad_ref, rest_ref, turn_ref, out_ref, tg_ref, all_ref, macc_ref = refs
    i = pl.program_id(0)
    images = pl.num_programs(0) - 1
    width = heads * HEAD_DIM

    @pl.when(i < images)
    def _():
        grid_rows, grid_cols = grid_of(bucket_ref, dims_ref, i)
        cosines, sines = turns_of(grid_rows, grid_cols, table_ref, width)
        ones = block_of_ones(width)
        inv = 1.0 / by_head(scale_ref, heads)
        key = lax.broadcasted_iota(jnp.int32, (BUCKET, 1), 0)
        bias = jnp.where(key < grid_rows * grid_cols, 0.0, NEG)
        branch = jnp.where(i < images // 2, b_own_ref[...], b_core_ref[...])
        q, k, v = q_ref[...], k_ref[...], v_ref[...]
        mixed = mixed_ref[...]
        dmix = nt(branch, m_ref[...]).astype(BF16)
        prod = (dmix.astype(F32) * mixed.astype(F32)).astype(BF16)
        lane_head = lax.broadcasted_iota(jnp.int32, (16, width), 1) // HEAD_DIM
        picks = lax.broadcasted_iota(jnp.int32, (16, width), 0) == lane_head
        deltas = nt(jnp.where(picks, 1.0, 0.0).astype(BF16), prod)
        zero = jnp.zeros_like(q)
        masks = [head_mask((BUCKET, width), head) for head in range(heads)]
        qs = [jnp.where(mask, q, zero) for mask in masks]
        ks = [jnp.where(mask, k, zero) for mask in masks]
        dhs = [jnp.where(mask, dmix, zero) for mask in masks]
        probs_all, ds_all = [], []
        for head in range(heads):
            e = jnp.exp(nt(k, qs[head]) + bias)
            probs = e * (1.0 / jnp.sum(e, 0, keepdims=True))
            dprobs = nt(v, dhs[head])
            probs_all.append(probs.astype(BF16))
            ds_all.append((probs * (dprobs - deltas[head : head + 1, :])).astype(BF16))
        dv = nn(jnp.concatenate(probs_all, 1), jnp.concatenate(dhs, 0))
        dk = nn(jnp.concatenate(ds_all, 1), jnp.concatenate(qs, 0))
        dq = tn(jnp.concatenate(ds_all, 0), jnp.concatenate(ks, 0))

        def back(low, grad, c):
            full = low.astype(F32)
            sums = head_sums(full * grad, ones)
            t = grad - full * (sums * inv)
            out = (c * (t * cosines - partner(t) * sines)).astype(BF16)
            return out, jnp.sum(sums, 0, keepdims=True)

        gq, sq = back(q, dq, cq_ref[...].astype(F32))
        gk, sk = back(k, dk, ck_ref[...].astype(F32))
        gv = dv.astype(BF16)
        at = pl.ds(pl.multiple_of(i * BUCKET, BUCKET), BUCKET)
        tg_ref[at, :width] = gq
        tg_ref[at, width : 2 * width] = gk
        tg_ref[at, 2 * width :] = gv
        all_ref[at, :] = n_ref[...]
        mg = tn(mixed, branch)

        @pl.when(i == 0)
        def _():
            turn_ref[...] = sq + sk
            macc_ref[...] = mg

        @pl.when(i > 0)
        def _():
            turn_ref[...] += sq + sk
            macc_ref[...] += mg

        if not second:
            out_ref[:, :width] = gq
            out_ref[:, width : 2 * width] = gk
            out_ref[:, 2 * width :] = gv
        else:
            part = nt(gq, w_ref[0]) + nt(gk, w_ref[1]) + nt(gv, w_ref[2])
            for which in range(3):
                part = part + nt(far_ref[:, which * width : (which + 1) * width], w_far_ref[which])

            @pl.when(i < images // 2)
            def _():
                keep_ref[...] = part

            @pl.when(i >= images // 2)
            def _():
                send_ref[...] = part.astype(BF16)

    @pl.when(i == images)
    def _():
        grad_ref[...] = tn(tg_ref[:, : 2 * width], all_ref[...]).astype(BF16)
        rest_ref[:width, :] = tn(tg_ref[:, 2 * width :], all_ref[...]).astype(BF16)
        rest_ref[width:, :] = macc_ref[...].astype(BF16)


def attend_backward(buckets, scale, table, normed, merge_weight, branch, saved, weights=None):
    n, d = normed.shape
    width = merge_weight.shape[0]
    images = n // BUCKET
    heads = width // HEAD_DIM
    half = images // 2

    def clip(i, low, high):
        return jnp.minimum(jnp.maximum(i - low, 0), high)

    image = pl.BlockSpec((BUCKET, width), lambda i: (clip(i, 0, images - 1), 0))
    triple = pl.BlockSpec((BUCKET, 3 * width), lambda i: (clip(i, 0, images - 1), 0))
    wide = pl.BlockSpec((BUCKET, d), lambda i: (clip(i, 0, images - 1), 0))
    keep_spec = pl.BlockSpec((BUCKET, d), lambda i: (clip(i, 0, half - 1), 0))
    send_spec = pl.BlockSpec((BUCKET, d), lambda i: (clip(i, half, half - 1), 0))
    dims = jnp.asarray(np.stack([GRID_ROWS, GRID_COLS]))
    in_specs = [smem()] * 3 + [
        whole(table.shape),
        wide,
        whole(merge_weight.shape),
        keep_spec,
        send_spec,
    ] + [image] * 6
    operands = [buckets, dims, scale, table, normed, merge_weight, *branch, *saved]
    out_specs = [whole((2 * width, d))] * 2 + [whole((1, width))]
    outs = [jax.ShapeDtypeStruct((2 * width, d), BF16)] * 2 + [jax.ShapeDtypeStruct((1, width), F32)]
    if weights is not None:
        in_specs += [whole(weights[0].shape)] * 2 + [triple]
        operands += list(weights)
        out_specs += [keep_spec, send_spec]
        outs += [jax.ShapeDtypeStruct((n // 2, d), F32), jax.ShapeDtypeStruct((n // 2, d), BF16)]
    else:
        out_specs.append(triple)
        outs.append(jax.ShapeDtypeStruct((n, 3 * width), BF16))
    return pl.pallas_call(
        functools.partial(attend_backward_kernel, weights is not None, heads),
        grid=(images + 1,),
        in_specs=in_specs,
        out_specs=out_specs,
        out_shape=outs,
        scratch_shapes=[
            pltpu.VMEM((n, 3 * width), BF16),
            pltpu.VMEM((n, d), BF16),
            pltpu.VMEM((width, d), F32),
        ],
        compiler_params=params(),
        cost_estimate=cost(),
        name="attend_backward",
    )(*operands)


def geglu_kernel(second, tile, na_ref, nb_ref, ga_ref, gb_ref, e_ref, r_ref, *refs):
    if second:
        prev_ref = refs[0]
        refs = refs[1:]
    o_keep_ref, o_send_ref, n_keep_ref, n_send_ref, grad_ref = refs[:5]
    n_all, g_all, e_all, r_all, act, o_keep, o_send, n_keep, n_send, grad = refs[5:15]
    sems = refs[-1]
    half = na_ref.shape[0]
    units = r_ref.shape[0]
    count = [0]

    def copy(source, target):
        made = pltpu.make_async_copy(source, target, sems.at[count[0]])
        count[0] += 1
        made.start()
        return made

    waits = {}
    starts = range(0, units, CHUNK)
    waits["na"] = copy(na_ref, n_all.at[:half])
    for u in starts:
        waits["e", u] = copy(e_ref.at[:, :, u : u + CHUNK], e_all.at[:, :, u : u + CHUNK])
    waits["ga"] = copy(ga_ref, g_all.at[:half])
    waits["r"] = copy(r_ref, r_all)
    waits["nb"] = copy(nb_ref, n_all.at[half:])
    waits["gb"] = copy(gb_ref, g_all.at[half:])
    if second:
        waits["prev"] = copy(prev_ref, refs[15])

    def ready(*keys):
        for key in keys:
            if key in waits:
                waits.pop(key).wait()

    outs = []
    for t in range(0, 2 * half, tile):
        first = t < half
        ready("na" if first else "nb")
        at = slice(t, t + tile)
        normed = n_all[at, :]
        for u in starts:
            here = slice(u, u + CHUNK)
            ready(("e", u))
            gate = nn(normed, e_all[0, :, here])
            up = nn(normed, e_all[1, :, here])
            ready("ga" if first else "gb", "r")
            hgrad = nt(g_all[at, :], r_all[here, :])
            square = gate * gate
            th = jnp.tanh(gate * (GELU_A + (GELU_A * GELU_B) * square))
            slant = 0.5 * (1.0 + th)
            gelu = gate * slant
            bend = (0.5 * GELU_A) + (1.5 * GELU_A * GELU_B) * square
            slope = slant + gate * (1.0 - th * th) * bend
            act[0, at, here] = (gelu * up).astype(BF16)
            act[1, at, here] = (hgrad * up * slope).astype(BF16)
            act[2, at, here] = (hgrad * gelu).astype(BF16)
        o_part = nn(act[0, at, :], r_all[...])
        n_part = nt(act[1, at, :], e_all[0]) + nt(act[2, at, :], e_all[1])
        local = slice(t % half, t % half + tile)
        if first:
            n_keep[local, :] = n_part
            o_keep[local, :] = o_part
        else:
            n_send[local, :] = n_part.astype(BF16)
            o_send[local, :] = o_part.astype(BF16)
        for source, target in (
            (n_keep, n_keep_ref) if first else (n_send, n_send_ref),
            (o_keep, o_keep_ref) if first else (o_send, o_send_ref),
        ):
            outs.append(copy(source.at[local, :], target.at[local, :]))
    ready("prev")
    for which in range(3):
        total = tn(act[which], (g_all if which == 0 else n_all)[...])
        here = slice(which * units, (which + 1) * units)
        if second:
            total = total + refs[15][here, :].astype(F32)
        grad[here, :] = total.astype(BF16)
        outs.append(copy(grad.at[here, :], grad_ref.at[here, :]))
    for out in outs:
        out.wait()


def geglu(normed_a, normed_b, grad_a, grad_b, expand, reduce, prev=None):
    half, d = normed_a.shape
    units = reduce.shape[0]
    tile = min(half, 256)
    operands = [normed_a, normed_b, grad_a, grad_b, expand, reduce]
    if prev is not None:
        operands.append(prev)
    anywhere = pl.BlockSpec(memory_space=pl.ANY)
    copies = 6 + units // CHUNK + 4 * half // tile + 3
    scratch = [
        pltpu.VMEM((2 * half, d), BF16),
        pltpu.VMEM((2 * half, d), BF16),
        pltpu.VMEM(expand.shape, BF16),
        pltpu.VMEM(reduce.shape, BF16),
        pltpu.VMEM((3, 2 * half, units), BF16),
        pltpu.VMEM((half, d), F32),
        pltpu.VMEM((half, d), BF16),
        pltpu.VMEM((half, d), F32),
        pltpu.VMEM((half, d), BF16),
        pltpu.VMEM((3 * units, d), BF16),
    ]
    if prev is not None:
        scratch.append(pltpu.VMEM((3 * units, d), BF16))
    scratch.append(pltpu.SemaphoreType.DMA((copies,)))
    return pl.pallas_call(
        functools.partial(geglu_kernel, prev is not None, tile),
        in_specs=[anywhere] * len(operands),
        out_specs=[anywhere] * 5,
        out_shape=[
            jax.ShapeDtypeStruct((half, d), F32),
            jax.ShapeDtypeStruct((half, d), BF16),
            jax.ShapeDtypeStruct((half, d), F32),
            jax.ShapeDtypeStruct((half, d), BF16),
            jax.ShapeDtypeStruct((3 * units, d), BF16),
        ],
        scratch_shapes=scratch,
        compiler_params=pltpu.CompilerParams(vmem_limit_bytes=VMEM_LIMIT),
        cost_estimate=cost(21),
        name="geglu",
    )(*operands)


def finish_geglu_kernel(mine_ref, x_ref, x_got_ref, y_ref, *refs):
    *y_got_refs, reduce_ref, expand_ref = refs
    def order(which, own, got):
        mine = mine_ref[which] != 0
        return jnp.where(mine, got, own), jnp.where(mine, own, got)

    y_got = jnp.concatenate([ref[...] for ref in y_got_refs], 0)
    parts = [*order(0, x_ref[...], x_got_ref[...]), *order(1, y_ref[...], y_got)]
    units = reduce_ref.shape[0]
    rows = jnp.concatenate(parts, 0).astype(F32)
    reduce_ref[...] = rows[:units]
    expand_ref[:, 0, :] = rows[units : 2 * units].T
    expand_ref[:, 1, :] = rows[2 * units :].T


def finish_geglu(mine, halves, units):
    d = halves[0].shape[1]
    block = min(d, 512)
    return pl.pallas_call(
        finish_geglu_kernel,
        grid=(d // block,),
        in_specs=[smem()]
        + [pl.BlockSpec((half.shape[0], block), lambda i: (0, i)) for half in halves],
        out_specs=[
            pl.BlockSpec((units, block), lambda i: (0, i)),
            pl.BlockSpec((block, 2, units), lambda i: (i, 0, 0)),
        ],
        out_shape=[
            jax.ShapeDtypeStruct((units, d), F32),
            jax.ShapeDtypeStruct((d, 2, units), F32),
        ],
        compiler_params=params(),
        cost_estimate=cost(7),
        name="finish_geglu",
    )(mine, *halves)


def finish_attend_kernel(mine_ref, x_ref, x_got_ref, y_ref, y_got_ref, heads_ref, merge_ref):
    def order(which, own, got):
        mine = mine_ref[which] != 0
        return jnp.where(mine, got, own), jnp.where(mine, own, got)

    q, k = order(0, x_ref[...], x_got_ref[...])
    v, merge = order(0, y_ref[...], y_got_ref[...])
    for which, part in enumerate((q, k, v)):
        heads_ref[which] = part.astype(F32).T
    merge_ref[...] = merge.astype(F32)


def finish_attend(mine, halves):
    count, d = halves[0].shape
    block = min(d, 512)
    part = pl.BlockSpec((count, block), lambda i: (0, i))
    return pl.pallas_call(
        finish_attend_kernel,
        grid=(d // block,),
        in_specs=[smem()] + [part] * 4,
        out_specs=[pl.BlockSpec((3, block, count), lambda i: (0, i, 0)), part],
        out_shape=[
            jax.ShapeDtypeStruct((3, d, count), F32),
            jax.ShapeDtypeStruct((count, d), F32),
        ],
        compiler_params=params(),
        cost_estimate=cost(4),
        name="finish_attend",
    )(mine, *halves)


def swap(values, axis, size, bit):
    return lax.ppermute(values, axis, [(i, i ^ bit) for i in range(size)])


def after(values, *before):
    return lax.optimization_barrier((values, *before))[0]


def fetch_parts(values, dp, index):
    if dp < 4:
        return (values,)
    part = values.shape[1] // 4
    place = index & 3
    return tuple(
        lax.dynamic_slice_in_dim(values, which * part, part, 1) for which in (place, place ^ 3)
    )


def split_terms(values):
    high = lax.reduce_precision(values, 8, 7)
    mid = lax.reduce_precision(values - high, 8, 7)
    return [term.astype(BF16) for term in (high, mid, values - high - mid)]


def pack_row(values, width):
    rows = jnp.stack(split_terms(values))
    return jnp.pad(rows, ((0, 13), (0, width - values.shape[0])))


def unpack_row(block, count):
    return jnp.sum(block[:3, :count].astype(F32), 0)


def relay_parts(near, dp):
    return [] if dp < 4 else [swap(near, "dp", dp, 1), swap(near, "dp", dp, 2)]


def assemble_parts(near, others, dp, index):
    if dp < 4:
        return near
    pieces = [near, *others]
    low, high = (index & 1) != 0, (index & 2) != 0
    a, b = jnp.where(low, pieces[1], pieces[0]), jnp.where(low, pieces[0], pieces[1])
    c, d = jnp.where(low, pieces[3], pieces[2]), jnp.where(low, pieces[2], pieces[3])
    first, last = jnp.where(high, c, a), jnp.where(high, a, c)
    second, third = jnp.where(high, d, b), jnp.where(high, b, d)
    return jnp.concatenate([first, second, last, third], 1)


ORDER = "mMgGaAbBm21aAbBgG@3aAbB@4gGb!%BgC"


class Reduction:
    def __init__(self, x, order, size, index, short=False):
        self.x, self.size, self.index = x, size, index
        down = order[:-1] if short else order
        self.steps = [(bit, "half") for bit in down]
        self.steps += [(bit, "add") for bit in order[len(down) :]]
        self.steps += [(bit, "double") for bit in reversed(down)]
        self.flying = None

    def split(self, *before):
        bit, kind = self.steps[0]
        if kind != "half":
            if before:
                self.x = after(self.x, *before)
            return self.x
        mine = (self.index & bit) != 0
        half = self.x.shape[0] // 2
        low, high = self.x[:half], self.x[half:]
        self.x = jnp.where(mine, high, low)
        return jnp.where(mine, low, high)

    def start(self, *before):
        bit = self.steps[0][0]
        sent = self.split(*before)
        self.flying = swap(sent, "dp", self.size, bit)

    def start_piece(self, which, count, *before):
        bit = self.steps[0][0]
        part = self.x.shape[0] // count
        sent = after(self.x[which * part : (which + 1) * part], *before)
        self.flying = (self.flying if which else []) + [swap(sent, "dp", self.size, bit)]

    def end(self, *before):
        bit, kind = self.steps.pop(0)
        mine = (self.index & bit) != 0
        got = after(self.flying, *before) if before else self.flying
        if kind == "double":
            parts = jnp.where(mine, got, self.x), jnp.where(mine, self.x, got)
            self.x = jnp.concatenate(parts, 0)
        else:
            self.x = (self.x.astype(F32) + got.astype(F32)).astype(BF16)

    def halves(self, *before):
        got = self.flying if isinstance(self.flying, list) else [self.flying]
        return [self.x, *(after(part, *before) for part in got)]


class Pair:
    def __init__(self, first, second, bits, turned, size, index):
        self.parts = Reduction(first, bits, size, index), Reduction(second, turned, size, index)
        self.size, self.both = size, None

    @property
    def x(self):
        return tuple(part.x for part in self.parts)

    def start(self):
        one, two = self.parts
        bit = one.steps[0][0]
        if bit != two.steps[0][0]:
            one.start()
            two.start()
            return
        self.both = swap(jnp.stack([one.split(), two.split()]), "dp", self.size, bit)

    def end(self, *before):
        one, two = self.parts
        if self.both is not None:
            both = after(self.both, *before)
            one.flying, two.flying, self.both = both[0], both[1], None
            before = ()
        one.end(*before)
        two.end(*before)


class Gather:
    def __init__(self, x, steps):
        self.x, self.steps = x, steps

    def start(self):
        axis, size, bit = self.steps[0]
        self.flying = swap(self.x, axis, size, bit)

    def end(self, *before):
        self.steps.pop(0)
        self.x = jnp.concatenate([self.x, after(self.flying, *before)], 0)


def per_device(
    dp,
    mp,
    tokens,
    condition,
    buckets,
    heads_weight,
    merge_weight,
    expand_weight,
    reduce_weight,
    adapt_first,
    adapt_second,
    cosine_scale,
    cotangent,
):
    own_rows, width = tokens.shape
    local_images = buckets.shape[0]
    local = cosine_scale.shape[0] * HEAD_DIM
    units = reduce_weight.shape[0]
    index = lax.axis_index("dp")
    core = functools.partial(swap, axis="mp", size=mp, bit=1)
    chip = functools.partial(swap, axis="mp", size=mp, bit=2)

    heads_own = jnp.transpose(heads_weight, (1, 0, 2))
    heads_parts = fetch_parts(heads_own, dp, index)
    tokens, *heads_parts = lax.optimization_barrier((tokens, *heads_parts))

    scale_first = 1.0 + jnp.dot(condition, adapt_first, preferred_element_type=F32)
    scale_first = scale_first.reshape(local_images, 1, width)
    normed_own = norm_first(tokens, scale_first)
    heads_near = chip(heads_parts[0])
    merge_packed = jnp.concatenate(
        [after(merge_weight, normed_own), pack_row(cosine_scale, width)], 0
    )
    buckets_chip = jnp.concatenate([buckets, core(buckets)], 0)
    normed = jnp.concatenate([normed_own, core(normed_own)], 0)
    normed, heads_near, cotangent_late, merge_packed, *cross = lax.optimization_barrier(
        (normed, heads_near, cotangent, merge_packed, *heads_parts[1:])
    )
    cross = [chip(part) for part in cross]
    relayed = relay_parts(heads_near, dp)
    merge_other = chip(merge_packed)
    cot_core = core(cotangent_late)
    table = jnp.asarray(turn_table())
    own = attend_forward(buckets_chip, cosine_scale, table, normed, heads_own)

    expand_own = jnp.transpose(after(expand_weight, own[5]), (1, 0, 2))
    scale_second = 1.0 + jnp.dot(
        after(condition, own[5]), adapt_second, preferred_element_type=F32
    )
    scale_second = scale_second.reshape(local_images, 1, width)
    expand_own = lax.optimization_barrier((expand_own, scale_second))[0]
    cot_first = chip(after(cotangent_late[: own_rows // 2], expand_own))
    *pieces, merge_other = lax.optimization_barrier(
        (*relayed, *cross, merge_other, expand_own)
    )[:-1]
    heads_other = assemble_parts(heads_near, pieces, dp, index)
    scale_other = unpack_row(merge_other[local:], cosine_scale.shape[0])
    merge_other = merge_other[:local]
    heads_other, expand_own, scale_second, merge_other, scale_other = lax.optimization_barrier(
        (heads_other, expand_own, scale_second, merge_other, scale_other)
    )
    cot_last = chip(after(cotangent_late[own_rows // 2 :], heads_other))
    *other, keep, send = attend_forward(
        buckets_chip, scale_other, table, normed, heads_other, (own[5], merge_weight, merge_other)
    )
    send, cot_first, cot_last, cot_core = lax.optimization_barrier(
        (send, cot_first, cot_last, cot_core)
    )
    middle, second_own = norm_second(tokens, keep, core(send), scale_second)
    second_chip = chip(second_own)
    second_core = core(second_own)
    cot_chip = jnp.concatenate([after(cot_first, second_own), cot_last], 0)
    cot_far = core(cot_chip)

    o_keep, o_send, n_keep, n_send, grads = geglu(
        second_own, second_core, cotangent, cot_core, expand_own, reduce_weight
    )
    second_chip, cot_far, grads = lax.optimization_barrier((second_chip, cot_far, grads))
    second_far = core(second_chip)
    o_near, n_near = core(o_send), core(n_send)
    o_chip, o_far, n_chip, n_far, grads = geglu(
        second_chip, second_far, cot_chip, cot_far, expand_own, reduce_weight, grads
    )

    bits = [1 << b for b in range(dp.bit_length() - 1)]
    turned = bits[1:2] + bits[:1] + bits[2:]
    n_pair = (n_chip + core(n_far).astype(F32)).astype(BF16)
    n_pair, grads = lax.optimization_barrier((n_pair, grads))
    n_sum = chip(n_pair)
    cut = 3 * units // 2
    mlp = Pair(grads[:cut], grads[cut:], bits, turned, dp, index)
    mlp.start()
    middle_grad, adapt_second_grad, branch_own = norm_back(
        after(n_keep, *mlp.x), (n_near, n_sum), middle, cotangent, scale_second, True
    )
    branch_core = core(branch_own)
    o_pair = (o_chip + after(core(after(o_far, n_pair)), branch_own).astype(F32)).astype(BF16)
    o_sum = chip(o_pair)
    mlp.end(branch_own)
    mlp.start()
    branch = lax.optimization_barrier((branch_own, branch_core, o_pair, *mlp.x))[:2]

    far_a, far_b, turn_far, triple_far = attend_backward(
        buckets_chip, scale_other, table, normed, merge_other, branch, other
    )
    got_a, got_b = chip(far_a), chip(far_b)
    o_sum = after(o_sum, far_a)
    mlp.end(far_a, o_sum)
    mlp.start()
    branch = lax.optimization_barrier((*branch, *mlp.x))[:2]
    near_a, near_b, turn_own, keep, send = attend_backward(
        buckets_chip,
        cosine_scale,
        table,
        normed,
        merge_weight,
        branch,
        own,
        (heads_own, heads_other, triple_far),
    )
    near_a, near_b, send, got_a, mlp.both = lax.optimization_barrier(
        (near_a, near_b, send, got_a, mlp.both)
    )
    attend_a = Reduction(
        (near_a.astype(F32) + got_a.astype(F32)).astype(BF16), bits, dp, index, True
    )
    attend_a.start()
    mlp.end(attend_a.x)
    mlp.start()
    tokens_grad, adapt_first_grad = norm_back(
        after(keep, *mlp.x), (core(send),), tokens, middle_grad, scale_first, False
    )
    n = local_images
    first_low = adapt_first_grad.reshape(n, width).astype(BF16)
    second_low = adapt_second_grad.reshape(n, width).astype(BF16)
    turn = split_terms(jnp.concatenate([turn_own, turn_far], 1))
    payload = jnp.concatenate(
        [
            first_low,
            second_low,
            jnp.pad(condition, ((0, 0), (0, width - condition.shape[1]))),
            jnp.concatenate([turn[0], turn[1]], 1),
            jnp.concatenate([turn[2], jnp.zeros_like(turn[2])], 1),
        ],
        0,
    )[None]
    adapters = Gather(
        payload, [("dp", dp, bit) for bit in bits] + [("mp", mp, bit) for bit in (1, 2)]
    )
    adapters.start()
    attend_a.end(tokens_grad)
    attend_a.start()
    attend_b = Reduction(
        (near_b.astype(F32) + after(got_b, attend_a.x).astype(F32)).astype(BF16),
        bits,
        dp,
        index,
        True,
    )
    attend_b.start()
    adapters.end(attend_b.x)
    adapters.start()
    middle, first_late = lax.optimization_barrier((middle, first_low, attend_b.x))[:2]
    layer_out = middle + (o_keep + o_near.astype(F32) + o_sum.astype(F32))
    condition_grad = nt(first_late, adapt_first) + nt(second_low, adapt_second)
    last = [adapters.x, layer_out, condition_grad]

    def end(one):
        one.end(*last)
        last.clear()
        last.extend(one.x if isinstance(one.x, tuple) else [one.x])

    def land(one):
        if isinstance(one.flying, list):
            one.flying[-1] = after(one.flying[-1], *last)
            last[:] = one.flying[-1:]
        else:
            one.flying = after(one.flying, *last)
            last[:] = [one.flying]

    def products():
        everyone = adapters.x
        first_all = everyone[:, :n].reshape(-1, width)
        second_all = everyone[:, n : 2 * n].reshape(-1, width)
        condition_all = everyone[:, 2 * n : 3 * n, : condition.shape[1]]
        condition_all = condition_all.reshape(-1, condition.shape[1])
        first_total = tn(condition_all, first_all)
        second_total = tn(condition_all, second_all)
        turns = everyone[:, 3 * n :].astype(F32)
        turns = turns[:, 0, : 2 * local] + turns[:, 0, 2 * local : 4 * local] + turns[:, 1, : 2 * local]
        turn_total = jnp.sum(turns[:dp, :local], 0) + jnp.sum(turns[2 * dp : 3 * dp, local:], 0)
        scale_total = turn_total[::HEAD_DIM] / (2.0 * cosine_scale)
        return first_total, second_total, scale_total

    names = {"a": attend_a, "b": attend_b, "m": mlp, "g": adapters}
    for name in ORDER if dp == 8 else "":
        if name == "C":
            first_total, second_total, scale_total = products()
            last[:] = [first_total, second_total]
            continue
        if name in "!@%":
            land({"!": mlp.parts[0], "@": mlp.parts[1], "%": attend_a}[name])
        elif name == "1":
            mlp.parts[0].start(*last)
        elif name in "234":
            mlp.parts[1].start_piece(int(name) - 2, 3, *last)
        elif name.islower():
            end(names[name])
        else:
            names[name.lower()].start()
    if dp != 8:
        for one in (mlp, attend_a, attend_b):
            part = one.parts[0] if one is mlp else one
            while len(part.steps) > 1:
                end(one)
                one.start()
        while adapters.steps:
            end(adapters)
            if adapters.steps:
                adapters.start()
        first_total, second_total, scale_total = products()
    if dp == 8 and "C" not in ORDER:
        first_total, second_total, scale_total = products()
    mine = jnp.stack([index & 1, (index >> 1) & 1])
    reduce_total, expand_total = finish_geglu(
        mine, [half for part in mlp.parts for half in part.halves(*last)], units
    )
    heads_total, merge_total = finish_attend(
        mine,
        [half for part in (attend_a, attend_b) for half in part.halves(reduce_total)],
    )
    heads_total = jnp.transpose(heads_total, (1, 0, 2))
    return (
        layer_out,
        tokens_grad,
        condition_grad,
        heads_total,
        merge_total,
        expand_total,
        reduce_total,
        first_total,
        second_total,
        scale_total,
    )


def solution(mesh):
    split = P(("dp", "mp"), None)
    return jax.shard_map(
        functools.partial(per_device, mesh.shape["dp"], mesh.shape["mp"]),
        mesh=mesh,
        in_specs=(
            split,
            split,
            P(("dp", "mp")),
            P(None, None, "mp"),
            P("mp", None),
            P(None, None, "mp"),
            P("mp", None),
            P(),
            P(),
            P("mp"),
            split,
        ),
        out_specs=(
            split,
            split,
            split,
            P(None, None, "mp"),
            P("mp", None),
            P(None, None, "mp"),
            P("mp", None),
            P(),
            P(),
            P("mp"),
        ),
        check_vma=False,
    )
```
